32 devices in a mesh: seq: 8 (over z, x), head: 4 (over y, core).
Axes of the slice: x: 2, y: 2, z: 4, core: 2. Of those that a mesh axis runs over, the one named last changes fastest.
Arguments:
- queries: bfloat16 [2048, 4096], P('seq', 'head'), may hold values from -8 to 8
- suffix_key_value: bfloat16 [2048, 2, 2048], P('seq', None, 'head'), may hold values from -8 to 8
- pooled_pages: bfloat16 [128, 256, 2, 2048], P('seq', None, None, 'head'), may hold values from -8 to 8
- out_weight: bfloat16 [4096, 5376], P('head'), may hold values from -0.5 to 0.5
- page_table: int32 [4, 32], replicated, may hold values from 0 to 127, as said below
- prefix_len: int32 [4], replicated, may hold values from 1024 to 8192, as said below
- suffix_len: int32 [4], replicated, may hold values from 2 to 512, as said below
Outputs:
- projected: bfloat16 [2048, 5376], P('seq', 'head')
The draws below stay inside these ranges and needn't reach their ends.
Inputs may be any that keep to these rules, and one draw needn't show every extreme that they name: `page_table`: every slot of the pool appears exactly once; slot s lies on index s // 16 of seq, and every index of seq holds exactly 4 pages of every request. `prefix_len`: some request has exactly 8192 prefix tokens. `suffix_len`: some request has exactly 512 live suffix tokens.
All inputs are finite; a program needn't handle non-finite values.
Results may differ from the reference program's by a relative error of at most 0.013.
Values may be sent and summed in bfloat16 or wider, within the bound.
No kernel may reach another device: no remote copies, remote signals or barrier semaphores. Data moves between devices by JAX's collectives and lax.ppermute only.
A program may use at most 192 MiB of HBM per device.

```python
import jax
import jax.numpy as jnp
from jax import lax

D = 5376
QUERY_HEADS = 32
KEY_VALUE_HEADS = 16
HEAD_WIDTH = 128
PAGE_TOKENS = 256
TOK_DEV = 256
PAGES_DEV = 16
SUFFIX_TOKENS = 512
REQUEST_COUNT = 4
PREFIX_PAGES = 32
CAP = 4
POOL_PAGES = 128
TOTAL_TOKENS = 2048
N_HEAD = 4


def draw_queries(key, part):
    unsigned_values = jnp.clip(2.0 * jax.random.normal(jax.random.fold_in(key, 32), (TOTAL_TOKENS, QUERY_HEADS * HEAD_WIDTH), jnp.float32), -8.0, 8.0)
    return unsigned_values.astype(jnp.bfloat16)


def draw_suffix_key_value(key, part):
    unsigned_values = jnp.clip(jax.random.normal(jax.random.fold_in(key, 33), (TOTAL_TOKENS, 2, KEY_VALUE_HEADS * HEAD_WIDTH), jnp.float32), -8.0, 8.0)
    return unsigned_values.astype(jnp.bfloat16)


def shuffle_local(subkey):
    return jax.random.permutation(subkey, PAGES_DEV)


def shuffle_pages(subkey):
    return jax.random.permutation(subkey, PREFIX_PAGES)


def draw_page_table(key, part):
    device_count = POOL_PAGES // PAGES_DEV
    local_order = jax.vmap(shuffle_local)(jax.random.split(jax.random.fold_in(key, 11), device_count))
    page_order = jax.vmap(shuffle_pages)(jax.random.split(jax.random.fold_in(key, 12), REQUEST_COUNT))
    device_of = page_order // CAP
    within = page_order % CAP
    request_ids = jnp.arange(REQUEST_COUNT, dtype=jnp.int32)[:, None]
    local_slot = local_order[device_of, request_ids * CAP + within]
    return (device_of * PAGES_DEV + local_slot).astype(jnp.int32)


def draw_prefix_len(key, part):
    longest = PREFIX_PAGES * PAGE_TOKENS
    floor_len = longest // 8
    first_draw = jax.random.randint(jax.random.fold_in(key, 21), (REQUEST_COUNT,), 0, longest - floor_len + 1)
    second = jax.random.randint(jax.random.fold_in(key, 22), (REQUEST_COUNT,), 0, longest - floor_len + 1)
    lengths = floor_len + jnp.minimum(first_draw, second)
    chosen = jax.random.randint(jax.random.fold_in(key, 23), (), 0, REQUEST_COUNT)
    return jnp.where(jnp.arange(REQUEST_COUNT, dtype=jnp.int32) == chosen, longest, lengths).astype(jnp.int32)


def draw_suffix_len(key, part):
    lengths = jax.random.randint(jax.random.fold_in(key, 24), (REQUEST_COUNT,), 2, SUFFIX_TOKENS + 1)
    chosen = jax.random.randint(jax.random.fold_in(key, 25), (), 0, REQUEST_COUNT)
    return jnp.where(jnp.arange(REQUEST_COUNT, dtype=jnp.int32) == chosen, SUFFIX_TOKENS, lengths).astype(jnp.int32)


def steps_of(own_key, dims, shards, least, high):
    gain = 1.0
    for dim, blocks in shards:
        heights = jax.random.uniform(jax.random.fold_in(jax.random.fold_in(own_key, 6), dim), (blocks,), jnp.float32, least / len(shards), high / len(shards))
        gain = gain * jnp.repeat(jnp.exp(heights), dims[dim] // blocks).reshape((-1,) + (1,) * (len(dims) - 1 - dim))
    return gain


def gaussian(key, extent, deviation, bound, cuts=(), held_as=jnp.bfloat16):
    entries = jax.random.normal(key, extent, jnp.float32) * deviation
    if len(cuts) > 0:
        entries = steps_of(key, extent, cuts, -0.22, 0.18) * entries
    return jnp.clip(entries, min=-bound, max=bound).astype(held_as)


def setup_inputs(seed: int = 0) -> dict:
    key_of = jax.random.split(jax.random.key(seed), 8)
    queries = draw_queries(jax.random.fold_in(key_of[7], 71), 0)
    suffix_key_value = draw_suffix_key_value(jax.random.fold_in(key_of[7], 71), 0)
    pooled_pages = gaussian(key_of[2], (POOL_PAGES, PAGE_TOKENS, 2, KEY_VALUE_HEADS * HEAD_WIDTH), 1.0, 8.0, ((0, 8), (3, 4)))
    out_weight = gaussian(key_of[3], (QUERY_HEADS * HEAD_WIDTH, D), HEAD_WIDTH ** -0.5, 0.5, ((0, 4),))
    page_table = draw_page_table(jax.random.fold_in(key_of[7], 71), 0)
    prefix_len = draw_prefix_len(jax.random.fold_in(key_of[7], 71), 0)
    suffix_len = draw_suffix_len(jax.random.fold_in(key_of[7], 71), 0)
    return dict(queries=queries, suffix_key_value=suffix_key_value, pooled_pages=pooled_pages, out_weight=out_weight, page_table=page_table, prefix_len=prefix_len, suffix_len=suffix_len)


def reference(queries, suffix_key_value, pooled_pages, out_weight, page_table, prefix_len, suffix_len):
    group_of_heads = QUERY_HEADS // KEY_VALUE_HEADS
    score_scale = float(D // QUERY_HEADS) ** -0.5
    query_layout = jnp.swapaxes(queries.reshape(2, REQUEST_COUNT, TOK_DEV, KEY_VALUE_HEADS, group_of_heads, HEAD_WIDTH), 0, 1).reshape(REQUEST_COUNT, SUFFIX_TOKENS, KEY_VALUE_HEADS, group_of_heads, HEAD_WIDTH)
    suffix_layout = jnp.swapaxes(suffix_key_value.reshape(2, REQUEST_COUNT, TOK_DEV, 2, KEY_VALUE_HEADS, HEAD_WIDTH), 0, 1).reshape(REQUEST_COUNT, SUFFIX_TOKENS, 2, KEY_VALUE_HEADS, HEAD_WIDTH)
    positions = jnp.arange(SUFFIX_TOKENS, dtype=jnp.int32)
    prefix_positions = jnp.arange(PREFIX_PAGES * PAGE_TOKENS, dtype=jnp.int32)

    def one_request(inputs):
        query_req, suffix_req, page_table_row, prefix_count, suffix_count = inputs
        rows_of_pages = jnp.take(pooled_pages, page_table_row.astype(jnp.int32), axis=0).reshape(PREFIX_PAGES * PAGE_TOKENS, 2, KEY_VALUE_HEADS, HEAD_WIDTH)
        key_rows = jnp.concatenate([rows_of_pages[:, 0], suffix_req[:, 0]], axis=0)
        value_rows = jnp.concatenate([rows_of_pages[:, 1], suffix_req[:, 1]], axis=0)
        prefix_seen = jnp.broadcast_to((prefix_positions < prefix_count)[None, :], (SUFFIX_TOKENS, PREFIX_PAGES * PAGE_TOKENS))
        suffix_seen = (positions[None, :] <= positions[:, None]) & (positions[None, :] < suffix_count)
        visible = jnp.concatenate([prefix_seen, suffix_seen], axis=1)
        live_query = positions < suffix_count

        def one_head(head_inputs):
            query_head, key_head, value_head = head_inputs
            scores = jnp.einsum("tgd,nd->tgn", query_head.astype(jnp.float32), key_head.astype(jnp.float32)) * score_scale
            row_max = jnp.max(jnp.where(visible[:, None, :], scores, -jnp.inf), axis=2, keepdims=True)
            weights = jnp.where(visible[:, None, :], jnp.exp(scores - row_max), 0.0)
            row_total = jnp.sum(weights, axis=2, keepdims=True)
            rounded = lax.optimization_barrier(weights.astype(jnp.bfloat16)).astype(jnp.float32)
            mixed = jnp.einsum("tgn,nd->tgd", rounded, value_head.astype(jnp.float32)) / row_total
            return jnp.where(live_query[:, None, None], mixed, 0.0).astype(jnp.bfloat16)

        head_outs = lax.map(one_head, (jnp.moveaxis(query_req, 1, 0), jnp.moveaxis(key_rows, 1, 0), jnp.moveaxis(value_rows, 1, 0)))
        return jnp.moveaxis(head_outs, 0, 1).reshape(SUFFIX_TOKENS, QUERY_HEADS * HEAD_WIDTH)

    attention = lax.map(one_request, (query_layout, suffix_layout, page_table, prefix_len, suffix_len))
    attention = jnp.swapaxes(attention.reshape(REQUEST_COUNT, 2, TOK_DEV, QUERY_HEADS * HEAD_WIDTH), 0, 1)
    attention = attention.reshape(REQUEST_COUNT * SUFFIX_TOKENS, QUERY_HEADS * HEAD_WIDTH)
    group_cols = QUERY_HEADS * HEAD_WIDTH // N_HEAD
    projected = jnp.zeros((REQUEST_COUNT * SUFFIX_TOKENS, D), jnp.float32)
    for head_slot in range(N_HEAD):
        partial_value = jnp.dot(attention[:, head_slot * group_cols:(head_slot + 1) * group_cols], out_weight[head_slot * group_cols:(head_slot + 1) * group_cols], preferred_element_type=jnp.float32)
        projected = projected + lax.optimization_barrier(partial_value.astype(jnp.bfloat16)).astype(jnp.float32)
    return projected.astype(jnp.bfloat16)
```

```python
import functools
import math

import jax
import jax.numpy as jnp
from jax import lax
from jax.experimental import pallas as pl
from jax.experimental.pallas import tpu as pltpu
from jax.sharding import PartitionSpec as P

D = 5376
QUERY_HEADS = 32
KEY_VALUE_HEADS = 16
HEAD_WIDTH = 128
GROUP = QUERY_HEADS // KEY_VALUE_HEADS
RATE = float(D // QUERY_HEADS) ** (-0.5) * math.log2(math.e)
HIDDEN = -(2.0**99)
STAT = 128
SUM_HIGH = 32
SUM_LOW = 64
F32 = jnp.float32
BF16 = jnp.bfloat16
MIB = 1 << 20


def ring_member(place, count):
    return jnp.where(place < count // 2, 2 * place, 2 * (count - 1 - place) + 1)


def ring_place(member, count):
    return jnp.where(member % 2 == 0, member // 2, count - 1 - member // 2)


def ring_order(count):
    return list(range(0, count, 2)) + list(range(count - 1, 0, -2))


def same_request_at(offset, count):
    order = ring_order(count)
    half = count // 2
    return any(order[(i + offset) % count] % half == order[i] % half for i in range(count))


def tables(page_table, prefix_len, suffix_len, pages_dev, holding, page_rows, seq_index, count):
    mine = page_table // pages_dev == seq_index
    index = jnp.arange(page_table.shape[1], dtype=jnp.int32)
    before = mine[:, None, :] & (index[None, None, :] < index[None, :, None])
    rank = jnp.sum(before.astype(jnp.int32), axis=2)
    wanted = jnp.arange(holding, dtype=jnp.int32)
    pick = mine[:, None, :] & (rank[:, None, :] == wanted[None, :, None])
    slots = jnp.sum(jnp.where(pick, (page_table % pages_dev)[:, None, :], 0), axis=2)
    first = jnp.sum(jnp.where(pick, index[None, None, :] * page_rows, 0), axis=2)
    valid = jnp.clip(prefix_len[:, None] - first, 0, page_rows)
    live = jnp.sum((valid > 0).astype(jnp.int32), axis=1)
    place = ring_place(seq_index, count)
    here = jnp.stack([place, seq_index]).astype(jnp.int32)
    return jnp.concatenate([slots.reshape(-1), valid.reshape(-1), live, suffix_len, here])


class Meta:
    def __init__(self, count, holding):
        self.count = count
        self.half = count // 2
        self.holding = holding
        self.valid_at = self.half * holding
        self.live_at = 2 * self.half * holding
        self.suffix_at = self.live_at + self.half
        self.place_at = self.suffix_at + self.half

    def chunk(self, meta, offset):
        place = (meta[self.place_at] + (offset + self.count)) % self.count
        return ring_member(place, self.count)

    def slot(self, meta, request, page):
        return meta[request * self.holding + page]

    def valid(self, meta, request, page):
        return meta[self.valid_at + request * self.holding + page]


def attend_kernel(info, offset, row_base, tok_rows, with_suffix, meta, q_ref, *refs):
    holding = info.holding
    k_refs = refs[:holding]
    v_refs = refs[holding : 2 * holding]
    sk_ref, sv_ref = refs[2 * holding : 2 * holding + 2]
    blocks = len(refs) - (2 * holding + 2) - 3
    out_refs = refs[2 * holding + 2 : 2 * holding + 2 + blocks]
    acc_ref, max_ref, sum_ref = refs[-3:]
    group = pl.program_id(0)
    block = pl.program_id(1)
    rows = q_ref.shape[0]
    keys = k_refs[0].shape[1]
    chunk = info.chunk(meta, offset)
    request = chunk % info.half
    member = chunk // info.half
    suffix = meta[info.suffix_at + request]
    first = member * tok_rows + row_base + block * rows
    live_rows = suffix > first
    live_pages = meta[info.live_at + request]
    width = HEAD_WIDTH

    def stacked():
        return jnp.concatenate(
            [q_ref[:, i * width : (i + 1) * width] for i in range(GROUP)], axis=0
        )

    def scores_of(query, keys_block):
        return lax.dot_general(
            query, keys_block, (((1,), (1,)), ((), ())), preferred_element_type=F32
        )

    max_ref[...] = jnp.full(max_ref.shape, HIDDEN, F32)
    sum_ref[...] = jnp.zeros(sum_ref.shape, F32)
    acc_ref[...] = jnp.zeros(acc_ref.shape, F32)

    for pages in range(1, holding + 1):

        @pl.when(live_rows & (live_pages == pages))
        def _(pages=pages):
            query = stacked()
            parts = [scores_of(query, k_refs[j][0]) for j in range(pages)]
            column = lax.broadcasted_iota(jnp.int32, parts[-1].shape, 1)
            limit = info.valid(meta, request, pages - 1)
            parts[-1] = jnp.where(column < limit, parts[-1], HIDDEN)
            top = parts[0]
            for part in parts[1:]:
                top = jnp.maximum(top, part)
            row_max = jnp.max(top, axis=1, keepdims=True).astype(BF16).astype(F32)
            total = None
            mixed = None
            for j in range(pages):
                weight = jnp.exp2((parts[j] - row_max) * RATE)
                total = weight if total is None else total + weight
                product = jnp.dot(weight.astype(BF16), v_refs[j][0], preferred_element_type=F32)
                mixed = product if mixed is None else mixed + product
            max_ref[...] = row_max
            sum_ref[...] = jnp.sum(total, axis=1, keepdims=True)
            acc_ref[...] = mixed

    if with_suffix:
        seq_index = meta[info.place_at + 1]
        here = seq_index // info.half
        sees = (request == seq_index % info.half) & (member >= here)

        @pl.when(live_rows & sees)
        def _():
            scores = scores_of(stacked(), sk_ref[...])
            key = here * tok_rows + lax.broadcasted_iota(jnp.int32, scores.shape, 1)
            row = lax.broadcasted_iota(jnp.int32, scores.shape, 0) % rows
            visible = (key < suffix) & (key <= first + row)
            scores = jnp.where(visible, scores, HIDDEN)
            old_max = max_ref[...]
            row_max = jnp.max(scores, axis=1, keepdims=True).astype(BF16).astype(F32)
            row_max = jnp.maximum(row_max, old_max)
            weight = jnp.where(visible, jnp.exp2((scores - row_max) * RATE), 0.0)
            keep = jnp.exp2((old_max - row_max) * RATE)
            product = jnp.dot(weight.astype(BF16), sv_ref[...], preferred_element_type=F32)
            max_ref[...] = row_max
            sum_ref[...] = sum_ref[...] * keep + jnp.sum(weight, axis=1, keepdims=True)
            acc_ref[...] = acc_ref[...] * keep + product

    stat_at = out_refs[0].shape[1] - STAT
    lane = lax.broadcasted_iota(jnp.int32, (rows, STAT), 1)
    for number, out_ref in enumerate(out_refs):

        @pl.when(block == number)
        def _(out_ref=out_ref):
            @pl.when(group == 0)
            def _():
                out_ref[:, stat_at:] = jnp.zeros((rows, STAT), BF16)

            stats = out_ref[:, stat_at:].astype(F32)
            for i in range(GROUP):
                part = slice(i * rows, (i + 1) * rows)
                head = group * GROUP + i
                column = pl.multiple_of(head * width, width)
                out_ref[:, pl.ds(column, width)] = acc_ref[part, :].astype(BF16)
                total = sum_ref[part, :]
                high = total.astype(BF16).astype(F32)
                stats = jnp.where(lane == head, max_ref[part, :], stats)
                stats = jnp.where(lane == SUM_HIGH + head, high, stats)
                stats = jnp.where(lane == SUM_LOW + head, total - high, stats)
            out_ref[:, stat_at:] = stats.astype(BF16)


def attend(info, meta, query, offset, row_base, tok_rows, key_pages, value_pages, suffix_keys, suffix_values):
    rows = min(128, query.shape[0])
    blocks = query.shape[0] // rows
    columns = query.shape[1]
    holding = info.holding
    kv_local = key_pages.shape[2] // HEAD_WIDTH
    page_rows = key_pages.shape[1]
    wide = GROUP * HEAD_WIDTH

    def page_map(page, group, block, meta):
        request = info.chunk(meta, offset) % info.half
        return (info.slot(meta, request, page), 0, group)

    page_specs = [
        pl.BlockSpec((1, page_rows, HEAD_WIDTH), functools.partial(page_map, j))
        for j in range(holding)
    ]
    suffix_spec = pl.BlockSpec((tok_rows, HEAD_WIDTH), lambda g, t, meta: (0, g))
    out_spec = pl.BlockSpec((rows, columns + STAT), lambda g, t, meta: (0, 0))
    out = jax.ShapeDtypeStruct((rows, columns + STAT), BF16)
    work = query.shape[0] * kv_local * GROUP * holding * page_rows
    return pl.pallas_call(
        functools.partial(
            attend_kernel, info, offset, row_base, tok_rows, same_request_at(offset, info.count)
        ),
        grid_spec=pltpu.PrefetchScalarGridSpec(
            num_scalar_prefetch=1,
            grid=(kv_local, blocks),
            in_specs=[pl.BlockSpec((rows, wide), lambda g, t, meta: (t, g))]
            + page_specs
            + page_specs
            + [suffix_spec, suffix_spec],
            out_specs=[out_spec] * blocks,
            scratch_shapes=[
                pltpu.VMEM((GROUP * rows, HEAD_WIDTH), F32),
                pltpu.VMEM((GROUP * rows, 1), F32),
                pltpu.VMEM((GROUP * rows, 1), F32),
            ],
        ),
        out_shape=[out] * blocks,
        compiler_params=pltpu.CompilerParams(vmem_limit_bytes=24 * MIB),
        cost_estimate=pl.CostEstimate(
            flops=4 * work * HEAD_WIDTH,
            bytes_accessed=2 * query.size * 2 + 4 * holding * page_rows * kv_local * HEAD_WIDTH,
            transcendentals=work,
        ),
        name="attend",
    )(meta, query, *([key_pages] * holding), *([value_pages] * holding), suffix_keys, suffix_values)


def combine(packed):
    stat_at = packed[0].shape[1] - STAT
    stats = [one[:, stat_at:].astype(F32) for one in packed]
    top = stats[0]
    for one in stats[1:]:
        top = jnp.maximum(top, one)
    factors = [jnp.exp2((jnp.minimum(one - top, 0.0)) * RATE) for one in stats]
    total = None
    for one, factor in zip(stats, factors):
        own = pltpu.roll(one, STAT - SUM_HIGH, 1) + pltpu.roll(one, STAT - SUM_LOW, 1)
        total = own * factor if total is None else total + own * factor
    heads = []
    for head in range(stat_at // HEAD_WIDTH):
        mixed = None
        for one, factor in zip(packed, factors):
            value = one[:, head * HEAD_WIDTH : (head + 1) * HEAD_WIDTH].astype(F32)
            value = value * factor[:, head : head + 1]
            mixed = value if mixed is None else mixed + value
        heads.append(mixed)
    return (heads, top, total)


def merge_kernel(a_ref, b_ref, out_ref):
    heads, top, total = combine([a_ref[...], b_ref[...]])
    for head, mixed in enumerate(heads):
        out_ref[:, head * HEAD_WIDTH : (head + 1) * HEAD_WIDTH] = mixed.astype(BF16)
    high = total.astype(BF16).astype(F32)
    lane = lax.broadcasted_iota(jnp.int32, top.shape, 1)
    stats = jnp.where(lane < SUM_HIGH, top, 0.0)
    stats = jnp.where((lane >= SUM_HIGH) & (lane < SUM_LOW), pltpu.roll(high, SUM_HIGH, 1), stats)
    low = pltpu.roll(total - high, SUM_LOW, 1)
    stats = jnp.where((lane >= SUM_LOW) & (lane < SUM_LOW + SUM_HIGH), low, stats)
    out_ref[:, len(heads) * HEAD_WIDTH :] = stats.astype(BF16)


def merge(a, b):
    return pl.pallas_call(
        merge_kernel,
        out_shape=jax.ShapeDtypeStruct(a.shape, BF16),
        in_specs=[pl.BlockSpec(memory_space=pltpu.VMEM)] * 2,
        out_specs=pl.BlockSpec(memory_space=pltpu.VMEM),
        compiler_params=pltpu.CompilerParams(vmem_limit_bytes=16 * MIB),
        cost_estimate=pl.CostEstimate(
            flops=6 * a.size, bytes_accessed=6 * a.size, transcendentals=0
        ),
        name="merge",
    )(a, b)


def finish_kernel(info, tok_rows, blocks, meta, target, *refs):
    packed = refs[: 3 * blocks]
    w_ref, give_ref, keep_ref, attention = refs[3 * blocks :]
    step = pl.program_id(0)
    half_steps = pl.num_programs(0) // 2
    rows = packed[0].shape[0]

    @pl.when(step == 0)
    def _():
        chunk = info.chunk(meta, 0)
        suffix = meta[info.suffix_at + chunk % info.half]
        for block in range(blocks):
            heads, _, total = combine([ref[...] for ref in packed[3 * block : 3 * block + 3]])
            first = (chunk // info.half) * tok_rows + block * rows
            place = first + lax.broadcasted_iota(jnp.int32, heads[0].shape, 0)
            for head, mixed in enumerate(heads):
                value = jnp.where(place < suffix, mixed / total[:, head : head + 1], 0.0)
                attention[
                    block * rows : (block + 1) * rows,
                    head * HEAD_WIDTH : (head + 1) * HEAD_WIDTH,
                ] = value.astype(BF16)

    product = jnp.dot(attention[...], w_ref[0], preferred_element_type=F32).astype(BF16)

    @pl.when(step < half_steps)
    def _():
        give_ref[0] = product

    @pl.when(step >= half_steps)
    def _():
        keep_ref[0] = product


def finish(info, meta, targets, packed, weight, tok_rows):
    blocks = len(packed) // 3
    count, depth, columns = weight.shape
    half = count // 2
    whole = pl.BlockSpec(packed[0].shape, lambda i, meta, target: (0, 0))
    out = jax.ShapeDtypeStruct((half, tok_rows, columns), BF16)
    return pl.pallas_call(
        functools.partial(finish_kernel, info, tok_rows, blocks),
        grid_spec=pltpu.PrefetchScalarGridSpec(
            num_scalar_prefetch=2,
            grid=(count,),
            in_specs=[whole] * len(packed)
            + [pl.BlockSpec((1, depth, columns), lambda i, meta, target: (target[i], 0, 0))],
            out_specs=[
                pl.BlockSpec(
                    (1, tok_rows, columns),
                    lambda i, meta, target: (jnp.minimum(i, half - 1), 0, 0),
                ),
                pl.BlockSpec(
                    (1, tok_rows, columns),
                    lambda i, meta, target: (jnp.maximum(i - half, 0), 0, 0),
                ),
            ],
            scratch_shapes=[pltpu.VMEM((tok_rows, depth), BF16)],
        ),
        out_shape=[out, out],
        compiler_params=pltpu.CompilerParams(vmem_limit_bytes=40 * MIB),
        cost_estimate=pl.CostEstimate(
            flops=2 * tok_rows * depth * columns * count,
            bytes_accessed=2 * weight.size,
            transcendentals=0,
        ),
        name="finish",
    )(meta, targets, *packed, weight)


def shards(queries, suffix_key_value, pooled_pages, out_weight, page_table, prefix_len, suffix_len):
    tok_rows = queries.shape[0]
    pages_dev, page_rows = pooled_pages.shape[:2]
    count = lax.axis_size("seq")
    reach = count // 2
    seq_index = lax.axis_index("seq")
    holding = 2 * pages_dev // count
    info = Meta(count, holding)
    order = ring_order(count)
    ahead = [(order[i], order[(i + 1) % count]) for i in range(count)]
    back = [(b, a) for a, b in ahead]

    middle = tok_rows // 2
    from_left = [queries]
    from_right = [queries]
    for step in range(1, reach):
        from_left.append(lax.ppermute(from_left[-1], "seq", ahead))
        from_right.append(lax.ppermute(from_right[-1], "seq", back))
    from_left.append(lax.ppermute(from_left[-1][:middle], "seq", ahead))
    from_right.append(lax.ppermute(from_right[-1][middle:], "seq", back))

    meta = tables(
        page_table, prefix_len, suffix_len, pages_dev, holding, page_rows, seq_index, count
    )
    keys = (
        pooled_pages[:, :, 0, :],
        pooled_pages[:, :, 1, :],
        suffix_key_value[:, 0, :],
        suffix_key_value[:, 1, :],
    )
    head_count = lax.axis_size("head")
    columns = out_weight.shape[1] // head_count
    weight = jnp.swapaxes(out_weight.reshape(-1, head_count, columns), 0, 1)

    home = attend(info, meta, queries, 0, 0, tok_rows, *keys)
    left = [home]
    right = [home]
    for step in range(1, reach):
        left.append(attend(info, meta, from_left[step], -step, 0, tok_rows, *keys))
        right.append(attend(info, meta, from_right[step], step, 0, tok_rows, *keys))
    left.append(attend(info, meta, from_left[reach], -reach, 0, tok_rows, *keys))
    right.append(attend(info, meta, from_right[reach], reach, middle, tok_rows, *keys))

    low_left = lax.ppermute(left[reach][0], "seq", back)
    high_right = lax.ppermute(right[reach][0], "seq", ahead)
    high_left = None
    low_right = None
    for step in range(reach - 1, 0, -1):
        low_left = lax.ppermute(merge(low_left, left[step][0]), "seq", back)
        high_right = lax.ppermute(merge(high_right, right[step][1]), "seq", ahead)
        mine_left = left[step][1] if high_left is None else merge(high_left, left[step][1])
        high_left = lax.ppermute(mine_left, "seq", back)
        mine_right = right[step][0] if low_right is None else merge(low_right, right[step][0])
        low_right = lax.ppermute(mine_right, "seq", ahead)

    head_index = lax.axis_index("head")
    half = head_count // 2
    pair = head_index // 2
    core = head_index % 2
    turn = (pair + jnp.arange(half, dtype=jnp.int32)) % half
    targets = jnp.concatenate([2 * turn + 1 - core, 2 * turn + core])
    packed = [home[0], low_left, low_right, home[1], high_left, high_right]
    give, keep = finish(info, meta, targets, packed, weight, tok_rows)
    taken = lax.ppermute(give, "head", [(i, i ^ 1) for i in range(head_count)])
    total = keep.astype(F32) + taken.astype(F32)
    result = total[0]
    for step in range(1, half):
        pairs = [(i, (i + 2 * step) % head_count) for i in range(head_count)]
        result = result + lax.ppermute(total[step].astype(BF16), "head", pairs).astype(F32)
    return result.astype(BF16)


def solution(mesh):
    placed = (
        P("seq", "head"),
        P("seq", None, "head"),
        P("seq", None, None, "head"),
        P("head", None),
        P(),
        P(),
        P(),
    )
    return jax.shard_map(
        shards, mesh=mesh, in_specs=placed, out_specs=P("seq", "head"), check_vma=False
    )
```

```python
import functools
import math

import jax
import jax.numpy as jnp
from jax import lax
from jax.experimental import pallas as pl
from jax.experimental.pallas import tpu as pltpu
from jax.sharding import PartitionSpec as P

D = 5376
QUERY_HEADS = 32
KEY_VALUE_HEADS = 16
HEAD_WIDTH = 128
GROUP = QUERY_HEADS // KEY_VALUE_HEADS
RATE = float(D // QUERY_HEADS) ** (-0.5) * math.log2(math.e)
HIDDEN = -(2.0**99)
STAT = 128
SUM_HIGH = 32
SUM_LOW = 64
F32 = jnp.float32
BF16 = jnp.bfloat16
MIB = 1 << 20


def ring_member(place, count):
    return jnp.where(place < count // 2, 2 * place, 2 * (count - 1 - place) + 1)


def ring_order(count):
    return list(range(0, count, 2)) + list(range(count - 1, 0, -2))


def same_request_at(offset, count):
    order = ring_order(count)
    half = count // 2
    return any(order[(i + offset) % count] % half == order[i] % half for i in range(count))


class Meta:
    def __init__(self, count, holding):
        self.count = count
        self.half = count // 2
        self.holding = holding
        self.stride = holding + 1
        self.valid_at = self.half * self.stride
        self.live_at = 2 * self.half * self.stride
        self.suffix_at = self.live_at + self.half
        self.place_at = self.suffix_at + self.half
        self.length = self.place_at + 2

    def chunk(self, meta, offset):
        place = meta[self.place_at] + offset
        place = jnp.where(place < 0, place + self.count, place)
        place = jnp.where(place >= self.count, place - self.count, place)
        return ring_member(place, self.count)

    def request(self, chunk):
        return jnp.where(chunk >= self.half, chunk - self.half, chunk)

    def member(self, chunk):
        return jnp.where(chunk >= self.half, 1, 0)

    def slot(self, meta, request, page):
        return meta[request * self.stride + page]

    def valid(self, meta, request, page):
        return meta[self.valid_at + request * self.stride + page]


def table_kernel(info, pages_dev, page_rows, page_table, prefix_len, suffix_len, meta):
    seq_index = lax.axis_index("seq")
    first_slot = seq_index * pages_dev
    odd = seq_index % 2
    meta[info.place_at] = jnp.where(odd == 0, seq_index // 2, info.count - 1 - seq_index // 2)
    meta[info.place_at + 1] = seq_index

    def one_request(request, carry):
        prefix = prefix_len[request]
        base = request * info.stride

        def one_page(page, state):
            found, live = state
            local = page_table[request, page] - first_slot
            mine = (local >= 0) & (local < pages_dev)
            valid = jnp.minimum(jnp.maximum(prefix - page * page_rows, 0), page_rows)
            meta[base + found] = local
            meta[info.valid_at + base + found] = valid
            return (
                found + jnp.where(mine, 1, 0),
                live + jnp.where(mine & (valid > 0), 1, 0),
            )

        _, live = lax.fori_loop(0, page_table.shape[1], one_page, (0, 0))
        meta[info.live_at + request] = live
        meta[info.suffix_at + request] = suffix_len[request]
        return carry

    lax.fori_loop(0, info.half, one_request, 0)


def tables(info, pages_dev, page_rows, page_table, prefix_len, suffix_len):
    smem = pl.BlockSpec(memory_space=pltpu.SMEM)
    return pl.pallas_call(
        functools.partial(table_kernel, info, pages_dev, page_rows),
        out_shape=jax.ShapeDtypeStruct((info.length,), jnp.int32),
        in_specs=[smem] * 3,
        out_specs=smem,
        cost_estimate=pl.CostEstimate(flops=0, bytes_accessed=4096, transcendentals=0),
        name="tables",
    )(page_table, prefix_len, suffix_len)


def attend_kernel(info, offset, row_base, tok_rows, with_suffix, blocks, meta, q_ref, *refs):
    holding = info.holding
    page_refs = refs[:holding]
    refs = refs[holding:]
    if with_suffix:
        suffix_ref = refs[0]
        refs = refs[1:]
    out_refs = refs[:blocks]
    acc_ref, max_ref, sum_ref = refs[blocks:]
    group = pl.program_id(0)
    rows = q_ref.shape[0] // blocks
    width = HEAD_WIDTH
    chunk = info.chunk(meta, offset)
    request = info.request(chunk)
    member = info.member(chunk)
    suffix = meta[info.suffix_at + request]
    first = member * tok_rows + row_base
    live_pages = meta[info.live_at + request]
    live_blocks = jnp.int32(0)
    for block in range(blocks):
        live_blocks = live_blocks + jnp.where(suffix > first + block * rows, 1, 0)

    def stacked(block):
        part = slice(block * rows, (block + 1) * rows)
        return jnp.concatenate(
            [q_ref[part, i * width : (i + 1) * width] for i in range(GROUP)], axis=0
        )

    def scores_of(query, keys):
        return lax.dot_general(
            query, keys, (((1,), (1,)), ((), ())), preferred_element_type=F32
        )

    for block in range(blocks):

        @pl.when((live_blocks <= block) | (live_pages == 0))
        def _(block=block):
            acc_ref[block] = jnp.zeros(acc_ref.shape[1:], F32)
            max_ref[block] = jnp.full(max_ref.shape[1:], HIDDEN, F32)
            sum_ref[block] = jnp.zeros(sum_ref.shape[1:], F32)

    def prefix(block, pages):
        query = stacked(block)
        parts = [scores_of(query, page_refs[j][0, 0]) for j in range(pages)]
        column = lax.broadcasted_iota(jnp.int32, parts[-1].shape, 1)
        limit = info.valid(meta, request, pages - 1)
        parts[-1] = jnp.where(column < limit, parts[-1], HIDDEN)
        top = parts[0]
        for part in parts[1:]:
            top = jnp.maximum(top, part)
        row_max = jnp.max(top, axis=1, keepdims=True).astype(BF16).astype(F32)
        total = None
        mixed = None
        for j in range(pages):
            weight = jnp.exp2((parts[j] - row_max) * RATE)
            total = weight if total is None else total + weight
            product = jnp.dot(weight.astype(BF16), page_refs[j][0, 1], preferred_element_type=F32)
            mixed = product if mixed is None else mixed + product
        max_ref[block] = row_max
        sum_ref[block] = jnp.sum(total, axis=1, keepdims=True)
        acc_ref[block] = mixed

    for pages in range(1, holding + 1):
        for some in range(1, blocks + 1):

            @pl.when((live_blocks == some) & (live_pages == pages))
            def _(pages=pages, some=some):
                for block in range(some):
                    prefix(block, pages)

    if with_suffix:
        here = info.member(meta[info.place_at + 1])
        sees = (request == info.request(meta[info.place_at + 1])) & (member >= here)
        for block in range(blocks):

            @pl.when((live_blocks > block) & sees)
            def _(block=block):
                scores = scores_of(stacked(block), suffix_ref[0])
                key = here * tok_rows + lax.broadcasted_iota(jnp.int32, scores.shape, 1)
                row = lax.broadcasted_iota(jnp.int32, scores.shape, 0)
                row = jnp.where(row >= rows, row - rows, row)
                visible = (key < suffix) & (key <= first + block * rows + row)
                scores = jnp.where(visible, scores, HIDDEN)
                old_max = max_ref[block]
                row_max = jnp.max(scores, axis=1, keepdims=True).astype(BF16).astype(F32)
                row_max = jnp.maximum(row_max, old_max)
                weight = jnp.where(visible, jnp.exp2((scores - row_max) * RATE), 0.0)
                keep = jnp.exp2((old_max - row_max) * RATE)
                product = jnp.dot(weight.astype(BF16), suffix_ref[1], preferred_element_type=F32)
                max_ref[block] = row_max
                sum_ref[block] = sum_ref[block] * keep + jnp.sum(weight, axis=1, keepdims=True)
                acc_ref[block] = acc_ref[block] * keep + product

    stat_at = out_refs[0].shape[1] - STAT
    lane = lax.broadcasted_iota(jnp.int32, (rows, STAT), 1)
    for block, out_ref in enumerate(out_refs):

        @pl.when(group == 0)
        def _(out_ref=out_ref):
            out_ref[:, stat_at:] = jnp.zeros((rows, STAT), BF16)

        stats = out_ref[:, stat_at:].astype(F32)
        for i in range(GROUP):
            part = slice(i * rows, (i + 1) * rows)
            head = group * GROUP + i
            column = pl.multiple_of(head * width, width)
            out_ref[:, pl.ds(column, width)] = acc_ref[block, part, :].astype(BF16)
            total = sum_ref[block, part, :]
            high = total.astype(BF16).astype(F32)
            stats = jnp.where(lane == head, max_ref[block, part, :], stats)
            stats = jnp.where(lane == SUM_HIGH + head, high, stats)
            stats = jnp.where(lane == SUM_LOW + head, total - high, stats)
        out_ref[:, stat_at:] = stats.astype(BF16)


def attend(info, meta, query, offset, row_base, tok_rows, pages, suffix):
    rows = tok_rows // 2
    blocks = query.shape[0] // rows
    columns = query.shape[1]
    holding = info.holding
    kv_local = pages.shape[3] // HEAD_WIDTH
    page_rows = pages.shape[2]
    with_suffix = same_request_at(offset, info.count)

    def page_map(page, group, meta):
        request = info.request(info.chunk(meta, offset))
        return (info.slot(meta, request, page), 0, 0, group)

    in_specs = [pl.BlockSpec((query.shape[0], GROUP * HEAD_WIDTH), lambda g, meta: (0, g))]
    in_specs += [
        pl.BlockSpec((1, 2, page_rows, HEAD_WIDTH), functools.partial(page_map, j))
        for j in range(holding)
    ]
    operands = [query] + [pages] * holding
    if with_suffix:
        in_specs.append(pl.BlockSpec((2, tok_rows, HEAD_WIDTH), lambda g, meta: (0, 0, g)))
        operands.append(suffix)
    out = jax.ShapeDtypeStruct((rows, columns + STAT), BF16)
    work = query.shape[0] * kv_local * GROUP * holding * page_rows
    return pl.pallas_call(
        functools.partial(
            attend_kernel, info, offset, row_base, tok_rows, with_suffix, blocks
        ),
        grid_spec=pltpu.PrefetchScalarGridSpec(
            num_scalar_prefetch=1,
            grid=(kv_local,),
            in_specs=in_specs,
            out_specs=[pl.BlockSpec((rows, columns + STAT), lambda g, meta: (0, 0))] * blocks,
            scratch_shapes=[
                pltpu.VMEM((blocks, GROUP * rows, HEAD_WIDTH), F32),
                pltpu.VMEM((blocks, GROUP * rows, 1), F32),
                pltpu.VMEM((blocks, GROUP * rows, 1), F32),
            ],
        ),
        out_shape=[out] * blocks,
        compiler_params=pltpu.CompilerParams(vmem_limit_bytes=24 * MIB),
        cost_estimate=pl.CostEstimate(
            flops=4 * work * HEAD_WIDTH,
            bytes_accessed=2 * query.size * 2 + 4 * holding * page_rows * kv_local * HEAD_WIDTH,
            transcendentals=work,
        ),
        name="attend",
    )(meta, *operands)


def combine(packed, divided=False):
    stat_at = packed[0].shape[1] - STAT
    stats = [one[:, stat_at:].astype(F32) for one in packed]
    top = stats[0]
    for one in stats[1:]:
        top = jnp.maximum(top, one)
    factors = [jnp.exp2((jnp.minimum(one - top, 0.0)) * RATE) for one in stats]
    total = None
    for one, factor in zip(stats, factors):
        own = pltpu.roll(one, STAT - SUM_HIGH, 1) + pltpu.roll(one, STAT - SUM_LOW, 1)
        total = own * factor if total is None else total + own * factor
    if divided:
        factors = [factor / total for factor in factors]
    heads = []
    for head in range(stat_at // HEAD_WIDTH):
        mixed = None
        for one, factor in zip(packed, factors):
            value = one[:, head * HEAD_WIDTH : (head + 1) * HEAD_WIDTH].astype(F32)
            value = value * factor[:, head : head + 1]
            mixed = value if mixed is None else mixed + value
        heads.append(mixed)
    return (heads, top, total)


def merge_kernel(a_ref, b_ref, out_ref):
    heads, top, total = combine([a_ref[...], b_ref[...]])
    for head, mixed in enumerate(heads):
        out_ref[:, head * HEAD_WIDTH : (head + 1) * HEAD_WIDTH] = mixed.astype(BF16)
    high = total.astype(BF16).astype(F32)
    lane = lax.broadcasted_iota(jnp.int32, top.shape, 1)
    stats = jnp.where(lane < SUM_HIGH, top, 0.0)
    stats = jnp.where((lane >= SUM_HIGH) & (lane < SUM_LOW), pltpu.roll(high, SUM_HIGH, 1), stats)
    low = pltpu.roll(total - high, SUM_LOW, 1)
    stats = jnp.where((lane >= SUM_LOW) & (lane < SUM_LOW + SUM_HIGH), low, stats)
    out_ref[:, len(heads) * HEAD_WIDTH :] = stats.astype(BF16)


def merge(a, b):
    return pl.pallas_call(
        merge_kernel,
        out_shape=jax.ShapeDtypeStruct(a.shape, BF16),
        in_specs=[pl.BlockSpec(memory_space=pltpu.VMEM)] * 2,
        out_specs=pl.BlockSpec(memory_space=pltpu.VMEM),
        compiler_params=pltpu.CompilerParams(vmem_limit_bytes=16 * MIB),
        cost_estimate=pl.CostEstimate(
            flops=6 * a.size, bytes_accessed=6 * a.size, transcendentals=0
        ),
        name="merge",
    )(a, b)


def window_of(columns, head_count):
    spans = [
        -(-(t + 1) * columns // STAT) - t * columns // STAT for t in range(head_count)
    ]
    return max(spans) * STAT


def window_start(target, columns, head_count):
    start = target * columns // STAT * STAT
    return jnp.minimum(start, columns * head_count - window_of(columns, head_count))


def project(flip, head_count, attention, weight, out_ref, window, sems):
    columns = weight.shape[1] // head_count
    half = head_count // 2
    head_index = lax.axis_index("head")
    core = head_index % 2
    pair = head_index // 2
    if flip:
        core = 1 - core
    copies = []
    for turn in range(half):
        target = 2 * ((pair + turn) % half) + core
        start = pl.multiple_of(window_start(target, columns, head_count), STAT)
        copies.append(
            pltpu.make_async_copy(
                weight.at[:, pl.ds(start, window.shape[2])], window.at[turn], sems.at[turn]
            )
        )
        copies[-1].start()
    rows = attention()
    for turn in range(half):
        copies[turn].wait()
        product = jnp.dot(rows, window[turn], preferred_element_type=F32)
        out_ref[turn] = product.astype(BF16)


def finish_kernel(info, tok_rows, first_row, blocks, head_count, meta, *refs):
    packed = refs[: 3 * blocks]
    weight, rows_ref, give_ref, window, sems = refs[3 * blocks :]
    rows = packed[0].shape[0]

    def attention():
        chunk = info.chunk(meta, 0)
        suffix = meta[info.suffix_at + info.request(chunk)]
        for block in range(blocks):
            heads, _, total = combine(
                [ref[...] for ref in packed[3 * block : 3 * block + 3]], True
            )
            first = info.member(chunk) * tok_rows + first_row + block * rows
            place = first + lax.broadcasted_iota(jnp.int32, heads[0].shape, 0)
            for head, mixed in enumerate(heads):
                value = jnp.where(place < suffix, mixed, 0.0)
                rows_ref[
                    block * rows : (block + 1) * rows,
                    head * HEAD_WIDTH : (head + 1) * HEAD_WIDTH,
                ] = value.astype(BF16)
        return rows_ref[...]

    project(True, head_count, attention, weight, give_ref, window, sems)


def keep_kernel(head_count, rows_ref, weight, keep_ref, window, sems):
    project(False, head_count, lambda: rows_ref[...], weight, keep_ref, window, sems)


def finish(info, meta, packed, weight, tok_rows, first_row, head_count):
    blocks = len(packed) // 3
    depth = weight.shape[0]
    half = head_count // 2
    columns = weight.shape[1] // head_count
    wide = window_of(columns, head_count)
    rows = packed[0].shape[0] * blocks
    vmem = pl.BlockSpec(memory_space=pltpu.VMEM)
    hbm = pl.BlockSpec(memory_space=pl.ANY)
    scratch = [pltpu.VMEM((half, depth, wide), BF16), pltpu.SemaphoreType.DMA((half,))]
    cost = pl.CostEstimate(
        flops=2 * rows * depth * wide * half,
        bytes_accessed=2 * half * depth * wide,
        transcendentals=0,
    )
    params = pltpu.CompilerParams(vmem_limit_bytes=24 * MIB)
    out = jax.ShapeDtypeStruct((half, rows, wide), BF16)
    attention, give = pl.pallas_call(
        functools.partial(finish_kernel, info, tok_rows, first_row, blocks, head_count),
        out_shape=[jax.ShapeDtypeStruct((rows, depth), BF16), out],
        in_specs=[pl.BlockSpec(memory_space=pltpu.SMEM)] + [vmem] * len(packed) + [hbm],
        out_specs=[vmem, vmem],
        scratch_shapes=scratch,
        compiler_params=params,
        cost_estimate=cost,
        name="finish",
    )(meta, *packed, weight)
    keep = pl.pallas_call(
        functools.partial(keep_kernel, head_count),
        out_shape=out,
        in_specs=[vmem, hbm],
        out_specs=vmem,
        scratch_shapes=scratch,
        compiler_params=params,
        cost_estimate=cost,
        name="keep",
    )(attention, weight)
    return (give, keep)


def last_kernel(columns, head_count, *refs):
    out_ref, turned = refs[-2:]
    total = refs[0][0].astype(F32)
    total = total + refs[1][0].astype(F32)
    for ref in refs[2:-2]:
        total = total + ref[...].astype(F32)
    head_index = lax.axis_index("head")
    shift = head_index * columns - window_start(head_index, columns, head_count)
    turned[...] = total.T
    out_ref[...] = turned[pl.ds(pl.multiple_of(shift, 8), columns), :].astype(BF16)


def last(keep, taken, received, columns, head_count):
    _, rows, wide = keep.shape
    first = pl.BlockSpec((1, rows, wide), lambda i: (0, 0, 0))
    whole = pl.BlockSpec((rows, wide), lambda i: (0, 0))
    return pl.pallas_call(
        functools.partial(last_kernel, columns, head_count),
        grid=(1,),
        out_shape=jax.ShapeDtypeStruct((columns, rows), BF16),
        in_specs=[first, first] + [whole] * len(received),
        out_specs=pl.BlockSpec((columns, rows), lambda i: (0, 0)),
        scratch_shapes=[pltpu.VMEM((wide, rows), F32)],
        compiler_params=pltpu.CompilerParams(vmem_limit_bytes=16 * MIB),
        cost_estimate=pl.CostEstimate(
            flops=4 * rows * wide, bytes_accessed=8 * rows * wide, transcendentals=0
        ),
        name="last",
    )(keep, taken, *received)


def reduce_heads(give, keep, columns, head_count):
    half = head_count // 2
    taken = lax.ppermute(give, "head", [(i, i ^ 1) for i in range(head_count)])
    received = []
    for step in range(1, half):
        pairs = [(i, (i + 2 * step) % head_count) for i in range(head_count)]
        share = keep[step].astype(F32) + taken[step].astype(F32)
        received.append(lax.ppermute(share.astype(BF16), "head", pairs))
    return last(keep, taken, received, columns, head_count).T


def after(value, *others):
    return lax.optimization_barrier((value, others))[0]


def shards(queries, suffix_key_value, pooled_pages, out_weight, page_table, prefix_len, suffix_len):
    tok_rows = queries.shape[0]
    pages_dev, page_rows = pooled_pages.shape[:2]
    count = lax.axis_size("seq")
    head_count = lax.axis_size("head")
    reach = count // 2
    info = Meta(count, 2 * pages_dev // count)
    order = ring_order(count)
    ahead = [(order[i], order[(i + 1) % count]) for i in range(count)]
    back = [(b, a) for a, b in ahead]
    middle = tok_rows // 2

    meta = tables(info, pages_dev, page_rows, page_table, prefix_len, suffix_len)
    pages = jnp.transpose(pooled_pages, (0, 2, 1, 3))
    suffix = jnp.transpose(suffix_key_value, (1, 0, 2))

    def partial_of(query, offset, row_base=0):
        return attend(info, meta, query, offset, row_base, tok_rows, pages, suffix)

    from_left = queries
    from_right = queries
    left = []
    right = []
    for step in range(reach):
        end = step == reach - 1
        next_left = lax.ppermute(from_left[:middle] if end else from_left, "seq", ahead)
        next_right = lax.ppermute(from_right[middle:] if end else from_right, "seq", back)
        left.append(partial_of(from_left, -step))
        right.append(partial_of(from_right, step) if step > 0 else left[0])
        if not end:
            next_left, next_right = lax.optimization_barrier(
                ((next_left, next_right), (left[-1], right[-1]))
            )[0]
        from_left, from_right = (next_left, next_right)
    left.append(partial_of(from_left, -reach))
    right.append(partial_of(from_right, reach, middle))
    home = left[0]

    low_left = lax.ppermute(left[reach][0], "seq", back)
    high_right = lax.ppermute(right[reach][0], "seq", ahead)
    high_left = None
    low_right = None
    for step in range(reach - 1, 0, -1):
        low_left = lax.ppermute(merge(low_left, left[step][0]), "seq", back)
        high_right = lax.ppermute(merge(high_right, right[step][1]), "seq", ahead)
        mine_left = left[step][1] if high_left is None else merge(high_left, left[step][1])
        high_left = lax.ppermute(mine_left, "seq", back)
        mine_right = right[step][0] if low_right is None else merge(low_right, right[step][0])
        low_right = lax.ppermute(mine_right, "seq", ahead)

    packed = [home[0], low_left, low_right, home[1], high_left, high_right]
    give, keep = finish(info, meta, packed, out_weight, tok_rows, 0, head_count)
    return reduce_heads(give, keep, out_weight.shape[1] // head_count, head_count)


def solution(mesh):
    placed = (
        P("seq", "head"),
        P("seq", None, "head"),
        P("seq", None, None, "head"),
        P("head", None),
        P(),
        P(),
        P(),
    )
    return jax.shard_map(
        shards, mesh=mesh, in_specs=placed, out_specs=P("seq", "head"), check_vma=False
    )
```

```python
import functools
import math

import jax
import jax.numpy as jnp
from jax import lax
from jax.experimental import pallas as pl
from jax.experimental.pallas import tpu as pltpu
from jax.sharding import PartitionSpec as P

D = 5376
QUERY_HEADS = 32
KEY_VALUE_HEADS = 16
HEAD_WIDTH = 128
GROUP = QUERY_HEADS // KEY_VALUE_HEADS
RATE = float(D // QUERY_HEADS) ** (-0.5) * math.log2(math.e)
HIDDEN = -(2.0**99)
STAT = 128
SUM_HIGH = 32
SUM_LOW = 64
F32 = jnp.float32
BF16 = jnp.bfloat16
MIB = 1 << 20
HINT = pl.CostEstimate(flops=1024, bytes_accessed=1024, transcendentals=0)


def ring_member(place, count):
    return jnp.where(place < count // 2, 2 * place, 2 * (count - 1 - place) + 1)


def ring_order(count):
    return list(range(0, count, 2)) + list(range(count - 1, 0, -2))


def same_request_at(offset, count):
    order = ring_order(count)
    half = count // 2
    return any(order[(i + offset) % count] % half == order[i] % half for i in range(count))


class Meta:
    def __init__(self, count, holding):
        self.count = count
        self.half = count // 2
        self.holding = holding
        self.stride = holding + 1
        self.valid_at = self.half * self.stride
        self.live_at = 2 * self.half * self.stride
        self.suffix_at = self.live_at + self.half
        self.place_at = self.suffix_at + self.half
        self.length = self.place_at + 2

    def chunk(self, meta, offset):
        place = meta[self.place_at] + offset
        place = jnp.where(place < 0, place + self.count, place)
        place = jnp.where(place >= self.count, place - self.count, place)
        return ring_member(place, self.count)

    def request(self, chunk):
        return jnp.where(chunk >= self.half, chunk - self.half, chunk)

    def member(self, chunk):
        return jnp.where(chunk >= self.half, 1, 0)

    def slot(self, meta, request, page):
        return meta[request * self.stride + page]

    def valid(self, meta, request, page):
        return meta[self.valid_at + request * self.stride + page]


def table_kernel(info, pages_dev, page_rows, page_table, prefix_len, suffix_len, meta):
    seq_index = lax.axis_index("seq")
    first_slot = seq_index * pages_dev
    odd = seq_index % 2
    meta[info.place_at] = jnp.where(odd == 0, seq_index // 2, info.count - 1 - seq_index // 2)
    meta[info.place_at + 1] = seq_index

    def one_request(request, carry):
        prefix = prefix_len[request]
        base = request * info.stride

        def one_page(page, state):
            found, live = state
            local = page_table[request, page] - first_slot
            mine = (local >= 0) & (local < pages_dev)
            valid = jnp.minimum(jnp.maximum(prefix - page * page_rows, 0), page_rows)
            meta[base + found] = local
            meta[info.valid_at + base + found] = valid
            return (
                found + jnp.where(mine, 1, 0),
                live + jnp.where(mine & (valid > 0), 1, 0),
            )

        _, live = lax.fori_loop(0, page_table.shape[1], one_page, (0, 0))
        meta[info.live_at + request] = live
        meta[info.suffix_at + request] = suffix_len[request]
        return carry

    lax.fori_loop(0, info.half, one_request, 0)


def tables(info, pages_dev, page_rows, page_table, prefix_len, suffix_len):
    smem = pl.BlockSpec(memory_space=pltpu.SMEM)
    return pl.pallas_call(
        functools.partial(table_kernel, info, pages_dev, page_rows),
        out_shape=jax.ShapeDtypeStruct((info.length,), jnp.int32),
        in_specs=[smem] * 3,
        out_specs=smem,
        cost_estimate=HINT,
        name="tables",
    )(page_table, prefix_len, suffix_len)


def attend_kernel(info, offset, row_base, tok_rows, with_suffix, blocks, meta, q_ref, *refs):
    holding = info.holding
    page_refs = refs[:holding]
    refs = refs[holding:]
    if with_suffix:
        suffix_ref = refs[0]
        refs = refs[1:]
    out_refs = refs[:blocks]
    acc_ref, max_ref, sum_ref = refs[blocks:]
    group = pl.program_id(0)
    rows = q_ref.shape[0] // blocks
    width = HEAD_WIDTH
    tall = GROUP * rows
    chunk = info.chunk(meta, offset)
    request = info.request(chunk)
    member = info.member(chunk)
    suffix = meta[info.suffix_at + request]
    first = member * tok_rows + row_base
    live_pages = meta[info.live_at + request]
    live_blocks = jnp.int32(0)
    for block in range(blocks):
        live_blocks = live_blocks + jnp.where(suffix > first + block * rows, 1, 0)

    def scores_of(query, keys):
        return lax.dot_general(
            query, keys, (((1,), (1,)), ((), ())), preferred_element_type=F32
        )

    def run(some, pages, suffix_keys):
        query = jnp.concatenate(
            [
                q_ref[b * rows : (b + 1) * rows, i * width : (i + 1) * width]
                for b in range(some)
                for i in range(GROUP)
            ],
            axis=0,
        )
        parts = []
        values = []
        if suffix_keys:
            scores = scores_of(query, suffix_ref[0])
            if offset == 0:
                shape = (rows, scores.shape[1])
                row = lax.broadcasted_iota(jnp.int32, shape, 0)
                key = lax.broadcasted_iota(jnp.int32, shape, 1)
                scores = jnp.concatenate(
                    [
                        jnp.where(
                            key <= row + b * rows,
                            scores[(b * GROUP + i) * rows : (b * GROUP + i + 1) * rows],
                            HIDDEN,
                        )
                        for b in range(some)
                        for i in range(GROUP)
                    ],
                    axis=0,
                )
            parts.append(scores)
            values.append(suffix_ref[1])
        for j in range(pages):
            scores = scores_of(query, page_refs[j][0, 0])
            if j == pages - 1:
                column = lax.broadcasted_iota(jnp.int32, scores.shape, 1)
                scores = jnp.where(column < info.valid(meta, request, j), scores, HIDDEN)
            parts.append(scores)
            values.append(page_refs[j][0, 1])
        top = parts[0]
        for part in parts[1:]:
            top = jnp.maximum(top, part)
        row_max = jnp.max(top, axis=1, keepdims=True).astype(BF16).astype(F32)
        total = None
        mixed = None
        for part, value in zip(parts, values):
            weight = jnp.exp2((part - row_max) * RATE)
            total = weight if total is None else total + weight
            product = jnp.dot(weight.astype(BF16), value, preferred_element_type=F32)
            mixed = product if mixed is None else mixed + product
        high = some * tall
        max_ref[:high] = jnp.broadcast_to(row_max, (high, STAT))
        sum_ref[:high] = jnp.broadcast_to(jnp.sum(total, axis=1, keepdims=True), (high, STAT))
        acc_ref[:high] = mixed

    if with_suffix:
        own = meta[info.place_at + 1]
        sees = (request == info.request(own)) & (member >= info.member(own))
        nothing = (live_pages == 0) & jnp.logical_not(sees)
    else:
        nothing = live_pages == 0
    for block in range(blocks):

        @pl.when((live_blocks <= block) | nothing)
        def _(block=block):
            part = slice(block * tall, (block + 1) * tall)
            acc_ref[part] = jnp.zeros((tall, width), F32)
            max_ref[part] = jnp.full((tall, STAT), HIDDEN, F32)
            sum_ref[part] = jnp.zeros((tall, STAT), F32)

    for pages in range(holding + 1):
        for some in range(1, blocks + 1):
            here = (live_blocks == some) & (live_pages == pages)
            if with_suffix:
                pl.when(here & sees)(functools.partial(run, some, pages, True))
                here = here & jnp.logical_not(sees)
            if pages > 0 and offset != 0:
                pl.when(here)(functools.partial(run, some, pages, False))

    stat_at = out_refs[0].shape[1] - STAT
    lane = lax.broadcasted_iota(jnp.int32, (rows, STAT), 1)
    for block, out_ref in enumerate(out_refs):

        @pl.when(group == 0)
        def _(out_ref=out_ref):
            out_ref[:, stat_at:] = jnp.zeros((rows, STAT), BF16)

        stats = out_ref[:, stat_at:].astype(F32)
        for i in range(GROUP):
            start = block * tall + i * rows
            head = group * GROUP + i
            column = pl.multiple_of(head * width, width)
            out_ref[:, pl.ds(column, width)] = acc_ref[start : start + rows, :].astype(BF16)
            total = sum_ref[start : start + rows, :]
            high = total.astype(BF16).astype(F32)
            stats = jnp.where(lane == head, max_ref[start : start + rows, :], stats)
            stats = jnp.where(lane == SUM_HIGH + head, high, stats)
            stats = jnp.where(lane == SUM_LOW + head, total - high, stats)
        out_ref[:, stat_at:] = stats.astype(BF16)


def attend(info, meta, query, offset, row_base, tok_rows, pages, suffix):
    rows = tok_rows // 2
    blocks = query.shape[0] // rows
    columns = query.shape[1]
    holding = info.holding
    kv_local = pages.shape[3] // HEAD_WIDTH
    page_rows = pages.shape[2]
    with_suffix = same_request_at(offset, info.count)

    def page_map(page, group, meta):
        request = info.request(info.chunk(meta, offset))
        return (info.slot(meta, request, page), 0, 0, group)

    in_specs = [pl.BlockSpec((query.shape[0], GROUP * HEAD_WIDTH), lambda g, meta: (0, g))]
    in_specs += [
        pl.BlockSpec((1, 2, page_rows, HEAD_WIDTH), functools.partial(page_map, j))
        for j in range(holding)
    ]
    operands = [query] + [pages] * holding
    if with_suffix:
        in_specs.append(pl.BlockSpec((2, tok_rows, HEAD_WIDTH), lambda g, meta: (0, 0, g)))
        operands.append(suffix)
    out = jax.ShapeDtypeStruct((rows, columns + STAT), BF16)
    return pl.pallas_call(
        functools.partial(
            attend_kernel, info, offset, row_base, tok_rows, with_suffix, blocks
        ),
        grid_spec=pltpu.PrefetchScalarGridSpec(
            num_scalar_prefetch=1,
            grid=(kv_local,),
            in_specs=in_specs,
            out_specs=[pl.BlockSpec((rows, columns + STAT), lambda g, meta: (0, 0))] * blocks,
            scratch_shapes=[
                pltpu.VMEM((query.shape[0] * GROUP, HEAD_WIDTH), F32),
                pltpu.VMEM((query.shape[0] * GROUP, STAT), F32),
                pltpu.VMEM((query.shape[0] * GROUP, STAT), F32),
            ],
        ),
        out_shape=[out] * blocks,
        compiler_params=pltpu.CompilerParams(vmem_limit_bytes=24 * MIB),
        cost_estimate=HINT,
        name="attend",
    )(meta, *operands)


def combine(packed, divided=False):
    stat_at = packed[0].shape[1] - STAT
    stats = [one[:, stat_at:].astype(F32) for one in packed]
    top = stats[0]
    for one in stats[1:]:
        top = jnp.maximum(top, one)
    factors = [jnp.exp2((jnp.minimum(one - top, 0.0)) * RATE) for one in stats]
    total = None
    for one, factor in zip(stats, factors):
        own = pltpu.roll(one, STAT - SUM_HIGH, 1) + pltpu.roll(one, STAT - SUM_LOW, 1)
        total = own * factor if total is None else total + own * factor
    if divided:
        factors = [factor / total for factor in factors]
    heads = []
    for head in range(stat_at // HEAD_WIDTH):
        mixed = None
        for one, factor in zip(packed, factors):
            value = one[:, head * HEAD_WIDTH : (head + 1) * HEAD_WIDTH].astype(F32)
            value = value * factor[:, head : head + 1]
            mixed = value if mixed is None else mixed + value
        heads.append(mixed)
    return (heads, top, total)


def merge_kernel(a_ref, b_ref, out_ref):
    heads, top, total = combine([a_ref[...], b_ref[...]])
    for head, mixed in enumerate(heads):
        out_ref[:, head * HEAD_WIDTH : (head + 1) * HEAD_WIDTH] = mixed.astype(BF16)
    high = total.astype(BF16).astype(F32)
    lane = lax.broadcasted_iota(jnp.int32, top.shape, 1)
    stats = jnp.where(lane < SUM_HIGH, top, 0.0)
    stats = jnp.where((lane >= SUM_HIGH) & (lane < SUM_LOW), pltpu.roll(high, SUM_HIGH, 1), stats)
    low = pltpu.roll(total - high, SUM_LOW, 1)
    stats = jnp.where((lane >= SUM_LOW) & (lane < SUM_LOW + SUM_HIGH), low, stats)
    out_ref[:, len(heads) * HEAD_WIDTH :] = stats.astype(BF16)


def merge(a, b):
    return pl.pallas_call(
        merge_kernel,
        out_shape=jax.ShapeDtypeStruct(a.shape, BF16),
        in_specs=[pl.BlockSpec(memory_space=pltpu.VMEM)] * 2,
        out_specs=pl.BlockSpec(memory_space=pltpu.VMEM),
        compiler_params=pltpu.CompilerParams(vmem_limit_bytes=16 * MIB),
        cost_estimate=HINT,
        name="merge",
    )(a, b)


def window_of(columns, head_count):
    spans = [
        -(-(t + 1) * columns // STAT) - t * columns // STAT for t in range(head_count)
    ]
    return max(spans) * STAT


def window_start(target, columns, head_count):
    start = target * columns // STAT * STAT
    return jnp.minimum(start, columns * head_count - window_of(columns, head_count))


def project(flip, head_count, attention, weight, out_ref, window, sems):
    columns = weight.shape[1] // head_count
    half = head_count // 2
    head_index = lax.axis_index("head")
    core = head_index % 2
    pair = head_index // 2
    if flip:
        core = 1 - core
    copies = []
    for turn in range(half):
        target = 2 * ((pair + turn) % half) + core
        start = pl.multiple_of(window_start(target, columns, head_count), STAT)
        copies.append(
            pltpu.make_async_copy(
                weight.at[:, pl.ds(start, window.shape[2])], window.at[turn], sems.at[turn]
            )
        )
        copies[-1].start()
    rows = attention()
    for turn in range(half):
        copies[turn].wait()
        product = jnp.dot(rows, window[turn], preferred_element_type=F32)
        out_ref[turn] = product.astype(BF16)


def finish_kernel(info, tok_rows, first_row, blocks, head_count, meta, *refs):
    packed = refs[: 3 * blocks]
    weight, rows_ref, give_ref, window, sems = refs[3 * blocks :]
    rows = packed[0].shape[0]

    def attention():
        chunk = info.chunk(meta, 0)
        suffix = meta[info.suffix_at + info.request(chunk)]
        for block in range(blocks):
            heads, _, total = combine(
                [ref[...] for ref in packed[3 * block : 3 * block + 3]], True
            )
            first = info.member(chunk) * tok_rows + first_row + block * rows
            place = first + lax.broadcasted_iota(jnp.int32, heads[0].shape, 0)
            for head, mixed in enumerate(heads):
                value = jnp.where(place < suffix, mixed, 0.0)
                rows_ref[
                    block * rows : (block + 1) * rows,
                    head * HEAD_WIDTH : (head + 1) * HEAD_WIDTH,
                ] = value.astype(BF16)
        return rows_ref[...]

    project(True, head_count, attention, weight, give_ref, window, sems)


def keep_kernel(head_count, rows_ref, weight, keep_ref, window, sems):
    project(False, head_count, lambda: rows_ref[...], weight, keep_ref, window, sems)


def finish(info, meta, packed, weight, tok_rows, first_row, head_count):
    blocks = len(packed) // 3
    depth = weight.shape[0]
    half = head_count // 2
    columns = weight.shape[1] // head_count
    wide = window_of(columns, head_count)
    rows = packed[0].shape[0] * blocks
    vmem = pl.BlockSpec(memory_space=pltpu.VMEM)
    hbm = pl.BlockSpec(memory_space=pl.ANY)
    scratch = [pltpu.VMEM((half, depth, wide), BF16), pltpu.SemaphoreType.DMA((half,))]
    cost = pl.CostEstimate(
        flops=2 * rows * depth * wide * half,
        bytes_accessed=4 * depth * wide * half,
        transcendentals=0,
    )
    params = pltpu.CompilerParams(vmem_limit_bytes=24 * MIB)
    out = jax.ShapeDtypeStruct((half, rows, wide), BF16)
    attention, give = pl.pallas_call(
        functools.partial(finish_kernel, info, tok_rows, first_row, blocks, head_count),
        out_shape=[jax.ShapeDtypeStruct((rows, depth), BF16), out],
        in_specs=[pl.BlockSpec(memory_space=pltpu.SMEM)] + [vmem] * len(packed) + [hbm],
        out_specs=[vmem, vmem],
        scratch_shapes=scratch,
        compiler_params=params,
        cost_estimate=cost,
        name="finish",
    )(meta, *packed, weight)
    keep = pl.pallas_call(
        functools.partial(keep_kernel, head_count),
        out_shape=out,
        in_specs=[vmem, hbm],
        out_specs=vmem,
        scratch_shapes=scratch,
        compiler_params=params,
        cost_estimate=cost,
        name="keep",
    )(attention, weight)
    return (give, keep)


def last_kernel(columns, head_count, before, *refs):
    out_ref, turned = refs[-2:]
    rows = turned.shape[1]
    total = refs[0][0].astype(F32)
    total = total + refs[1][0].astype(F32)
    for ref in refs[2 : -2 - before]:
        total = total + ref[...].astype(F32)
    head_index = lax.axis_index("head")
    shift = head_index * columns - window_start(head_index, columns, head_count)
    turned[...] = total.T
    mine = turned[pl.ds(pl.multiple_of(shift, 8), columns), :].astype(BF16)
    if before:
        out_ref[:, :rows] = refs[-3][...]
        out_ref[:, rows:] = mine
    else:
        out_ref[...] = mine


def last(keep, taken, received, turned, columns, head_count):
    _, rows, wide = keep.shape
    first = pl.BlockSpec((1, rows, wide), lambda i: (0, 0, 0))
    whole = pl.BlockSpec((rows, wide), lambda i: (0, 0))
    earlier = [] if turned is None else [turned]
    out = (columns, rows * (1 + len(earlier)))
    return pl.pallas_call(
        functools.partial(last_kernel, columns, head_count, len(earlier)),
        grid=(1,),
        out_shape=jax.ShapeDtypeStruct(out, BF16),
        in_specs=[first, first]
        + [whole] * len(received)
        + [pl.BlockSpec((columns, rows), lambda i: (0, 0))] * len(earlier),
        out_specs=pl.BlockSpec(out, lambda i: (0, 0)),
        scratch_shapes=[pltpu.VMEM((wide, rows), F32)],
        compiler_params=pltpu.CompilerParams(vmem_limit_bytes=16 * MIB),
        cost_estimate=HINT,
        name="last",
    )(keep, taken, *received, *earlier)


def reduce_heads(give, keep, head_count):
    half = head_count // 2
    taken = lax.ppermute(give, "head", [(i, i ^ 1) for i in range(head_count)])
    received = []
    sent = []
    for step in range(1, half):
        pairs = [(i, (i + 2 * step) % head_count) for i in range(head_count)]
        share = (keep[step].astype(F32) + taken[step].astype(F32)).astype(BF16)
        sent.append(share)
        received.append(lax.ppermute(share, "head", pairs))
    return (keep, taken, received, sent)


def after(value, *others):
    return lax.optimization_barrier((value, others))[0]


def shards(queries, suffix_key_value, pooled_pages, out_weight, page_table, prefix_len, suffix_len):
    tok_rows = queries.shape[0]
    pages_dev, page_rows = pooled_pages.shape[:2]
    count = lax.axis_size("seq")
    head_count = lax.axis_size("head")
    reach = count // 2
    info = Meta(count, 2 * pages_dev // count)
    order = ring_order(count)
    ahead = [(order[i], order[(i + 1) % count]) for i in range(count)]
    back = [(b, a) for a, b in ahead]
    middle = tok_rows // 2

    meta = tables(info, pages_dev, page_rows, page_table, prefix_len, suffix_len)
    pages = jnp.transpose(pooled_pages, (0, 2, 1, 3))
    suffix = jnp.transpose(suffix_key_value, (1, 0, 2))

    def partial_of(query, offset, row_base=0):
        return attend(info, meta, query, offset, row_base, tok_rows, pages, suffix)

    left = [queries]
    right = [queries]
    part_left = {}
    part_right = {}

    def attend_both(step):
        part_left[step] = partial_of(left[step], -step)
        part_right[step] = partial_of(right[step], step)
        return (part_left[step], part_right[step])

    for step in range(1, reach + 1):
        end = step == reach
        next_left = lax.ppermute(left[-1][:middle] if end else left[-1], "seq", ahead)
        next_right = lax.ppermute(right[-1][middle:] if end else right[-1], "seq", back)
        if step == 1:
            done = (meta, pages)
        elif step == reach - 1:
            home = partial_of(queries, 0)
            done = home
        else:
            done = attend_both(step - 1)
        next_left, next_right = after((next_left, next_right), done)
        left.append(next_left)
        right.append(next_right)

    low_right = lax.ppermute(part_right[reach - 1][0], "seq", ahead)
    high_left = lax.ppermute(part_left[reach - 1][1], "seq", back)
    far_left = partial_of(left[reach], -reach)[0]
    far_right = partial_of(right[reach], reach, middle)[0]
    low_left = lax.ppermute(far_left, "seq", back)
    high_right = lax.ppermute(far_right, "seq", ahead)
    late = reach - 2
    left[late], right[late] = after((left[late], right[late]), far_left, far_right)
    attend_both(late)
    high = ()
    for step in range(reach - 1, 0, -1):
        low_left, low_right = after((low_left, low_right), high)
        low = [merge(low_left, part_left[step][0])]
        low_left = lax.ppermute(low[0], "seq", back)
        if step > 1:
            low.append(merge(low_right, part_right[step - 1][0]))
            low_right = lax.ppermute(low[1], "seq", ahead)
        high_left, high_right = after((high_left, high_right), low)
        high = [merge(high_right, part_right[step][1])]
        high_right = lax.ppermute(high[0], "seq", ahead)
        if step > 1:
            high.append(merge(high_left, part_left[step - 1][1]))
            high_left = lax.ppermute(high[1], "seq", back)

    columns = out_weight.shape[1] // head_count
    low = after([home[0], low_left, low_right], high)
    give, keep = finish(info, meta, low, out_weight, tok_rows, 0, head_count)
    shares = reduce_heads(give, keep, head_count)
    turned = last(*shares[:-1], None, columns, head_count)
    high = [home[1], high_left, high_right]
    high[0] = after(high[0], shares[-1])
    give, keep = finish(info, meta, high, out_weight, tok_rows, middle, head_count)
    shares = reduce_heads(give, keep, head_count)
    return last(*shares[:-1], turned, columns, head_count).T


def solution(mesh):
    placed = (
        P("seq", "head"),
        P("seq", None, "head"),
        P("seq", None, None, "head"),
        P("head", None),
        P(),
        P(),
        P(),
    )
    return jax.shard_map(
        shards, mesh=mesh, in_specs=placed, out_specs=P("seq", "head"), check_vma=False
    )
```

```python
import functools
import math

import jax
import jax.numpy as jnp
from jax import lax
from jax.experimental import pallas as pl
from jax.experimental.pallas import tpu as pltpu
from jax.sharding import PartitionSpec as P

D = 5376
QUERY_HEADS = 32
KEY_VALUE_HEADS = 16
HEAD_WIDTH = 128
GROUP = QUERY_HEADS // KEY_VALUE_HEADS
RATE = float(D // QUERY_HEADS) ** (-0.5) * math.log2(math.e)
HIDDEN = -(2.0**99)
STAT = 128
SUM_HIGH = 32
SUM_LOW = 64
F32 = jnp.float32
BF16 = jnp.bfloat16
MIB = 1 << 20
LARGE_VMEM = 52 * MIB
HINT = pl.CostEstimate(flops=1024, bytes_accessed=1024, transcendentals=0)


def ring_member(place, count):
    return jnp.where(place < count // 2, 2 * place, 2 * (count - 1 - place) + 1)


def ring_order(count):
    return list(range(0, count, 2)) + list(range(count - 1, 0, -2))


def same_request_at(offset, count):
    order = ring_order(count)
    half = count // 2
    return any(order[(i + offset) % count] % half == order[i] % half for i in range(count))


class Meta:
    def __init__(self, count, holding):
        self.count = count
        self.half = count // 2
        self.holding = holding
        self.stride = holding + 1
        self.valid_at = self.half * self.stride
        self.live_at = 2 * self.half * self.stride
        self.suffix_at = self.live_at + self.half
        self.place_at = self.suffix_at + self.half
        self.length = self.place_at + 2

    def chunk(self, meta, offset):
        place = meta[self.place_at] + offset
        place = jnp.where(place < 0, place + self.count, place)
        place = jnp.where(place >= self.count, place - self.count, place)
        return ring_member(place, self.count)

    def request(self, chunk):
        return jnp.where(chunk >= self.half, chunk - self.half, chunk)

    def member(self, chunk):
        return jnp.where(chunk >= self.half, 1, 0)

    def slot(self, meta, request, page):
        return meta[request * self.stride + page]

    def valid(self, meta, request, page):
        return meta[self.valid_at + request * self.stride + page]


def table_kernel(info, pages_dev, page_rows, page_table, prefix_len, suffix_len, meta):
    seq_index = lax.axis_index("seq")
    first_slot = seq_index * pages_dev
    odd = seq_index % 2
    meta[info.place_at] = jnp.where(odd == 0, seq_index // 2, info.count - 1 - seq_index // 2)
    meta[info.place_at + 1] = seq_index

    def one_request(request, carry):
        prefix = prefix_len[request]
        base = request * info.stride

        def one_page(page, state):
            found, live = state
            local = page_table[request, page] - first_slot
            mine = (local >= 0) & (local < pages_dev)
            valid = jnp.minimum(jnp.maximum(prefix - page * page_rows, 0), page_rows)
            meta[base + found] = local
            meta[info.valid_at + base + found] = valid
            return (
                found + jnp.where(mine, 1, 0),
                live + jnp.where(mine & (valid > 0), 1, 0),
            )

        _, live = lax.fori_loop(0, page_table.shape[1], one_page, (0, 0))
        meta[info.live_at + request] = live
        meta[info.suffix_at + request] = suffix_len[request]
        return carry

    lax.fori_loop(0, info.half, one_request, 0)


def tables(info, pages_dev, page_rows, page_table, prefix_len, suffix_len):
    smem = pl.BlockSpec(memory_space=pltpu.SMEM)
    return pl.pallas_call(
        functools.partial(table_kernel, info, pages_dev, page_rows),
        out_shape=jax.ShapeDtypeStruct((info.length,), jnp.int32),
        in_specs=[smem] * 3,
        out_specs=smem,
        cost_estimate=HINT,
        name="tables",
    )(page_table, prefix_len, suffix_len)


def attend_kernel(info, offset, row_base, tok_rows, with_suffix, blocks, span, meta, q_ref, *refs):
    holding = info.holding
    page_refs = refs[:holding]
    refs = refs[holding:]
    if with_suffix:
        suffix_ref = refs[0]
        refs = refs[1:]
    out_refs = refs[:blocks]
    acc_ref, max_ref, sum_ref = refs[blocks:]
    step = pl.program_id(0)
    rows = q_ref.shape[0] // blocks
    width = HEAD_WIDTH
    tall = GROUP * rows
    chunk = info.chunk(meta, offset)
    request = info.request(chunk)
    member = info.member(chunk)
    suffix = meta[info.suffix_at + request]
    first = member * tok_rows + row_base
    live_pages = meta[info.live_at + request]
    live_blocks = jnp.int32(0)
    for block in range(blocks):
        live_blocks = live_blocks + jnp.where(suffix > first + block * rows, 1, 0)

    def scores_of(query, keys):
        return lax.dot_general(
            query, keys, (((1,), (1,)), ((), ())), preferred_element_type=F32
        )

    def score_unit(group, block, pages, suffix_keys):
        part = slice(block * rows, (block + 1) * rows)
        lanes = slice(group * width, (group + 1) * width)
        query = jnp.concatenate(
            [
                q_ref[part, (group * GROUP + i) * width : (group * GROUP + i + 1) * width]
                for i in range(GROUP)
            ],
            axis=0,
        )
        scored = []
        if suffix_keys:
            scores = scores_of(query, suffix_ref[0, :, lanes])
            if offset == 0:
                shape = (rows, scores.shape[1])
                row = block * rows + lax.broadcasted_iota(jnp.int32, shape, 0)
                hidden = lax.broadcasted_iota(jnp.int32, shape, 1) > row
                scores = jnp.concatenate(
                    [
                        jnp.where(hidden, HIDDEN, scores[i * rows : (i + 1) * rows])
                        for i in range(GROUP)
                    ],
                    axis=0,
                )
            scored.append(scores)
        for j in range(pages):
            scores = scores_of(query, page_refs[j][0, 0, :, lanes])
            if j >= pages - 2:
                column = lax.broadcasted_iota(jnp.int32, scores.shape, 1)
                scores = jnp.where(column < info.valid(meta, request, j), scores, HIDDEN)
            scored.append(scores)
        return scored

    def weigh_unit(group, block, pages, suffix_keys, scored):
        lanes = slice(group * width, (group + 1) * width)
        values = [suffix_ref[1, :, lanes]] if suffix_keys else []
        values += [page_refs[j][0, 1, :, lanes] for j in range(pages)]
        top = scored[0]
        for scores in scored[1:]:
            top = jnp.maximum(top, scores)
        row_max = jnp.max(top, axis=1, keepdims=True).astype(BF16).astype(F32)
        total = None
        mixed = None
        for scores, value in zip(scored, values):
            weight = jnp.exp2((scores - row_max) * RATE)
            total = weight if total is None else total + weight
            product = jnp.dot(weight.astype(BF16), value, preferred_element_type=F32)
            mixed = product if mixed is None else mixed + product
        at = group * blocks + block
        max_ref[at] = jnp.broadcast_to(row_max, (tall, STAT))
        sum_ref[at] = jnp.broadcast_to(jnp.sum(total, axis=1, keepdims=True), (tall, STAT))
        acc_ref[at] = mixed

    def run(some, pages, suffix_keys):
        units = [(group, block) for group in range(span) for block in range(some)]
        coming = score_unit(*units[0], pages, suffix_keys)
        for number, unit in enumerate(units):
            scored = coming
            if number + 1 < len(units):
                coming = score_unit(*units[number + 1], pages, suffix_keys)
            weigh_unit(*unit, pages, suffix_keys, scored)

    if with_suffix:
        own = meta[info.place_at + 1]
        sees = (request == info.request(own)) & (member >= info.member(own))
        nothing = (live_pages == 0) & jnp.logical_not(sees)
    else:
        nothing = live_pages == 0
    for block in range(blocks):

        @pl.when((live_blocks <= block) | nothing)
        def _(block=block):
            for group in range(span):
                at = group * blocks + block
                acc_ref[at] = jnp.zeros((tall, width), F32)
                max_ref[at] = jnp.full((tall, STAT), HIDDEN, F32)
                sum_ref[at] = jnp.zeros((tall, STAT), F32)

    for pages in [0] + list(range(holding, 0, -2)):
        for some in range(1, blocks + 1):
            here = (live_blocks == some) & (live_pages <= pages) & (live_pages >= pages - 1)
            if pages == 0:
                here = (live_blocks == some) & (live_pages == 0)
            elif pages == 1 or pages == 2:
                here = here & (live_pages > 0)
            if with_suffix:
                pl.when(here & sees)(functools.partial(run, some, pages, True))
                here = here & jnp.logical_not(sees)
            if pages > 0 and offset != 0:
                pl.when(here)(functools.partial(run, some, pages, False))

    stat_at = out_refs[0].shape[1] - STAT
    lane = lax.broadcasted_iota(jnp.int32, (rows, STAT), 1)
    for block, out_ref in enumerate(out_refs):

        @pl.when(step == 0)
        def _(out_ref=out_ref):
            out_ref[:, stat_at:] = jnp.zeros((rows, STAT), BF16)

        stats = out_ref[:, stat_at:].astype(F32)
        for group in range(span):
            at = group * blocks + block
            for i in range(GROUP):
                part = slice(i * rows, (i + 1) * rows)
                head = (step * span + group) * GROUP + i
                column = pl.multiple_of(head * width, width)
                out_ref[:, pl.ds(column, width)] = acc_ref[at, part, :].astype(BF16)
                total = sum_ref[at, part, :]
                high = total.astype(BF16).astype(F32)
                stats = jnp.where(lane == head, max_ref[at, part, :], stats)
                stats = jnp.where(lane == SUM_HIGH + head, high, stats)
                stats = jnp.where(lane == SUM_LOW + head, total - high, stats)
        out_ref[:, stat_at:] = stats.astype(BF16)


def attend(info, meta, query, offset, row_base, tok_rows, pages, suffix):
    rows = tok_rows // 2
    blocks = query.shape[0] // rows
    columns = query.shape[1]
    holding = info.holding
    kv_local = pages.shape[3] // HEAD_WIDTH
    span = 2 if kv_local % 2 == 0 else 1
    page_rows = pages.shape[2]
    with_suffix = same_request_at(offset, info.count)

    def page_map(page, step, meta):
        request = info.request(info.chunk(meta, offset))
        return (info.slot(meta, request, page), 0, 0, step)

    in_specs = [pl.BlockSpec((query.shape[0], span * GROUP * HEAD_WIDTH), lambda g, meta: (0, g))]
    in_specs += [
        pl.BlockSpec((1, 2, page_rows, span * HEAD_WIDTH), functools.partial(page_map, j))
        for j in range(holding)
    ]
    operands = [query] + [pages] * holding
    if with_suffix:
        in_specs.append(
            pl.BlockSpec((2, tok_rows, span * HEAD_WIDTH), lambda g, meta: (0, 0, g))
        )
        operands.append(suffix)
    out = jax.ShapeDtypeStruct((rows, columns + STAT), BF16)
    scratch = pltpu.VMEM((span * blocks, GROUP * rows, STAT), F32)
    return pl.pallas_call(
        functools.partial(
            attend_kernel, info, offset, row_base, tok_rows, with_suffix, blocks, span
        ),
        grid_spec=pltpu.PrefetchScalarGridSpec(
            num_scalar_prefetch=1,
            grid=(kv_local // span,),
            in_specs=in_specs,
            out_specs=[pl.BlockSpec((rows, columns + STAT), lambda g, meta: (0, 0))] * blocks,
            scratch_shapes=[scratch] * 3,
        ),
        out_shape=[out] * blocks,
        compiler_params=pltpu.CompilerParams(vmem_limit_bytes=LARGE_VMEM),
        cost_estimate=HINT,
        name="attend",
    )(meta, *operands)


def combine(packed, divided=False):
    stat_at = packed[0].shape[1] - STAT
    stats = [one[:, stat_at:].astype(F32) for one in packed]
    top = stats[0]
    for one in stats[1:]:
        top = jnp.maximum(top, one)
    factors = [jnp.exp2((jnp.minimum(one - top, 0.0)) * RATE) for one in stats]
    total = None
    for one, factor in zip(stats, factors):
        own = pltpu.roll(one, STAT - SUM_HIGH, 1) + pltpu.roll(one, STAT - SUM_LOW, 1)
        total = own * factor if total is None else total + own * factor
    if divided:
        factors = [factor / total for factor in factors]
    heads = []
    for head in range(stat_at // HEAD_WIDTH):
        mixed = None
        for one, factor in zip(packed, factors):
            value = one[:, head * HEAD_WIDTH : (head + 1) * HEAD_WIDTH].astype(F32)
            value = value * factor[:, head : head + 1]
            mixed = value if mixed is None else mixed + value
        heads.append(mixed)
    return (heads, top, total)


def merge_kernel(a_ref, b_ref, out_ref):
    heads, top, total = combine([a_ref[...], b_ref[...]])
    for head, mixed in enumerate(heads):
        out_ref[:, head * HEAD_WIDTH : (head + 1) * HEAD_WIDTH] = mixed.astype(BF16)
    high = total.astype(BF16).astype(F32)
    lane = lax.broadcasted_iota(jnp.int32, top.shape, 1)
    stats = jnp.where(lane < SUM_HIGH, top, 0.0)
    stats = jnp.where((lane >= SUM_HIGH) & (lane < SUM_LOW), pltpu.roll(high, SUM_HIGH, 1), stats)
    low = pltpu.roll(total - high, SUM_LOW, 1)
    stats = jnp.where((lane >= SUM_LOW) & (lane < SUM_LOW + SUM_HIGH), low, stats)
    out_ref[:, len(heads) * HEAD_WIDTH :] = stats.astype(BF16)


def merge(a, b):
    return pl.pallas_call(
        merge_kernel,
        out_shape=jax.ShapeDtypeStruct(a.shape, BF16),
        in_specs=[pl.BlockSpec(memory_space=pltpu.VMEM)] * 2,
        out_specs=pl.BlockSpec(memory_space=pltpu.VMEM),
        compiler_params=pltpu.CompilerParams(vmem_limit_bytes=16 * MIB),
        cost_estimate=HINT,
        name="merge",
    )(a, b)


def window_of(columns, head_count):
    spans = [
        -(-(t + 1) * columns // STAT) - t * columns // STAT for t in range(head_count)
    ]
    return max(spans) * STAT


def window_start(target, columns, head_count):
    start = target * columns // STAT * STAT
    return jnp.minimum(start, columns * head_count - window_of(columns, head_count))


def project(flip, head_count, attention, weight, out_ref, window, sems):
    columns = weight.shape[1] // head_count
    half = head_count // 2
    head_index = lax.axis_index("head")
    core = head_index % 2
    pair = head_index // 2
    if flip:
        core = 1 - core
    copies = []
    for turn in range(half):
        target = 2 * ((pair + turn) % half) + core
        start = pl.multiple_of(window_start(target, columns, head_count), STAT)
        copies.append(
            pltpu.make_async_copy(
                weight.at[:, pl.ds(start, window.shape[2])], window.at[turn], sems.at[turn]
            )
        )
        copies[-1].start()
    rows = attention()
    for turn in range(half):
        copies[turn].wait()
        product = jnp.dot(rows, window[turn], preferred_element_type=F32)
        out_ref[turn] = product.astype(BF16)


def finish_kernel(info, tok_rows, first_row, blocks, head_count, meta, *refs):
    packed = refs[: 3 * blocks]
    weight, rows_ref, give_ref, window, sems = refs[3 * blocks :]
    rows = packed[0].shape[0]

    def attention():
        chunk = info.chunk(meta, 0)
        suffix = meta[info.suffix_at + info.request(chunk)]
        for block in range(blocks):
            heads, _, total = combine(
                [ref[...] for ref in packed[3 * block : 3 * block + 3]], True
            )
            first = info.member(chunk) * tok_rows + first_row + block * rows
            place = first + lax.broadcasted_iota(jnp.int32, heads[0].shape, 0)
            for head, mixed in enumerate(heads):
                value = jnp.where(place < suffix, mixed, 0.0)
                rows_ref[
                    block * rows : (block + 1) * rows,
                    head * HEAD_WIDTH : (head + 1) * HEAD_WIDTH,
                ] = value.astype(BF16)
        return rows_ref[...]

    project(True, head_count, attention, weight, give_ref, window, sems)


def keep_kernel(head_count, rows_ref, weight, keep_ref, window, sems):
    project(False, head_count, lambda: rows_ref[...], weight, keep_ref, window, sems)


def finish(info, meta, packed, weight, tok_rows, first_row, head_count):
    blocks = len(packed) // 3
    depth = weight.shape[0]
    half = head_count // 2
    columns = weight.shape[1] // head_count
    wide = window_of(columns, head_count)
    rows = packed[0].shape[0] * blocks
    vmem = pl.BlockSpec(memory_space=pltpu.VMEM)
    hbm = pl.BlockSpec(memory_space=pl.ANY)
    scratch = [pltpu.VMEM((half, depth, wide), BF16), pltpu.SemaphoreType.DMA((half,))]
    cost = pl.CostEstimate(
        flops=2 * rows * depth * wide * half,
        bytes_accessed=4 * depth * wide * half,
        transcendentals=0,
    )
    params = pltpu.CompilerParams(vmem_limit_bytes=LARGE_VMEM)
    out = jax.ShapeDtypeStruct((half, rows, wide), BF16)
    attention, give = pl.pallas_call(
        functools.partial(finish_kernel, info, tok_rows, first_row, blocks, head_count),
        out_shape=[jax.ShapeDtypeStruct((rows, depth), BF16), out],
        in_specs=[pl.BlockSpec(memory_space=pltpu.SMEM)] + [vmem] * len(packed) + [hbm],
        out_specs=[vmem, vmem],
        scratch_shapes=scratch,
        compiler_params=params,
        cost_estimate=cost,
        name="finish",
    )(meta, *packed, weight)
    keep = pl.pallas_call(
        functools.partial(keep_kernel, head_count),
        out_shape=out,
        in_specs=[vmem, hbm],
        out_specs=vmem,
        scratch_shapes=scratch,
        compiler_params=params,
        cost_estimate=cost,
        name="keep",
    )(attention, weight)
    return (give, keep)


def last_kernel(columns, head_count, before, *refs):
    out_ref, turned = refs[-2:]
    rows = turned.shape[1]
    total = refs[0][0].astype(F32)
    total = total + refs[1][0].astype(F32)
    for ref in refs[2 : -2 - before]:
        total = total + ref[...].astype(F32)
    head_index = lax.axis_index("head")
    shift = head_index * columns - window_start(head_index, columns, head_count)
    turned[...] = total.T
    mine = turned[pl.ds(pl.multiple_of(shift, 8), columns), :].astype(BF16)
    if before:
        out_ref[:, :rows] = refs[-3][...]
        out_ref[:, rows:] = mine
    else:
        out_ref[...] = mine


def last(keep, taken, received, turned, columns, head_count):
    _, rows, wide = keep.shape
    first = pl.BlockSpec((1, rows, wide), lambda i: (0, 0, 0))
    whole = pl.BlockSpec((rows, wide), lambda i: (0, 0))
    earlier = [] if turned is None else [turned]
    out = (columns, rows * (1 + len(earlier)))
    return pl.pallas_call(
        functools.partial(last_kernel, columns, head_count, len(earlier)),
        grid=(1,),
        out_shape=jax.ShapeDtypeStruct(out, BF16),
        in_specs=[first, first]
        + [whole] * len(received)
        + [pl.BlockSpec((columns, rows), lambda i: (0, 0))] * len(earlier),
        out_specs=pl.BlockSpec(out, lambda i: (0, 0)),
        scratch_shapes=[pltpu.VMEM((wide, rows), F32)],
        compiler_params=pltpu.CompilerParams(vmem_limit_bytes=16 * MIB),
        cost_estimate=HINT,
        name="last",
    )(keep, taken, *received, *earlier)


def reduce_heads(give, keep, earlier, head_count):
    half = head_count // 2
    taken = lax.ppermute(give, "head", [(i, i ^ 1) for i in range(head_count)])
    taken = after(taken, earlier)
    received = []
    sent = []
    for step in range(1, half):
        pairs = [(i, (i + 2 * step) % head_count) for i in range(head_count)]
        share = (keep[step].astype(F32) + taken[step].astype(F32)).astype(BF16)
        sent.append(share)
        received.append(lax.ppermute(share, "head", pairs))
    return (keep, taken, received, sent)


def after(value, *others):
    return lax.optimization_barrier((value, others))[0]


def shards(queries, suffix_key_value, pooled_pages, out_weight, page_table, prefix_len, suffix_len):
    tok_rows = queries.shape[0]
    pages_dev, page_rows = pooled_pages.shape[:2]
    count = lax.axis_size("seq")
    head_count = lax.axis_size("head")
    reach = count // 2
    info = Meta(count, 2 * pages_dev // count)
    order = ring_order(count)
    ahead = [(order[i], order[(i + 1) % count]) for i in range(count)]
    back = [(b, a) for a, b in ahead]
    middle = tok_rows // 2

    meta = tables(info, pages_dev, page_rows, page_table, prefix_len, suffix_len)
    pages = jnp.transpose(pooled_pages, (0, 2, 1, 3))
    suffix = jnp.transpose(suffix_key_value, (1, 0, 2))

    def partial_of(query, offset, row_base=0):
        return attend(info, meta, query, offset, row_base, tok_rows, pages, suffix)

    left = [queries]
    right = [queries]
    part_left = {}
    part_right = {}

    def attend_both(step):
        part_left[step] = partial_of(left[step], -step)
        part_right[step] = partial_of(right[step], step)
        return (part_left[step], part_right[step])

    for step in range(1, reach + 1):
        end = step == reach
        next_left = lax.ppermute(left[-1][:middle] if end else left[-1], "seq", ahead)
        next_right = lax.ppermute(right[-1][middle:] if end else right[-1], "seq", back)
        if step == 1:
            done = (meta, pages)
        elif step == reach - 1:
            home = partial_of(queries, 0)
            done = home
        else:
            done = attend_both(step - 1)
        next_left, next_right = after((next_left, next_right), done)
        left.append(next_left)
        right.append(next_right)

    low_right = lax.ppermute(part_right[reach - 1][0], "seq", ahead)
    high_left = lax.ppermute(part_left[reach - 1][1], "seq", back)
    far_left = partial_of(left[reach], -reach)[0]
    far_right = partial_of(right[reach], reach, middle)[0]
    low_left = lax.ppermute(far_left, "seq", back)
    high_right = lax.ppermute(far_right, "seq", ahead)
    late = reach - 2
    left[late], right[late] = after((left[late], right[late]), far_left, far_right)
    attend_both(late)
    high = ()
    for step in range(reach - 1, 0, -1):
        low_left, low_right = after((low_left, low_right), high)
        low = [merge(low_left, part_left[step][0])]
        low_left = lax.ppermute(low[0], "seq", back)
        if step > 1:
            low.append(merge(low_right, part_right[step - 1][0]))
            low_right = lax.ppermute(low[1], "seq", ahead)
        high_left, high_right = after((high_left, high_right), low)
        high = [merge(high_right, part_right[step][1])]
        high_right = lax.ppermute(high[0], "seq", ahead)
        if step > 1:
            high.append(merge(high_left, part_left[step - 1][1]))
            high_left = lax.ppermute(high[1], "seq", back)

    columns = out_weight.shape[1] // head_count
    low_left, low_right, high_left, high_right = after(
        (low_left, low_right, high_left, high_right)
    )
    low = [home[0], low_left, low_right]
    give, keep = finish(info, meta, low, out_weight, tok_rows, 0, head_count)
    shares = reduce_heads(give, keep, (), head_count)
    turned = last(*shares[:-1], None, columns, head_count)
    high = [home[1], high_left, high_right]
    high[0] = after(high[0], shares[-1])
    give, keep = finish(info, meta, high, out_weight, tok_rows, middle, head_count)
    shares = reduce_heads(give, keep, turned, head_count)
    return last(*shares[:-1], turned, columns, head_count).T


def solution(mesh):
    placed = (
        P("seq", "head"),
        P("seq", None, "head"),
        P("seq", None, None, "head"),
        P("head", None),
        P(),
        P(),
        P(),
    )
    return jax.shard_map(
        shards, mesh=mesh, in_specs=placed, out_specs=P("seq", "head"), check_vma=False
    )
```

```python
import functools
import math

import jax
import jax.numpy as jnp
from jax import lax
from jax.experimental import pallas as pl
from jax.experimental.pallas import tpu as pltpu
from jax.sharding import PartitionSpec as P

D = 5376
QUERY_HEADS = 32
KEY_VALUE_HEADS = 16
HEAD_WIDTH = 128
GROUP = QUERY_HEADS // KEY_VALUE_HEADS
RATE = float(D // QUERY_HEADS) ** (-0.5) * math.log2(math.e)
HIDDEN = -(2.0**99)
STAT = 128
SUM_HIGH = 32
SUM_LOW = 64
F32 = jnp.float32
BF16 = jnp.bfloat16
MIB = 1 << 20
LARGE_VMEM = 52 * MIB
HINT = pl.CostEstimate(flops=1024, bytes_accessed=1024, transcendentals=0)
LONG = pl.CostEstimate(flops=1 << 33, bytes_accessed=1024, transcendentals=0)


def ring_member(place, count):
    return jnp.where(place < count // 2, 2 * place, 2 * (count - 1 - place) + 1)


def ring_order(count):
    return list(range(0, count, 2)) + list(range(count - 1, 0, -2))


def same_request_at(offset, count):
    order = ring_order(count)
    half = count // 2
    return any(order[(i + offset) % count] % half == order[i] % half for i in range(count))


class Meta:
    def __init__(self, count, holding):
        self.count = count
        self.half = count // 2
        self.holding = holding
        self.stride = holding + 1
        self.valid_at = self.half * self.stride
        self.live_at = 2 * self.half * self.stride
        self.suffix_at = self.live_at + self.half
        self.place_at = self.suffix_at + self.half
        self.length = self.place_at + 2

    def chunk(self, meta, offset):
        place = meta[self.place_at] + offset
        place = jnp.where(place < 0, place + self.count, place)
        place = jnp.where(place >= self.count, place - self.count, place)
        return ring_member(place, self.count)

    def request(self, chunk):
        return jnp.where(chunk >= self.half, chunk - self.half, chunk)

    def member(self, chunk):
        return jnp.where(chunk >= self.half, 1, 0)

    def slot(self, meta, request, page):
        return meta[request * self.stride + page]

    def valid(self, meta, request, page):
        return meta[self.valid_at + request * self.stride + page]


def table_kernel(info, pages_dev, page_rows, page_table, prefix_len, suffix_len, meta):
    seq_index = lax.axis_index("seq")
    first_slot = seq_index * pages_dev
    odd = seq_index % 2
    meta[info.place_at] = jnp.where(odd == 0, seq_index // 2, info.count - 1 - seq_index // 2)
    meta[info.place_at + 1] = seq_index

    def one_request(request, carry):
        prefix = prefix_len[request]
        base = request * info.stride

        def one_page(page, state):
            found, live = state
            local = page_table[request, page] - first_slot
            mine = (local >= 0) & (local < pages_dev)
            valid = jnp.minimum(jnp.maximum(prefix - page * page_rows, 0), page_rows)
            meta[base + found] = local
            meta[info.valid_at + base + found] = valid
            return (
                found + jnp.where(mine, 1, 0),
                live + jnp.where(mine & (valid > 0), 1, 0),
            )

        _, live = lax.fori_loop(0, page_table.shape[1], one_page, (0, 0))
        meta[info.live_at + request] = live
        meta[info.suffix_at + request] = suffix_len[request]
        return carry

    lax.fori_loop(0, info.half, one_request, 0)


def tables(info, pages_dev, page_rows, page_table, prefix_len, suffix_len):
    smem = pl.BlockSpec(memory_space=pltpu.SMEM)
    return pl.pallas_call(
        functools.partial(table_kernel, info, pages_dev, page_rows),
        out_shape=jax.ShapeDtypeStruct((info.length,), jnp.int32),
        in_specs=[smem] * 3,
        out_specs=smem,
        cost_estimate=HINT,
        name="tables",
    )(page_table, prefix_len, suffix_len)


def attend_kernel(info, offset, row_base, tok_rows, with_suffix, blocks, span, meta, q_ref, *refs):
    holding = info.holding
    page_refs = refs[:holding]
    refs = refs[holding:]
    if with_suffix:
        suffix_ref = refs[0]
        refs = refs[1:]
    out_refs = refs[:blocks]
    acc_ref, max_ref, sum_ref = refs[blocks:]
    step = pl.program_id(0)
    rows = q_ref.shape[0] // blocks
    width = HEAD_WIDTH
    tall = GROUP * rows
    chunk = info.chunk(meta, offset)
    request = info.request(chunk)
    member = info.member(chunk)
    suffix = meta[info.suffix_at + request]
    first = member * tok_rows + row_base
    live_pages = meta[info.live_at + request]
    live_blocks = jnp.int32(0)
    for block in range(blocks):
        live_blocks = live_blocks + jnp.where(suffix > first + block * rows, 1, 0)

    def scores_of(query, keys):
        return lax.dot_general(
            query, keys, (((1,), (1,)), ((), ())), preferred_element_type=F32
        )

    def score_unit(group, block, pages, suffix_keys):
        part = slice(block * rows, (block + 1) * rows)
        lanes = slice(group * width, (group + 1) * width)
        query = jnp.concatenate(
            [
                q_ref[part, (group * GROUP + i) * width : (group * GROUP + i + 1) * width]
                for i in range(GROUP)
            ],
            axis=0,
        )
        scored = []
        if suffix_keys:
            scores = scores_of(query, suffix_ref[0, :, lanes])
            if offset == 0:
                shape = (rows, scores.shape[1])
                row = block * rows + lax.broadcasted_iota(jnp.int32, shape, 0)
                hidden = lax.broadcasted_iota(jnp.int32, shape, 1) > row
                scores = jnp.concatenate(
                    [
                        jnp.where(hidden, HIDDEN, scores[i * rows : (i + 1) * rows])
                        for i in range(GROUP)
                    ],
                    axis=0,
                )
            scored.append(scores)
        for j in range(pages):
            scores = scores_of(query, page_refs[j][0, 0, :, lanes])
            if j >= pages - 2:
                column = lax.broadcasted_iota(jnp.int32, scores.shape, 1)
                scores = jnp.where(column < info.valid(meta, request, j), scores, HIDDEN)
            scored.append(scores)
        return scored

    def weigh_unit(group, block, pages, suffix_keys, scored):
        lanes = slice(group * width, (group + 1) * width)
        values = [suffix_ref[1, :, lanes]] if suffix_keys else []
        values += [page_refs[j][0, 1, :, lanes] for j in range(pages)]
        top = scored[0]
        for scores in scored[1:]:
            top = jnp.maximum(top, scores)
        row_max = jnp.max(top, axis=1, keepdims=True).astype(BF16).astype(F32)
        total = None
        mixed = None
        for scores, value in zip(scored, values):
            weight = jnp.exp2((scores - row_max) * RATE)
            total = weight if total is None else total + weight
            product = jnp.dot(weight.astype(BF16), value, preferred_element_type=F32)
            mixed = product if mixed is None else mixed + product
        at = group * blocks + block
        max_ref[at] = jnp.broadcast_to(row_max, (tall, STAT))
        sum_ref[at] = jnp.broadcast_to(jnp.sum(total, axis=1, keepdims=True), (tall, STAT))
        acc_ref[at] = mixed

    def run(some, pages, suffix_keys):
        units = [(group, block) for group in range(span) for block in range(some)]
        coming = score_unit(*units[0], pages, suffix_keys)
        for number, unit in enumerate(units):
            scored = coming
            if number + 1 < len(units):
                coming = score_unit(*units[number + 1], pages, suffix_keys)
            weigh_unit(*unit, pages, suffix_keys, scored)

    if with_suffix:
        own = meta[info.place_at + 1]
        sees = (request == info.request(own)) & (member >= info.member(own))
        nothing = (live_pages == 0) & jnp.logical_not(sees)
    else:
        nothing = live_pages == 0
    for block in range(blocks):

        @pl.when((live_blocks <= block) | nothing)
        def _(block=block):
            for group in range(span):
                at = group * blocks + block
                acc_ref[at] = jnp.zeros((tall, width), F32)
                max_ref[at] = jnp.full((tall, STAT), HIDDEN, F32)
                sum_ref[at] = jnp.zeros((tall, STAT), F32)

    for pages in [0] + list(range(holding, 0, -2)):
        for some in range(1, blocks + 1):
            here = (live_blocks == some) & (live_pages <= pages) & (live_pages >= pages - 1)
            if pages == 0:
                here = (live_blocks == some) & (live_pages == 0)
            elif pages == 1 or pages == 2:
                here = here & (live_pages > 0)
            if with_suffix:
                pl.when(here & sees)(functools.partial(run, some, pages, True))
                here = here & jnp.logical_not(sees)
            if pages > 0 and offset != 0:
                pl.when(here)(functools.partial(run, some, pages, False))

    stat_at = out_refs[0].shape[1] - STAT
    lane = lax.broadcasted_iota(jnp.int32, (rows, STAT), 1)
    for block, out_ref in enumerate(out_refs):

        @pl.when(step == 0)
        def _(out_ref=out_ref):
            out_ref[:, stat_at:] = jnp.zeros((rows, STAT), BF16)

        stats = out_ref[:, stat_at:].astype(F32)
        for group in range(span):
            at = group * blocks + block
            for i in range(GROUP):
                part = slice(i * rows, (i + 1) * rows)
                head = (step * span + group) * GROUP + i
                column = pl.multiple_of(head * width, width)
                out_ref[:, pl.ds(column, width)] = acc_ref[at, part, :].astype(BF16)
                total = sum_ref[at, part, :]
                high = total.astype(BF16).astype(F32)
                stats = jnp.where(lane == head, max_ref[at, part, :], stats)
                stats = jnp.where(lane == SUM_HIGH + head, high, stats)
                stats = jnp.where(lane == SUM_LOW + head, total - high, stats)
        out_ref[:, stat_at:] = stats.astype(BF16)


def attend(info, meta, query, offset, row_base, tok_rows, pages, suffix, hint):
    rows = tok_rows // 2
    blocks = query.shape[0] // rows
    columns = query.shape[1]
    holding = info.holding
    kv_local = pages.shape[3] // HEAD_WIDTH
    span = 2 if kv_local % 2 == 0 else 1
    page_rows = pages.shape[2]
    with_suffix = same_request_at(offset, info.count)

    def page_map(page, step, meta):
        request = info.request(info.chunk(meta, offset))
        return (info.slot(meta, request, page), 0, 0, step)

    in_specs = [pl.BlockSpec((query.shape[0], span * GROUP * HEAD_WIDTH), lambda g, meta: (0, g))]
    in_specs += [
        pl.BlockSpec((1, 2, page_rows, span * HEAD_WIDTH), functools.partial(page_map, j))
        for j in range(holding)
    ]
    operands = [query] + [pages] * holding
    if with_suffix:
        in_specs.append(
            pl.BlockSpec((2, tok_rows, span * HEAD_WIDTH), lambda g, meta: (0, 0, g))
        )
        operands.append(suffix)
    out = jax.ShapeDtypeStruct((rows, columns + STAT), BF16)
    scratch = pltpu.VMEM((span * blocks, GROUP * rows, STAT), F32)
    return pl.pallas_call(
        functools.partial(
            attend_kernel, info, offset, row_base, tok_rows, with_suffix, blocks, span
        ),
        grid_spec=pltpu.PrefetchScalarGridSpec(
            num_scalar_prefetch=1,
            grid=(kv_local // span,),
            in_specs=in_specs,
            out_specs=[pl.BlockSpec((rows, columns + STAT), lambda g, meta: (0, 0))] * blocks,
            scratch_shapes=[scratch] * 3,
        ),
        out_shape=[out] * blocks,
        compiler_params=pltpu.CompilerParams(vmem_limit_bytes=LARGE_VMEM),
        cost_estimate=hint,
        name="attend",
    )(meta, *operands)


def combine(packed, divided=False):
    stat_at = packed[0].shape[1] - STAT
    stats = [one[:, stat_at:].astype(F32) for one in packed]
    top = stats[0]
    for one in stats[1:]:
        top = jnp.maximum(top, one)
    factors = [jnp.exp2((jnp.minimum(one - top, 0.0)) * RATE) for one in stats]
    total = None
    for one, factor in zip(stats, factors):
        own = pltpu.roll(one, STAT - SUM_HIGH, 1) + pltpu.roll(one, STAT - SUM_LOW, 1)
        total = own * factor if total is None else total + own * factor
    if divided:
        factors = [factor / total for factor in factors]
    heads = []
    for head in range(stat_at // HEAD_WIDTH):
        mixed = None
        for one, factor in zip(packed, factors):
            value = one[:, head * HEAD_WIDTH : (head + 1) * HEAD_WIDTH].astype(F32)
            value = value * factor[:, head : head + 1]
            mixed = value if mixed is None else mixed + value
        heads.append(mixed)
    return (heads, top, total)


def merge_kernel(a_ref, b_ref, out_ref):
    heads, top, total = combine([a_ref[...], b_ref[...]])
    for head, mixed in enumerate(heads):
        out_ref[:, head * HEAD_WIDTH : (head + 1) * HEAD_WIDTH] = mixed.astype(BF16)
    high = total.astype(BF16).astype(F32)
    lane = lax.broadcasted_iota(jnp.int32, top.shape, 1)
    stats = jnp.where(lane < SUM_HIGH, top, 0.0)
    stats = jnp.where((lane >= SUM_HIGH) & (lane < SUM_LOW), pltpu.roll(high, SUM_HIGH, 1), stats)
    low = pltpu.roll(total - high, SUM_LOW, 1)
    stats = jnp.where((lane >= SUM_LOW) & (lane < SUM_LOW + SUM_HIGH), low, stats)
    out_ref[:, len(heads) * HEAD_WIDTH :] = stats.astype(BF16)


def merge(a, b):
    return pl.pallas_call(
        merge_kernel,
        out_shape=jax.ShapeDtypeStruct(a.shape, BF16),
        in_specs=[pl.BlockSpec(memory_space=pltpu.VMEM)] * 2,
        out_specs=pl.BlockSpec(memory_space=pltpu.VMEM),
        compiler_params=pltpu.CompilerParams(vmem_limit_bytes=16 * MIB),
        cost_estimate=HINT,
        name="merge",
    )(a, b)


def window_of(columns, head_count):
    spans = [
        -(-(t + 1) * columns // STAT) - t * columns // STAT for t in range(head_count)
    ]
    return max(spans) * STAT


def window_start(target, columns, head_count):
    start = target * columns // STAT * STAT
    return jnp.minimum(start, columns * head_count - window_of(columns, head_count))


def project(head_count, wanted, attention, weight, out_refs, window, sems):
    columns = weight.shape[1] // head_count
    half = head_count // 2
    head_index = lax.axis_index("head")
    pair = head_index // 2
    copies = []
    for number, (other, turn) in enumerate(wanted):
        core = head_index % 2
        core = 1 - core if other else core
        target = 2 * ((pair + turn) % half) + core
        start = pl.multiple_of(window_start(target, columns, head_count), STAT)
        copies.append(
            pltpu.make_async_copy(
                weight.at[:, pl.ds(start, window.shape[2])], window.at[number], sems.at[number]
            )
        )
        copies[-1].start()
    rows = attention()
    for number, copy in enumerate(copies):
        copy.wait()
        product = jnp.dot(rows, window[number], preferred_element_type=F32)
        out_refs[number][...] = product.astype(BF16)


def finish_kernel(info, tok_rows, blocks, head_count, wanted, meta, *refs):
    packed = refs[: 3 * blocks]
    weight, rows_ref = refs[3 * blocks : 3 * blocks + 2]
    rest = refs[3 * blocks + 2 :]
    rows = packed[0].shape[0]

    def attention():
        chunk = info.chunk(meta, 0)
        suffix = meta[info.suffix_at + info.request(chunk)]
        for block in range(blocks):
            heads, _, total = combine(
                [ref[...] for ref in packed[3 * block : 3 * block + 3]], True
            )
            first = info.member(chunk) * tok_rows + block * rows
            place = first + lax.broadcasted_iota(jnp.int32, heads[0].shape, 0)
            for head, mixed in enumerate(heads):
                value = jnp.where(place < suffix, mixed, 0.0)
                rows_ref[
                    block * rows : (block + 1) * rows,
                    head * HEAD_WIDTH : (head + 1) * HEAD_WIDTH,
                ] = value.astype(BF16)
        return rows_ref[...]

    project(head_count, wanted, attention, weight, rest[: len(wanted)], *rest[len(wanted) :])


def share_kernel(head_count, wanted, rows_ref, weight, *refs):
    outs = refs[: len(wanted)]
    project(head_count, wanted, lambda: rows_ref[...], weight, outs, *refs[len(wanted) :])


def project_call(kernel, name, wanted, rows, weight, head_count, operands, with_rows, with_meta):
    depth = weight.shape[0]
    wide = window_of(weight.shape[1] // head_count, head_count)
    vmem = pl.BlockSpec(memory_space=pltpu.VMEM)
    smem = [pl.BlockSpec(memory_space=pltpu.SMEM)] * with_meta
    out = [jax.ShapeDtypeStruct((rows, depth), BF16)] * with_rows
    out += [jax.ShapeDtypeStruct((rows, wide), BF16)] * len(wanted)
    return pl.pallas_call(
        kernel,
        out_shape=out,
        in_specs=smem
        + [vmem] * (len(operands) - with_meta)
        + [pl.BlockSpec(memory_space=pl.ANY)],
        out_specs=[vmem] * len(out),
        scratch_shapes=[
            pltpu.VMEM((len(wanted), depth, wide), BF16),
            pltpu.SemaphoreType.DMA((len(wanted),)),
        ],
        compiler_params=pltpu.CompilerParams(vmem_limit_bytes=LARGE_VMEM),
        cost_estimate=HINT,
        name=name,
    )(*operands, weight)


def finish(info, meta, packed, weight, tok_rows, head_count):
    blocks = len(packed) // 3
    half = head_count // 2
    columns = weight.shape[1] // head_count
    far_other = [(True, turn) for turn in range(1, half)]
    far_own = [(False, turn) for turn in range(1, half)]
    swap = [(i, i ^ 1) for i in range(head_count)]
    attention, *given = project_call(
        functools.partial(finish_kernel, info, tok_rows, blocks, head_count, far_other),
        "finish", far_other, tok_rows, weight, head_count, [meta, *packed], 1, 1,
    )
    taken = [lax.ppermute(one, "head", swap) for one in given]
    wanted = far_own + [(True, 0)]
    *kept, near = project_call(
        functools.partial(share_kernel, head_count, wanted),
        "share", wanted, tok_rows, weight, head_count, [attention], 0, 0,
    )
    received = []
    sent = []
    for step in range(1, half):
        pairs = [(i, (i + 2 * step) % head_count) for i in range(head_count)]
        sent.append(
            (kept[step - 1].astype(F32) + taken[step - 1].astype(F32)).astype(BF16)
        )
        received.append(lax.ppermute(sent[-1], "head", pairs))
    near = lax.ppermute(near, "head", swap)
    (own,) = project_call(
        functools.partial(share_kernel, head_count, [(False, 0)]),
        "own", [(False, 0)], tok_rows, weight, head_count, [after(attention, sent)], 0, 0,
    )
    return last([own, near, *received], columns, head_count)


def last_kernel(columns, head_count, *refs):
    out_ref, turned = refs[-2:]
    total = refs[0][...].astype(F32)
    for ref in refs[1:-2]:
        total = total + ref[...].astype(F32)
    head_index = lax.axis_index("head")
    shift = head_index * columns - window_start(head_index, columns, head_count)
    turned[...] = total.T
    out_ref[...] = turned[pl.ds(pl.multiple_of(shift, 8), columns), :].astype(BF16)


def last(shares, columns, head_count):
    rows, wide = shares[0].shape
    vmem = pl.BlockSpec(memory_space=pltpu.VMEM)
    return pl.pallas_call(
        functools.partial(last_kernel, columns, head_count),
        out_shape=jax.ShapeDtypeStruct((columns, rows), BF16),
        in_specs=[vmem] * len(shares),
        out_specs=vmem,
        scratch_shapes=[pltpu.VMEM((wide, rows), F32)],
        compiler_params=pltpu.CompilerParams(vmem_limit_bytes=16 * MIB),
        cost_estimate=HINT,
        name="last",
    )(*shares)


def after(value, *others):
    return lax.optimization_barrier((value, others))[0]


def shards(queries, suffix_key_value, pooled_pages, out_weight, page_table, prefix_len, suffix_len):
    tok_rows = queries.shape[0]
    pages_dev, page_rows = pooled_pages.shape[:2]
    count = lax.axis_size("seq")
    head_count = lax.axis_size("head")
    reach = count // 2
    info = Meta(count, 2 * pages_dev // count)
    order = ring_order(count)
    ahead = [(order[i], order[(i + 1) % count]) for i in range(count)]
    back = [(b, a) for a, b in ahead]
    middle = tok_rows // 2

    meta = tables(info, pages_dev, page_rows, page_table, prefix_len, suffix_len)
    pages = jnp.transpose(pooled_pages, (0, 2, 1, 3))
    suffix = jnp.transpose(suffix_key_value, (1, 0, 2))

    def partial_of(query, offset, row_base=0, hint=HINT):
        return attend(info, meta, query, offset, row_base, tok_rows, pages, suffix, hint)

    left = [queries]
    right = [queries]
    part_left = {}
    part_right = {}

    def attend_both(step):
        part_left[step] = partial_of(left[step], -step)
        part_right[step] = partial_of(right[step], step)
        return (part_left[step], part_right[step])

    for step in range(1, reach + 1):
        end = step == reach
        next_left = lax.ppermute(left[-1][:middle] if end else left[-1], "seq", ahead)
        next_right = lax.ppermute(right[-1][middle:] if end else right[-1], "seq", back)
        if step == 1:
            done = (meta, pages)
        elif step == reach - 1:
            home = partial_of(queries, 0)
            done = home
        else:
            done = attend_both(step - 1)
        next_left, next_right = after((next_left, next_right), done)
        left.append(next_left)
        right.append(next_right)

    low_right = lax.ppermute(part_right[reach - 1][0], "seq", ahead)
    high_left = lax.ppermute(part_left[reach - 1][1], "seq", back)
    far_left = partial_of(left[reach], -reach)[0]
    far_right = partial_of(right[reach], reach, middle)[0]
    low_left = lax.ppermute(far_left, "seq", back)
    high_right = lax.ppermute(far_right, "seq", ahead)
    late = reach - 2
    left[late] = after(left[late], far_left, far_right)
    part_left[late] = partial_of(left[late], -late, 0, LONG)
    latest = part_left[late]

    def onward(travelled, mine, pairs):
        merged = merge(after(travelled, latest), mine)
        return (lax.ppermute(merged, "seq", pairs), merged)

    for step in range(reach - 1, 0, -1):
        low_left, latest = onward(low_left, part_left[step][0], back)
        high_right, latest = onward(high_right, part_right[step][1], ahead)
        if step > 1:
            high_left, latest = onward(high_left, part_left[step - 1][1], back)
            if step == reach - 1:
                right[late] = after(right[late], latest)
                part_right[late] = partial_of(right[late], late, 0, LONG)
                latest = part_right[late]
            low_right, latest = onward(low_right, part_right[step - 1][0], ahead)

    packed = [home[0], low_left, low_right, home[1], high_left, high_right]
    return finish(info, meta, packed, out_weight, tok_rows, head_count).T


def solution(mesh):
    placed = (
        P("seq", "head"),
        P("seq", None, "head"),
        P("seq", None, None, "head"),
        P("head", None),
        P(),
        P(),
        P(),
    )
    return jax.shard_map(
        shards, mesh=mesh, in_specs=placed, out_specs=P("seq", "head"), check_vma=False
    )
```

```python
import functools
import math

import jax
import jax.numpy as jnp
from jax import lax
from jax.experimental import pallas as pl
from jax.experimental.pallas import tpu as pltpu
from jax.sharding import PartitionSpec as P

D = 5376
QUERY_HEADS = 32
KEY_VALUE_HEADS = 16
HEAD_WIDTH = 128
GROUP = QUERY_HEADS // KEY_VALUE_HEADS
RATE = float(D // QUERY_HEADS) ** (-0.5) * math.log2(math.e)
HIDDEN = -(2.0**99)
STAT = 128
SUM_HIGH = 32
SUM_LOW = 64
F32 = jnp.float32
BF16 = jnp.bfloat16
MIB = 1 << 20
LARGE_VMEM = 52 * MIB
HINT = pl.CostEstimate(flops=1024, bytes_accessed=1024, transcendentals=0)
LONG = pl.CostEstimate(flops=1 << 33, bytes_accessed=1024, transcendentals=0)


def ring_member(place, count):
    return jnp.where(place < count // 2, 2 * place, 2 * (count - 1 - place) + 1)


def ring_order(count):
    return list(range(0, count, 2)) + list(range(count - 1, 0, -2))


def same_request_at(offset, count):
    order = ring_order(count)
    half = count // 2
    return any(order[(i + offset) % count] % half == order[i] % half for i in range(count))


class Meta:
    def __init__(self, count, holding):
        self.count = count
        self.half = count // 2
        self.holding = holding
        self.stride = holding + 1
        self.valid_at = self.half * self.stride
        self.live_at = 2 * self.half * self.stride
        self.suffix_at = self.live_at + self.half
        self.place_at = self.suffix_at + self.half
        self.length = self.place_at + 2

    def chunk(self, meta, offset):
        place = meta[self.place_at] + offset
        place = jnp.where(place < 0, place + self.count, place)
        place = jnp.where(place >= self.count, place - self.count, place)
        return ring_member(place, self.count)

    def request(self, chunk):
        return jnp.where(chunk >= self.half, chunk - self.half, chunk)

    def member(self, chunk):
        return jnp.where(chunk >= self.half, 1, 0)

    def slot(self, meta, request, page):
        return meta[request * self.stride + page]

    def valid(self, meta, request, page):
        return meta[self.valid_at + request * self.stride + page]


def table_kernel(info, pages_dev, page_rows, page_table, prefix_len, suffix_len, meta):
    seq_index = lax.axis_index("seq")
    first_slot = seq_index * pages_dev
    odd = seq_index % 2
    meta[info.place_at] = jnp.where(odd == 0, seq_index // 2, info.count - 1 - seq_index // 2)
    meta[info.place_at + 1] = seq_index

    def one_request(request, carry):
        prefix = prefix_len[request]
        base = request * info.stride

        def one_page(page, state):
            found, live = state
            local = page_table[request, page] - first_slot
            mine = (local >= 0) & (local < pages_dev)
            valid = jnp.minimum(jnp.maximum(prefix - page * page_rows, 0), page_rows)
            meta[base + found] = local
            meta[info.valid_at + base + found] = valid
            return (
                found + jnp.where(mine, 1, 0),
                live + jnp.where(mine & (valid > 0), 1, 0),
            )

        _, live = lax.fori_loop(0, page_table.shape[1], one_page, (0, 0))
        meta[info.live_at + request] = live
        meta[info.suffix_at + request] = suffix_len[request]
        return carry

    lax.fori_loop(0, info.half, one_request, 0)


def tables(info, pages_dev, page_rows, page_table, prefix_len, suffix_len):
    smem = pl.BlockSpec(memory_space=pltpu.SMEM)
    return pl.pallas_call(
        functools.partial(table_kernel, info, pages_dev, page_rows),
        out_shape=jax.ShapeDtypeStruct((info.length,), jnp.int32),
        in_specs=[smem] * 3,
        out_specs=smem,
        cost_estimate=HINT,
        name="tables",
    )(page_table, prefix_len, suffix_len)


def attend_kernel(info, offset, row_base, tok_rows, with_suffix, blocks, span, meta, q_ref, *refs):
    holding = info.holding
    page_refs = refs[:holding]
    refs = refs[holding:]
    if with_suffix:
        suffix_ref = refs[0]
        refs = refs[1:]
    out_refs = refs[:blocks]
    acc_ref, max_ref, sum_ref = refs[blocks:]
    step = pl.program_id(0)
    rows = q_ref.shape[0] // blocks
    width = HEAD_WIDTH
    tall = GROUP * rows
    chunk = info.chunk(meta, offset)
    request = info.request(chunk)
    member = info.member(chunk)
    suffix = meta[info.suffix_at + request]
    first = member * tok_rows + row_base
    live_pages = meta[info.live_at + request]
    live_blocks = jnp.int32(0)
    for block in range(blocks):
        live_blocks = live_blocks + jnp.where(suffix > first + block * rows, 1, 0)

    def scores_of(query, keys):
        return lax.dot_general(
            query, keys, (((1,), (1,)), ((), ())), preferred_element_type=F32
        )

    def score_unit(group, block, pages, suffix_keys):
        part = slice(block * rows, (block + 1) * rows)
        lanes = slice(group * width, (group + 1) * width)
        query = jnp.concatenate(
            [
                q_ref[part, (group * GROUP + i) * width : (group * GROUP + i + 1) * width]
                for i in range(GROUP)
            ],
            axis=0,
        )
        scored = []
        if suffix_keys:
            scores = scores_of(query, suffix_ref[0, :, lanes])
            if offset == 0:
                shape = (rows, scores.shape[1])
                row = block * rows + lax.broadcasted_iota(jnp.int32, shape, 0)
                hidden = lax.broadcasted_iota(jnp.int32, shape, 1) > row
                scores = jnp.concatenate(
                    [
                        jnp.where(hidden, HIDDEN, scores[i * rows : (i + 1) * rows])
                        for i in range(GROUP)
                    ],
                    axis=0,
                )
            scored.append(scores)
        for j in range(pages):
            scores = scores_of(query, page_refs[j][0, 0, :, lanes])
            if j >= pages - 2:
                column = lax.broadcasted_iota(jnp.int32, scores.shape, 1)
                scores = jnp.where(column < info.valid(meta, request, j), scores, HIDDEN)
            scored.append(scores)
        return scored

    def weigh_unit(group, block, pages, suffix_keys, scored):
        lanes = slice(group * width, (group + 1) * width)
        values = [suffix_ref[1, :, lanes]] if suffix_keys else []
        values += [page_refs[j][0, 1, :, lanes] for j in range(pages)]
        top = scored[0]
        for scores in scored[1:]:
            top = jnp.maximum(top, scores)
        row_max = jnp.max(top, axis=1, keepdims=True).astype(BF16).astype(F32)
        total = None
        mixed = None
        for scores, value in zip(scored, values):
            weight = jnp.exp2((scores - row_max) * RATE)
            total = weight if total is None else total + weight
            product = jnp.dot(weight.astype(BF16), value, preferred_element_type=F32)
            mixed = product if mixed is None else mixed + product
        at = group * blocks + block
        max_ref[at] = jnp.broadcast_to(row_max, (tall, STAT))
        sum_ref[at] = jnp.broadcast_to(jnp.sum(total, axis=1, keepdims=True), (tall, STAT))
        acc_ref[at] = mixed

    def run(some, pages, suffix_keys):
        units = [(group, block) for group in range(span) for block in range(some)]
        coming = score_unit(*units[0], pages, suffix_keys)
        for number, unit in enumerate(units):
            scored = coming
            if number + 1 < len(units):
                coming = score_unit(*units[number + 1], pages, suffix_keys)
            weigh_unit(*unit, pages, suffix_keys, scored)

    if with_suffix:
        own = meta[info.place_at + 1]
        sees = (request == info.request(own)) & (member >= info.member(own))
        nothing = (live_pages == 0) & jnp.logical_not(sees)
    else:
        nothing = live_pages == 0
    for block in range(blocks):

        @pl.when((live_blocks <= block) | nothing)
        def _(block=block):
            for group in range(span):
                at = group * blocks + block
                acc_ref[at] = jnp.zeros((tall, width), F32)
                max_ref[at] = jnp.full((tall, STAT), HIDDEN, F32)
                sum_ref[at] = jnp.zeros((tall, STAT), F32)

    for pages in [0] + list(range(holding, 0, -2)):
        for some in range(1, blocks + 1):
            here = (live_blocks == some) & (live_pages <= pages) & (live_pages >= pages - 1)
            if pages == 0:
                here = (live_blocks == some) & (live_pages == 0)
            elif pages == 1 or pages == 2:
                here = here & (live_pages > 0)
            if with_suffix:
                pl.when(here & sees)(functools.partial(run, some, pages, True))
                here = here & jnp.logical_not(sees)
            if pages > 0 and offset != 0:
                pl.when(here)(functools.partial(run, some, pages, False))

    stat_at = out_refs[0].shape[1] - STAT
    lane = lax.broadcasted_iota(jnp.int32, (rows, STAT), 1)
    for block, out_ref in enumerate(out_refs):

        @pl.when(step == 0)
        def _(out_ref=out_ref):
            out_ref[:, stat_at:] = jnp.zeros((rows, STAT), BF16)

        stats = out_ref[:, stat_at:].astype(F32)
        for group in range(span):
            at = group * blocks + block
            for i in range(GROUP):
                part = slice(i * rows, (i + 1) * rows)
                head = (step * span + group) * GROUP + i
                column = pl.multiple_of(head * width, width)
                out_ref[:, pl.ds(column, width)] = acc_ref[at, part, :].astype(BF16)
                total = sum_ref[at, part, :]
                high = total.astype(BF16).astype(F32)
                stats = jnp.where(lane == head, max_ref[at, part, :], stats)
                stats = jnp.where(lane == SUM_HIGH + head, high, stats)
                stats = jnp.where(lane == SUM_LOW + head, total - high, stats)
        out_ref[:, stat_at:] = stats.astype(BF16)


def attend(info, meta, query, offset, row_base, tok_rows, pages, suffix, hint):
    rows = tok_rows // 2
    blocks = query.shape[0] // rows
    columns = query.shape[1]
    holding = info.holding
    kv_local = pages.shape[3] // HEAD_WIDTH
    span = 2 if kv_local % 2 == 0 else 1
    page_rows = pages.shape[2]
    with_suffix = same_request_at(offset, info.count)

    def page_map(page, step, meta):
        request = info.request(info.chunk(meta, offset))
        return (info.slot(meta, request, page), 0, 0, step)

    in_specs = [pl.BlockSpec((query.shape[0], span * GROUP * HEAD_WIDTH), lambda g, meta: (0, g))]
    in_specs += [
        pl.BlockSpec((1, 2, page_rows, span * HEAD_WIDTH), functools.partial(page_map, j))
        for j in range(holding)
    ]
    operands = [query] + [pages] * holding
    if with_suffix:
        in_specs.append(
            pl.BlockSpec((2, tok_rows, span * HEAD_WIDTH), lambda g, meta: (0, 0, g))
        )
        operands.append(suffix)
    out = jax.ShapeDtypeStruct((rows, columns + STAT), BF16)
    scratch = pltpu.VMEM((span * blocks, GROUP * rows, STAT), F32)
    return pl.pallas_call(
        functools.partial(
            attend_kernel, info, offset, row_base, tok_rows, with_suffix, blocks, span
        ),
        grid_spec=pltpu.PrefetchScalarGridSpec(
            num_scalar_prefetch=1,
            grid=(kv_local // span,),
            in_specs=in_specs,
            out_specs=[pl.BlockSpec((rows, columns + STAT), lambda g, meta: (0, 0))] * blocks,
            scratch_shapes=[scratch] * 3,
        ),
        out_shape=[out] * blocks,
        compiler_params=pltpu.CompilerParams(vmem_limit_bytes=LARGE_VMEM),
        cost_estimate=hint,
        name="attend",
    )(meta, *operands)


def combine(packed, divided=False):
    stat_at = packed[0].shape[1] - STAT
    stats = [one[:, stat_at:].astype(F32) for one in packed]
    top = stats[0]
    for one in stats[1:]:
        top = jnp.maximum(top, one)
    factors = [jnp.exp2((jnp.minimum(one - top, 0.0)) * RATE) for one in stats]
    total = None
    for one, factor in zip(stats, factors):
        own = pltpu.roll(one, STAT - SUM_HIGH, 1) + pltpu.roll(one, STAT - SUM_LOW, 1)
        total = own * factor if total is None else total + own * factor
    if divided:
        factors = [factor / total for factor in factors]
    heads = []
    for head in range(stat_at // HEAD_WIDTH):
        mixed = None
        for one, factor in zip(packed, factors):
            value = one[:, head * HEAD_WIDTH : (head + 1) * HEAD_WIDTH].astype(F32)
            value = value * factor[:, head : head + 1]
            mixed = value if mixed is None else mixed + value
        heads.append(mixed)
    return (heads, top, total)


def merge_kernel(a_ref, b_ref, out_ref):
    heads, top, total = combine([a_ref[...], b_ref[...]])
    for head, mixed in enumerate(heads):
        out_ref[:, head * HEAD_WIDTH : (head + 1) * HEAD_WIDTH] = mixed.astype(BF16)
    high = total.astype(BF16).astype(F32)
    lane = lax.broadcasted_iota(jnp.int32, top.shape, 1)
    stats = jnp.where(lane < SUM_HIGH, top, 0.0)
    stats = jnp.where((lane >= SUM_HIGH) & (lane < SUM_LOW), pltpu.roll(high, SUM_HIGH, 1), stats)
    low = pltpu.roll(total - high, SUM_LOW, 1)
    stats = jnp.where((lane >= SUM_LOW) & (lane < SUM_LOW + SUM_HIGH), low, stats)
    out_ref[:, len(heads) * HEAD_WIDTH :] = stats.astype(BF16)


def merge(a, b):
    return pl.pallas_call(
        merge_kernel,
        out_shape=jax.ShapeDtypeStruct(a.shape, BF16),
        in_specs=[pl.BlockSpec(memory_space=pltpu.VMEM)] * 2,
        out_specs=pl.BlockSpec(memory_space=pltpu.VMEM),
        compiler_params=pltpu.CompilerParams(vmem_limit_bytes=16 * MIB),
        cost_estimate=HINT,
        name="merge",
    )(a, b)


def window_of(columns, head_count):
    spans = [
        -(-(t + 1) * columns // STAT) - t * columns // STAT for t in range(head_count)
    ]
    return max(spans) * STAT


def window_start(target, columns, head_count):
    start = target * columns // STAT * STAT
    return jnp.minimum(start, columns * head_count - window_of(columns, head_count))


def project(head_count, wanted, attention, weight, out_refs, window, sems):
    columns = weight.shape[1] // head_count
    half = head_count // 2
    head_index = lax.axis_index("head")
    pair = head_index // 2
    copies = []
    for number, (other, turn) in enumerate(wanted):
        core = head_index % 2
        core = 1 - core if other else core
        target = 2 * ((pair + turn) % half) + core
        start = pl.multiple_of(window_start(target, columns, head_count), STAT)
        copies.append(
            pltpu.make_async_copy(
                weight.at[:, pl.ds(start, window.shape[2])], window.at[number], sems.at[number]
            )
        )
        copies[-1].start()
    rows = attention()
    for number, copy in enumerate(copies):
        copy.wait()
        product = jnp.dot(rows, window[number], preferred_element_type=F32)
        out_refs[number][...] = product.astype(BF16)


def finish_kernel(info, tok_rows, first_row, shares, head_count, wanted, meta, *refs):
    weight, rows_ref = refs[shares : shares + 2]
    rest = refs[shares + 2 :]

    def attention():
        chunk = info.chunk(meta, 0)
        suffix = meta[info.suffix_at + info.request(chunk)]
        heads, _, total = combine([ref[...] for ref in refs[:shares]], True)
        first = info.member(chunk) * tok_rows + first_row
        place = first + lax.broadcasted_iota(jnp.int32, heads[0].shape, 0)
        for head, mixed in enumerate(heads):
            value = jnp.where(place < suffix, mixed, 0.0)
            rows_ref[:, head * HEAD_WIDTH : (head + 1) * HEAD_WIDTH] = value.astype(BF16)
        return rows_ref[...]

    project(head_count, wanted, attention, weight, rest[: len(wanted)], *rest[len(wanted) :])


def share_kernel(head_count, wanted, parts, *refs):
    weight = refs[parts]
    outs = refs[parts + 1 : parts + 1 + len(wanted)]

    def attention():
        return jnp.concatenate([ref[...] for ref in refs[:parts]], axis=0)

    project(head_count, wanted, attention, weight, outs, *refs[parts + 1 + len(wanted) :])


def project_call(kernel, name, wanted, rows, weight, head_count, operands, with_rows, with_meta):
    depth = weight.shape[0]
    wide = window_of(weight.shape[1] // head_count, head_count)
    vmem = pl.BlockSpec(memory_space=pltpu.VMEM)
    smem = [pl.BlockSpec(memory_space=pltpu.SMEM)] * with_meta
    out = [jax.ShapeDtypeStruct((rows, depth), BF16)] * with_rows
    out += [jax.ShapeDtypeStruct((rows, wide), BF16)] * len(wanted)
    return pl.pallas_call(
        kernel,
        out_shape=out,
        in_specs=smem
        + [vmem] * (len(operands) - with_meta)
        + [pl.BlockSpec(memory_space=pl.ANY)],
        out_specs=[vmem] * len(out),
        scratch_shapes=[
            pltpu.VMEM((len(wanted), depth, wide), BF16),
            pltpu.SemaphoreType.DMA((len(wanted),)),
        ],
        compiler_params=pltpu.CompilerParams(vmem_limit_bytes=LARGE_VMEM),
        cost_estimate=HINT,
        name=name,
    )(*operands, weight)


def share(name, wanted, attention, weight, head_count):
    return project_call(
        functools.partial(share_kernel, head_count, wanted, len(attention)),
        name,
        wanted,
        sum(part.shape[0] for part in attention),
        weight,
        head_count,
        list(attention),
        0,
        0,
    )


def finish(info, meta, packed, first_row, weight, tok_rows, head_count):
    half = head_count // 2
    other = [(True, turn) for turn in range(1, half)]
    own = [(False, turn) for turn in range(1, half)]
    attention, *given = project_call(
        functools.partial(
            finish_kernel, info, tok_rows, first_row, len(packed), head_count, other
        ),
        "finish",
        other,
        packed[0].shape[0],
        weight,
        head_count,
        [meta, *packed],
        1,
        1,
    )
    taken = [swap_cores(one, head_count, 2) for one in given]
    return (attention, share("far", own, [attention], weight, head_count), taken)


def swap_cores(value, head_count, pieces):
    rows = value.shape[0] // pieces
    pairs = [(i, i ^ 1) for i in range(head_count)]
    return [
        lax.ppermute(value[i * rows : (i + 1) * rows], "head", pairs) for i in range(pieces)
    ]


def send_far(kept, taken, head_count):
    sent = []
    received = []
    for number, (mine, theirs) in enumerate(zip(kept, taken)):
        step = number + 1
        pairs = [(i, (i + 2 * step) % head_count) for i in range(head_count)]
        theirs = jnp.concatenate(theirs, axis=0)
        sent.append((mine.astype(F32) + theirs.astype(F32)).astype(BF16))
        received.append(lax.ppermute(sent[-1], "head", pairs))
    return (sent, received)


def last_kernel(columns, head_count, pieces, own_ref, *refs):
    near_refs = refs[:pieces]
    refs = refs[pieces:]
    out_ref, turned = refs[-2:]
    halves = [refs[: (len(refs) - 2) // 2], refs[(len(refs) - 2) // 2 : -2]]
    head_index = lax.axis_index("head")
    shift = head_index * columns - window_start(head_index, columns, head_count)
    rows = own_ref.shape[0] // 2
    for number, received in enumerate(halves):
        part = slice(number * rows, (number + 1) * rows)
        near = near_refs[number * pieces // 2 : (number + 1) * pieces // 2]
        total = own_ref[part].astype(F32)
        total = total + jnp.concatenate([ref[...] for ref in near], axis=0).astype(F32)
        for ref in received:
            total = total + ref[...].astype(F32)
        turned[:, part] = total.T
    out_ref[...] = turned[pl.ds(pl.multiple_of(shift, 8), columns), :].astype(BF16)


def last(own, near, received, columns, head_count):
    rows, wide = own.shape
    vmem = pl.BlockSpec(memory_space=pltpu.VMEM)
    return pl.pallas_call(
        functools.partial(last_kernel, columns, head_count, len(near)),
        out_shape=jax.ShapeDtypeStruct((columns, rows), BF16),
        in_specs=[vmem] * (1 + len(near) + len(received)),
        out_specs=vmem,
        scratch_shapes=[pltpu.VMEM((wide, rows), F32)],
        compiler_params=pltpu.CompilerParams(vmem_limit_bytes=16 * MIB),
        cost_estimate=HINT,
        name="last",
    )(own, *near, *received)


def after(value, *others):
    return lax.optimization_barrier((value, others))[0]


def shards(queries, suffix_key_value, pooled_pages, out_weight, page_table, prefix_len, suffix_len):
    tok_rows = queries.shape[0]
    pages_dev, page_rows = pooled_pages.shape[:2]
    count = lax.axis_size("seq")
    head_count = lax.axis_size("head")
    reach = count // 2
    info = Meta(count, 2 * pages_dev // count)
    order = ring_order(count)
    ahead = [(order[i], order[(i + 1) % count]) for i in range(count)]
    back = [(b, a) for a, b in ahead]
    middle = tok_rows // 2

    meta = tables(info, pages_dev, page_rows, page_table, prefix_len, suffix_len)
    pages = jnp.transpose(pooled_pages, (0, 2, 1, 3))
    suffix = jnp.transpose(suffix_key_value, (1, 0, 2))

    def partial_of(query, offset, row_base=0, hint=HINT):
        return attend(info, meta, query, offset, row_base, tok_rows, pages, suffix, hint)

    left = [queries]
    right = [queries]
    part_left = {}
    part_right = {}
    late = reach - 2

    def attend_both(step):
        part_left[step] = partial_of(left[step], -step)
        part_right[step] = partial_of(right[step], step)
        return (part_left[step], part_right[step])

    for step in range(1, reach + 1):
        end = step == reach
        next_left = lax.ppermute(left[-1][:middle] if end else left[-1], "seq", ahead)
        next_right = lax.ppermute(right[-1][middle:] if end else right[-1], "seq", back)
        if step == 1:
            done = (meta, pages)
        elif step == reach - 1:
            home = partial_of(queries, 0)
            part_left[late] = partial_of(left[late], -late)
            done = (home, part_left[late])
        else:
            done = attend_both(step - 1)
        next_left, next_right = after((next_left, next_right), done)
        left.append(next_left)
        right.append(next_right)

    low_right = lax.ppermute(part_right[reach - 1][0], "seq", ahead)
    high_left = lax.ppermute(part_left[reach - 1][1], "seq", back)
    far_left = partial_of(left[reach], -reach)[0]
    far_right = partial_of(right[reach], reach, middle)[0]
    low_left = lax.ppermute(far_left, "seq", back)
    high_right = lax.ppermute(far_right, "seq", ahead)
    right[late] = after(right[late], far_left, far_right)
    part_right[late] = partial_of(right[late], late, 0, LONG)
    latest = part_right[late]

    def onward(travelled, mine, pairs):
        merged = merge(after(travelled, latest), mine)
        return (lax.ppermute(merged, "seq", pairs), merged)

    for step in range(reach - 1, 1, -1):
        low_left, latest = onward(low_left, part_left[step][0], back)
        if step == 2:
            low_right, latest = onward(low_right, part_right[step - 1][0], ahead)
            high_right, latest = onward(high_right, part_right[step][1], ahead)
        else:
            high_right, latest = onward(high_right, part_right[step][1], ahead)
            high_left, latest = onward(high_left, part_left[step - 1][1], back)
            low_right, latest = onward(low_right, part_right[step - 1][0], ahead)
    low_left, latest = onward(low_left, part_left[1][0], back)
    high_left, latest = onward(high_left, part_left[1][1], back)
    high_right, latest = onward(high_right, part_right[1][1], ahead)

    low = [merge(after(low_right, latest), home[0]), low_left]
    rest = (out_weight, tok_rows, head_count)
    rows_low, kept, taken = finish(info, meta, low, 0, *rest)
    taken, high_left, high_right = after((taken, high_left, high_right))
    sent, received_low = send_far(kept, taken, head_count)
    high = [after(home[1], sent), high_left, high_right]
    rows_high, kept, taken = finish(info, meta, high, middle, *rest)
    taken, received_low = after((taken, received_low))
    sent, received_high = send_far(kept, taken, head_count)
    near, own = share(
        "near",
        [(True, 0), (False, 0)],
        after([rows_low, rows_high], sent),
        out_weight,
        head_count,
    )
    near = after(swap_cores(near, head_count, 4), received_high)
    columns = out_weight.shape[1] // head_count
    return last(own, near, received_low + received_high, columns, head_count).T


def solution(mesh):
    placed = (
        P("seq", "head"),
        P("seq", None, "head"),
        P("seq", None, None, "head"),
        P("head", None),
        P(),
        P(),
        P(),
    )
    return jax.shard_map(
        shards, mesh=mesh, in_specs=placed, out_specs=P("seq", "head"), check_vma=False
    )
```

```python
import functools
import math

import jax
import jax.numpy as jnp
from jax import lax
from jax.experimental import pallas as pl
from jax.experimental.pallas import tpu as pltpu
from jax.sharding import PartitionSpec as P

D = 5376
QUERY_HEADS = 32
KEY_VALUE_HEADS = 16
HEAD_WIDTH = 128
GROUP = QUERY_HEADS // KEY_VALUE_HEADS
RATE = float(D // QUERY_HEADS) ** (-0.5) * math.log2(math.e)
HIDDEN = -(2.0**99)
STAT = 128
SUM_HIGH = 32
SUM_LOW = 64
F32 = jnp.float32
BF16 = jnp.bfloat16
MIB = 1 << 20
LARGE_VMEM = 52 * MIB
ATTEND_VMEM = 24 * MIB
HINT = pl.CostEstimate(flops=1024, bytes_accessed=1024, transcendentals=0)
LONG = pl.CostEstimate(flops=1 << 33, bytes_accessed=1024, transcendentals=0)


def ring_member(place, count):
    return jnp.where(place < count // 2, 2 * place, 2 * (count - 1 - place) + 1)


def ring_order(count):
    return list(range(0, count, 2)) + list(range(count - 1, 0, -2))


def same_request_at(offset, count):
    order = ring_order(count)
    half = count // 2
    return any(order[(i + offset) % count] % half == order[i] % half for i in range(count))


class Meta:
    def __init__(self, count, holding):
        self.count = count
        self.half = count // 2
        self.holding = holding
        self.stride = holding + 1
        self.valid_at = self.half * self.stride
        self.live_at = 2 * self.half * self.stride
        self.suffix_at = self.live_at + self.half
        self.place_at = self.suffix_at + self.half
        self.length = self.place_at + 2

    def chunk(self, meta, offset):
        place = meta[self.place_at] + offset
        place = jnp.where(place < 0, place + self.count, place)
        place = jnp.where(place >= self.count, place - self.count, place)
        return ring_member(place, self.count)

    def request(self, chunk):
        return jnp.where(chunk >= self.half, chunk - self.half, chunk)

    def member(self, chunk):
        return jnp.where(chunk >= self.half, 1, 0)

    def slot(self, meta, request, page):
        return meta[request * self.stride + page]

    def valid(self, meta, request, page):
        return meta[self.valid_at + request * self.stride + page]


def table_kernel(info, pages_dev, page_rows, page_table, prefix_len, suffix_len, meta):
    seq_index = lax.axis_index("seq")
    first_slot = seq_index * pages_dev
    odd = seq_index % 2
    meta[info.place_at] = jnp.where(odd == 0, seq_index // 2, info.count - 1 - seq_index // 2)
    meta[info.place_at + 1] = seq_index

    def one_request(request, carry):
        prefix = prefix_len[request]
        base = request * info.stride

        def one_page(page, state):
            found, live = state
            local = page_table[request, page] - first_slot
            mine = (local >= 0) & (local < pages_dev)
            valid = jnp.minimum(jnp.maximum(prefix - page * page_rows, 0), page_rows)
            meta[base + found] = local
            meta[info.valid_at + base + found] = valid
            return (
                found + jnp.where(mine, 1, 0),
                live + jnp.where(mine & (valid > 0), 1, 0),
            )

        _, live = lax.fori_loop(0, page_table.shape[1], one_page, (0, 0))
        meta[info.live_at + request] = live
        meta[info.suffix_at + request] = suffix_len[request]
        return carry

    lax.fori_loop(0, info.half, one_request, 0)


def tables(info, pages_dev, page_rows, page_table, prefix_len, suffix_len):
    smem = pl.BlockSpec(memory_space=pltpu.SMEM)
    return pl.pallas_call(
        functools.partial(table_kernel, info, pages_dev, page_rows),
        out_shape=jax.ShapeDtypeStruct((info.length,), jnp.int32),
        in_specs=[smem] * 3,
        out_specs=smem,
        cost_estimate=HINT,
        name="tables",
    )(page_table, prefix_len, suffix_len)


def attend_kernel(info, offset, row_base, tok_rows, with_suffix, blocks, span, meta, q_ref, *refs):
    holding = info.holding
    page_refs = refs[:holding]
    refs = refs[holding:]
    if with_suffix:
        suffix_ref = refs[0]
        refs = refs[1:]
    out_refs = refs[:blocks]
    acc_ref, max_ref, sum_ref = refs[blocks:]
    step = pl.program_id(0)
    rows = q_ref.shape[0] // blocks
    width = HEAD_WIDTH
    tall = GROUP * rows
    chunk = info.chunk(meta, offset)
    request = info.request(chunk)
    member = info.member(chunk)
    suffix = meta[info.suffix_at + request]
    first = member * tok_rows + row_base
    live_pages = meta[info.live_at + request]
    live_blocks = jnp.int32(0)
    for block in range(blocks):
        live_blocks = live_blocks + jnp.where(suffix > first + block * rows, 1, 0)

    def scores_of(query, keys):
        return lax.dot_general(
            query, keys, (((1,), (1,)), ((), ())), preferred_element_type=F32
        )

    def score_unit(group, block, pages, suffix_keys):
        part = slice(block * rows, (block + 1) * rows)
        lanes = slice(group * width, (group + 1) * width)
        query = jnp.concatenate(
            [
                q_ref[part, (group * GROUP + i) * width : (group * GROUP + i + 1) * width]
                for i in range(GROUP)
            ],
            axis=0,
        )
        scored = []
        if suffix_keys:
            scores = scores_of(query, suffix_ref[0, :, lanes])
            if offset == 0:
                shape = (rows, scores.shape[1])
                row = block * rows + lax.broadcasted_iota(jnp.int32, shape, 0)
                hidden = lax.broadcasted_iota(jnp.int32, shape, 1) > row
                scores = jnp.concatenate(
                    [
                        jnp.where(hidden, HIDDEN, scores[i * rows : (i + 1) * rows])
                        for i in range(GROUP)
                    ],
                    axis=0,
                )
            scored.append(scores)
        for j in range(pages):
            scores = scores_of(query, page_refs[j][0, 0, :, lanes])
            if j >= pages - 2:
                column = lax.broadcasted_iota(jnp.int32, scores.shape, 1)
                scores = jnp.where(column < info.valid(meta, request, j), scores, HIDDEN)
            scored.append(scores)
        return scored

    def weigh_unit(group, block, pages, suffix_keys, scored):
        lanes = slice(group * width, (group + 1) * width)
        values = [suffix_ref[1, :, lanes]] if suffix_keys else []
        values += [page_refs[j][0, 1, :, lanes] for j in range(pages)]
        top = scored[0]
        for scores in scored[1:]:
            top = jnp.maximum(top, scores)
        row_max = jnp.max(top, axis=1, keepdims=True).astype(BF16).astype(F32)
        weights = [jnp.exp2((scores - row_max) * RATE).astype(BF16) for scores in scored]
        summed = [
            jnp.concatenate([value, jnp.ones(value.shape, BF16)], axis=1) for value in values
        ]
        product = jnp.dot(
            jnp.concatenate(weights, axis=1),
            jnp.concatenate(summed, axis=0),
            preferred_element_type=F32,
        )
        at = group * blocks + block
        max_ref[at] = jnp.broadcast_to(row_max, (tall, STAT))
        sum_ref[at] = product[:, width:]
        acc_ref[at] = product[:, :width]

    def run(some, pages, suffix_keys):
        units = [(group, block) for group in range(span) for block in range(some)]
        coming = score_unit(*units[0], pages, suffix_keys)
        for number, unit in enumerate(units):
            scored = coming
            if number + 1 < len(units):
                coming = score_unit(*units[number + 1], pages, suffix_keys)
            weigh_unit(*unit, pages, suffix_keys, scored)

    if with_suffix:
        own = meta[info.place_at + 1]
        sees = (request == info.request(own)) & (member >= info.member(own))
        nothing = (live_pages == 0) & jnp.logical_not(sees)
    else:
        nothing = live_pages == 0
    for block in range(blocks):

        @pl.when((live_blocks <= block) | nothing)
        def _(block=block):
            for group in range(span):
                at = group * blocks + block
                acc_ref[at] = jnp.zeros((tall, width), F32)
                max_ref[at] = jnp.full((tall, STAT), HIDDEN, F32)
                sum_ref[at] = jnp.zeros((tall, STAT), F32)

    for pages in [0] + list(range(holding, 0, -2)):
        for some in range(1, blocks + 1):
            here = (live_blocks == some) & (live_pages <= pages) & (live_pages >= pages - 1)
            if pages == 0:
                here = (live_blocks == some) & (live_pages == 0)
            elif pages == 1 or pages == 2:
                here = here & (live_pages > 0)
            if with_suffix:
                pl.when(here & sees)(functools.partial(run, some, pages, True))
                here = here & jnp.logical_not(sees)
            if pages > 0 and offset != 0:
                pl.when(here)(functools.partial(run, some, pages, False))

    stat_at = out_refs[0].shape[1] - STAT
    lane = lax.broadcasted_iota(jnp.int32, (rows, STAT), 1)
    for block, out_ref in enumerate(out_refs):

        @pl.when(step == 0)
        def _(out_ref=out_ref):
            out_ref[:, stat_at:] = jnp.zeros((rows, STAT), BF16)

        stats = out_ref[:, stat_at:].astype(F32)
        for group in range(span):
            at = group * blocks + block
            for i in range(GROUP):
                part = slice(i * rows, (i + 1) * rows)
                head = (step * span + group) * GROUP + i
                column = pl.multiple_of(head * width, width)
                out_ref[:, pl.ds(column, width)] = acc_ref[at, part, :].astype(BF16)
                total = sum_ref[at, part, :]
                high = total.astype(BF16).astype(F32)
                stats = jnp.where(lane == head, max_ref[at, part, :], stats)
                stats = jnp.where(lane == SUM_HIGH + head, high, stats)
                stats = jnp.where(lane == SUM_LOW + head, total - high, stats)
        out_ref[:, stat_at:] = stats.astype(BF16)


def attend(info, meta, query, offset, row_base, tok_rows, pages, suffix, hint):
    rows = tok_rows // 2
    blocks = query.shape[0] // rows
    columns = query.shape[1]
    holding = info.holding
    kv_local = pages.shape[3] // HEAD_WIDTH
    span = 2 if kv_local % 2 == 0 else 1
    page_rows = pages.shape[2]
    with_suffix = same_request_at(offset, info.count)

    def page_map(page, step, meta):
        request = info.request(info.chunk(meta, offset))
        return (info.slot(meta, request, page), 0, 0, step)

    in_specs = [pl.BlockSpec((query.shape[0], span * GROUP * HEAD_WIDTH), lambda g, meta: (0, g))]
    in_specs += [
        pl.BlockSpec((1, 2, page_rows, span * HEAD_WIDTH), functools.partial(page_map, j))
        for j in range(holding)
    ]
    operands = [query] + [pages] * holding
    if with_suffix:
        in_specs.append(
            pl.BlockSpec((2, tok_rows, span * HEAD_WIDTH), lambda g, meta: (0, 0, g))
        )
        operands.append(suffix)
    out = jax.ShapeDtypeStruct((rows, columns + STAT), BF16)
    scratch = pltpu.VMEM((span * blocks, GROUP * rows, STAT), F32)
    return pl.pallas_call(
        functools.partial(
            attend_kernel, info, offset, row_base, tok_rows, with_suffix, blocks, span
        ),
        grid_spec=pltpu.PrefetchScalarGridSpec(
            num_scalar_prefetch=1,
            grid=(kv_local // span,),
            in_specs=in_specs,
            out_specs=[pl.BlockSpec((rows, columns + STAT), lambda g, meta: (0, 0))] * blocks,
            scratch_shapes=[scratch] * 3,
        ),
        out_shape=[out] * blocks,
        compiler_params=pltpu.CompilerParams(vmem_limit_bytes=ATTEND_VMEM),
        cost_estimate=hint,
        name="attend",
    )(meta, *operands)


def combine(packed, divided=False):
    stat_at = packed[0].shape[1] - STAT
    stats = [one[:, stat_at:].astype(F32) for one in packed]
    top = stats[0]
    for one in stats[1:]:
        top = jnp.maximum(top, one)
    factors = [jnp.exp2((jnp.minimum(one - top, 0.0)) * RATE) for one in stats]
    total = None
    for one, factor in zip(stats, factors):
        own = pltpu.roll(one, STAT - SUM_HIGH, 1) + pltpu.roll(one, STAT - SUM_LOW, 1)
        total = own * factor if total is None else total + own * factor
    if divided:
        factors = [factor / total for factor in factors]
    heads = []
    for head in range(stat_at // HEAD_WIDTH):
        mixed = None
        for one, factor in zip(packed, factors):
            value = one[:, head * HEAD_WIDTH : (head + 1) * HEAD_WIDTH].astype(F32)
            value = value * factor[:, head : head + 1]
            mixed = value if mixed is None else mixed + value
        heads.append(mixed)
    return (heads, top, total)


def merge_kernel(a_ref, b_ref, out_ref):
    heads, top, total = combine([a_ref[...], b_ref[...]])
    for head, mixed in enumerate(heads):
        out_ref[:, head * HEAD_WIDTH : (head + 1) * HEAD_WIDTH] = mixed.astype(BF16)
    high = total.astype(BF16).astype(F32)
    lane = lax.broadcasted_iota(jnp.int32, top.shape, 1)
    stats = jnp.where(lane < SUM_HIGH, top, 0.0)
    stats = jnp.where((lane >= SUM_HIGH) & (lane < SUM_LOW), pltpu.roll(high, SUM_HIGH, 1), stats)
    low = pltpu.roll(total - high, SUM_LOW, 1)
    stats = jnp.where((lane >= SUM_LOW) & (lane < SUM_LOW + SUM_HIGH), low, stats)
    out_ref[:, len(heads) * HEAD_WIDTH :] = stats.astype(BF16)


def merge(a, b):
    return pl.pallas_call(
        merge_kernel,
        out_shape=jax.ShapeDtypeStruct(a.shape, BF16),
        in_specs=[pl.BlockSpec(memory_space=pltpu.VMEM)] * 2,
        out_specs=pl.BlockSpec(memory_space=pltpu.VMEM),
        compiler_params=pltpu.CompilerParams(vmem_limit_bytes=16 * MIB),
        cost_estimate=HINT,
        name="merge",
    )(a, b)


def window_of(columns, head_count):
    spans = [
        -(-(t + 1) * columns // STAT) - t * columns // STAT for t in range(head_count)
    ]
    return max(spans) * STAT


def window_start(target, columns, head_count):
    start = target * columns // STAT * STAT
    return jnp.minimum(start, columns * head_count - window_of(columns, head_count))


def project(head_count, wanted, attention, weight, out_refs, window, sems):
    columns = weight.shape[1] // head_count
    half = head_count // 2
    head_index = lax.axis_index("head")
    pair = head_index // 2
    copies = []
    for number, (other, turn) in enumerate(wanted):
        core = head_index % 2
        core = 1 - core if other else core
        target = 2 * ((pair + turn) % half) + core
        start = pl.multiple_of(window_start(target, columns, head_count), STAT)
        copies.append(
            pltpu.make_async_copy(
                weight.at[:, pl.ds(start, window.shape[2])], window.at[number], sems.at[number]
            )
        )
        copies[-1].start()
    rows = attention()
    for number, copy in enumerate(copies):
        copy.wait()
        product = jnp.dot(rows, window[number], preferred_element_type=F32)
        out_refs[number][...] = product.astype(BF16)


def finish_kernel(info, tok_rows, first_row, shares, head_count, wanted, meta, *refs):
    weight, rows_ref = refs[shares : shares + 2]
    rest = refs[shares + 2 :]

    def attention():
        chunk = info.chunk(meta, 0)
        suffix = meta[info.suffix_at + info.request(chunk)]
        heads, _, total = combine([ref[...] for ref in refs[:shares]], True)
        first = info.member(chunk) * tok_rows + first_row
        place = first + lax.broadcasted_iota(jnp.int32, heads[0].shape, 0)
        for head, mixed in enumerate(heads):
            value = jnp.where(place < suffix, mixed, 0.0)
            rows_ref[:, head * HEAD_WIDTH : (head + 1) * HEAD_WIDTH] = value.astype(BF16)
        return rows_ref[...]

    project(head_count, wanted, attention, weight, rest[: len(wanted)], *rest[len(wanted) :])


def share_kernel(head_count, wanted, parts, *refs):
    weight = refs[parts]
    outs = refs[parts + 1 : parts + 1 + len(wanted)]

    def attention():
        return jnp.concatenate([ref[...] for ref in refs[:parts]], axis=0)

    project(head_count, wanted, attention, weight, outs, *refs[parts + 1 + len(wanted) :])


def project_call(kernel, name, wanted, rows, weight, head_count, operands, with_rows, with_meta):
    depth = weight.shape[0]
    wide = window_of(weight.shape[1] // head_count, head_count)
    vmem = pl.BlockSpec(memory_space=pltpu.VMEM)
    smem = [pl.BlockSpec(memory_space=pltpu.SMEM)] * with_meta
    out = [jax.ShapeDtypeStruct((rows, depth), BF16)] * with_rows
    out += [jax.ShapeDtypeStruct((rows, wide), BF16)] * len(wanted)
    return pl.pallas_call(
        kernel,
        out_shape=out,
        in_specs=smem
        + [vmem] * (len(operands) - with_meta)
        + [pl.BlockSpec(memory_space=pl.ANY)],
        out_specs=[vmem] * len(out),
        scratch_shapes=[
            pltpu.VMEM((len(wanted), depth, wide), BF16),
            pltpu.SemaphoreType.DMA((len(wanted),)),
        ],
        compiler_params=pltpu.CompilerParams(vmem_limit_bytes=LARGE_VMEM),
        cost_estimate=HINT,
        name=name,
    )(*operands, weight)


def share(name, wanted, attention, weight, head_count):
    return project_call(
        functools.partial(share_kernel, head_count, wanted, len(attention)),
        name,
        wanted,
        sum(part.shape[0] for part in attention),
        weight,
        head_count,
        list(attention),
        0,
        0,
    )


def finish(info, meta, packed, first_row, weight, tok_rows, head_count):
    half = head_count // 2
    other = [(True, turn) for turn in range(1, half)]
    own = [(False, turn) for turn in range(1, half)]
    attention, *given = project_call(
        functools.partial(
            finish_kernel, info, tok_rows, first_row, len(packed), head_count, other
        ),
        "finish",
        other,
        packed[0].shape[0],
        weight,
        head_count,
        [meta, *packed],
        1,
        1,
    )
    taken = [swap_cores(one, head_count, 2) for one in given]
    return (attention, share("far", own, [attention], weight, head_count), taken)


def swap_cores(value, head_count, pieces):
    rows = value.shape[0] // pieces
    pairs = [(i, i ^ 1) for i in range(head_count)]
    return [
        lax.ppermute(value[i * rows : (i + 1) * rows], "head", pairs) for i in range(pieces)
    ]


def send_far(kept, taken, head_count):
    sent = []
    received = []
    for number, (mine, theirs) in enumerate(zip(kept, taken)):
        step = number + 1
        pairs = [(i, (i + 2 * step) % head_count) for i in range(head_count)]
        theirs = jnp.concatenate(theirs, axis=0)
        sent.append((mine.astype(F32) + theirs.astype(F32)).astype(BF16))
        received.append(lax.ppermute(sent[-1], "head", pairs))
    return (sent, received)


def last_kernel(columns, head_count, pieces, own_ref, *refs):
    near_refs = refs[:pieces]
    refs = refs[pieces:]
    out_ref, turned = refs[-2:]
    halves = [refs[: (len(refs) - 2) // 2], refs[(len(refs) - 2) // 2 : -2]]
    head_index = lax.axis_index("head")
    shift = head_index * columns - window_start(head_index, columns, head_count)
    rows = own_ref.shape[0] // 2
    for number, received in enumerate(halves):
        part = slice(number * rows, (number + 1) * rows)
        near = near_refs[number * pieces // 2 : (number + 1) * pieces // 2]
        total = own_ref[part].astype(F32)
        total = total + jnp.concatenate([ref[...] for ref in near], axis=0).astype(F32)
        for ref in received:
            total = total + ref[...].astype(F32)
        turned[:, part] = total.T
    out_ref[...] = turned[pl.ds(pl.multiple_of(shift, 8), columns), :].astype(BF16)


def last(own, near, received, columns, head_count):
    rows, wide = own.shape
    vmem = pl.BlockSpec(memory_space=pltpu.VMEM)
    return pl.pallas_call(
        functools.partial(last_kernel, columns, head_count, len(near)),
        out_shape=jax.ShapeDtypeStruct((columns, rows), BF16),
        in_specs=[vmem] * (1 + len(near) + len(received)),
        out_specs=vmem,
        scratch_shapes=[pltpu.VMEM((wide, rows), F32)],
        compiler_params=pltpu.CompilerParams(vmem_limit_bytes=16 * MIB),
        cost_estimate=HINT,
        name="last",
    )(own, *near, *received)


def after(value, *others):
    return lax.optimization_barrier((value, others))[0]


def shards(queries, suffix_key_value, pooled_pages, out_weight, page_table, prefix_len, suffix_len):
    tok_rows = queries.shape[0]
    pages_dev, page_rows = pooled_pages.shape[:2]
    count = lax.axis_size("seq")
    head_count = lax.axis_size("head")
    reach = count // 2
    info = Meta(count, 2 * pages_dev // count)
    order = ring_order(count)
    ahead = [(order[i], order[(i + 1) % count]) for i in range(count)]
    back = [(b, a) for a, b in ahead]
    middle = tok_rows // 2

    meta = tables(info, pages_dev, page_rows, page_table, prefix_len, suffix_len)
    pages = jnp.transpose(pooled_pages, (0, 2, 1, 3))
    suffix = jnp.transpose(suffix_key_value, (1, 0, 2))

    def partial_of(query, offset, row_base=0, hint=HINT):
        return attend(info, meta, query, offset, row_base, tok_rows, pages, suffix, hint)

    left = [queries]
    right = [queries]
    part_left = {}
    part_right = {}
    late = reach - 2

    def attend_both(step):
        part_left[step] = partial_of(left[step], -step)
        part_right[step] = partial_of(right[step], step)
        return (part_left[step], part_right[step])

    for step in range(1, reach + 1):
        end = step == reach
        next_left = lax.ppermute(left[-1][:middle] if end else left[-1], "seq", ahead)
        next_right = lax.ppermute(right[-1][middle:] if end else right[-1], "seq", back)
        if step == 1:
            done = (meta, pages)
        elif step == reach - 1:
            home = partial_of(queries, 0)
            part_left[late] = partial_of(left[late], -late)
            done = (home, part_left[late])
        else:
            done = attend_both(step - 1)
        next_left, next_right = after((next_left, next_right), done)
        left.append(next_left)
        right.append(next_right)

    low_right = lax.ppermute(part_right[reach - 1][0], "seq", ahead)
    high_left = lax.ppermute(part_left[reach - 1][1], "seq", back)
    far_left = partial_of(left[reach], -reach)[0]
    far_right = partial_of(right[reach], reach, middle)[0]
    low_left = lax.ppermute(far_left, "seq", back)
    high_right = lax.ppermute(far_right, "seq", ahead)
    right[late] = after(right[late], far_left, far_right)
    part_right[late] = partial_of(right[late], late, 0, LONG)
    latest = part_right[late]

    def onward(travelled, mine, pairs):
        merged = merge(after(travelled, latest), mine)
        return (lax.ppermute(merged, "seq", pairs), merged)

    for step in range(reach - 1, 1, -1):
        low_left, latest = onward(low_left, part_left[step][0], back)
        if step == 2:
            low_right, latest = onward(low_right, part_right[step - 1][0], ahead)
            high_left, high_right = after((high_left, high_right), latest)
            high_right, latest = onward(high_right, part_right[step][1], ahead)
        else:
            high_right, latest = onward(high_right, part_right[step][1], ahead)
            high_left, latest = onward(high_left, part_left[step - 1][1], back)
            low_right, latest = onward(low_right, part_right[step - 1][0], ahead)
    low_left, latest = onward(low_left, part_left[1][0], back)
    high_left, latest = onward(high_left, part_left[1][1], back)
    high_right, latest = onward(high_right, part_right[1][1], ahead)

    low = [merge(after(low_right, latest), home[0]), low_left]
    rest = (out_weight, tok_rows, head_count)
    rows_low, kept, taken = finish(info, meta, low, 0, *rest)
    taken, high_left, high_right = after((taken, high_left, high_right))
    sent, received_low = send_far(kept, taken, head_count)
    high = [after(home[1], sent), high_left, high_right]
    rows_high, kept, taken = finish(info, meta, high, middle, *rest)
    taken, received_low = after((taken, received_low))
    sent, received_high = send_far(kept, taken, head_count)
    near, own = share(
        "near",
        [(True, 0), (False, 0)],
        after([rows_low, rows_high], sent),
        out_weight,
        head_count,
    )
    near = after(swap_cores(near, head_count, 4), received_high)
    columns = out_weight.shape[1] // head_count
    return last(own, near, received_low + received_high, columns, head_count).T


def solution(mesh):
    placed = (
        P("seq", "head"),
        P("seq", None, "head"),
        P("seq", None, None, "head"),
        P("head", None),
        P(),
        P(),
        P(),
    )
    return jax.shard_map(
        shards, mesh=mesh, in_specs=placed, out_specs=P("seq", "head"), check_vma=False
    )
```

```python
import functools
import math

import jax
import jax.numpy as jnp
from jax import lax
from jax.experimental import pallas as pl
from jax.experimental.pallas import tpu as pltpu
from jax.sharding import PartitionSpec as P

D = 5376
QUERY_HEADS = 32
KEY_VALUE_HEADS = 16
HEAD_WIDTH = 128
GROUP = QUERY_HEADS // KEY_VALUE_HEADS
RATE = float(D // QUERY_HEADS) ** (-0.5) * math.log2(math.e)
HIDDEN = -(2.0**99)
STAT = 128
SUM_HIGH = 32
SUM_LOW = 64
F32 = jnp.float32
BF16 = jnp.bfloat16
MIB = 1 << 20
LARGE_VMEM = 52 * MIB
ATTEND_VMEM = 24 * MIB
HINT = pl.CostEstimate(flops=1024, bytes_accessed=1024, transcendentals=0)
LONG = pl.CostEstimate(flops=1 << 33, bytes_accessed=1024, transcendentals=0)


def ring_member(place, count):
    return jnp.where(place < count // 2, 2 * place, 2 * (count - 1 - place) + 1)


def ring_order(count):
    return list(range(0, count, 2)) + list(range(count - 1, 0, -2))


def same_request_at(offset, count):
    order = ring_order(count)
    half = count // 2
    return any(order[(i + offset) % count] % half == order[i] % half for i in range(count))


class Meta:
    def __init__(self, count, holding):
        self.count = count
        self.half = count // 2
        self.holding = holding
        self.stride = holding + 1
        self.valid_at = self.half * self.stride
        self.live_at = 2 * self.half * self.stride
        self.suffix_at = self.live_at + self.half
        self.place_at = self.suffix_at + self.half
        self.length = self.place_at + 2

    def chunk(self, meta, offset):
        place = meta[self.place_at] + offset
        place = jnp.where(place < 0, place + self.count, place)
        place = jnp.where(place >= self.count, place - self.count, place)
        return ring_member(place, self.count)

    def request(self, chunk):
        return jnp.where(chunk >= self.half, chunk - self.half, chunk)

    def member(self, chunk):
        return jnp.where(chunk >= self.half, 1, 0)

    def slot(self, meta, request, page):
        return meta[request * self.stride + page]

    def valid(self, meta, request, page):
        return meta[self.valid_at + request * self.stride + page]


def table_kernel(info, pages_dev, page_rows, page_table, prefix_len, suffix_len, meta):
    seq_index = lax.axis_index("seq")
    first_slot = seq_index * pages_dev
    odd = seq_index % 2
    meta[info.place_at] = jnp.where(odd == 0, seq_index // 2, info.count - 1 - seq_index // 2)
    meta[info.place_at + 1] = seq_index

    def one_request(request, carry):
        prefix = prefix_len[request]
        base = request * info.stride

        def one_page(page, state):
            found, live = state
            local = page_table[request, page] - first_slot
            mine = (local >= 0) & (local < pages_dev)
            valid = jnp.minimum(jnp.maximum(prefix - page * page_rows, 0), page_rows)
            meta[base + found] = local
            meta[info.valid_at + base + found] = valid
            return (
                found + jnp.where(mine, 1, 0),
                live + jnp.where(mine & (valid > 0), 1, 0),
            )

        _, live = lax.fori_loop(0, page_table.shape[1], one_page, (0, 0))
        meta[info.live_at + request] = live
        meta[info.suffix_at + request] = suffix_len[request]
        return carry

    lax.fori_loop(0, info.half, one_request, 0)


def tables(info, pages_dev, page_rows, page_table, prefix_len, suffix_len):
    smem = pl.BlockSpec(memory_space=pltpu.SMEM)
    return pl.pallas_call(
        functools.partial(table_kernel, info, pages_dev, page_rows),
        out_shape=jax.ShapeDtypeStruct((info.length,), jnp.int32),
        in_specs=[smem] * 3,
        out_specs=smem,
        cost_estimate=HINT,
        name="tables",
    )(page_table, prefix_len, suffix_len)


def attend_kernel(info, offset, row_base, tok_rows, with_suffix, blocks, span, meta, q_ref, *refs):
    holding = info.holding
    page_refs = refs[:holding]
    refs = refs[holding:]
    if with_suffix:
        suffix_ref = refs[0]
        refs = refs[1:]
    out_refs = refs[:blocks]
    acc_ref, max_ref, sum_ref = refs[blocks:]
    step = pl.program_id(0)
    rows = q_ref.shape[0] // blocks
    width = HEAD_WIDTH
    tall = GROUP * rows
    chunk = info.chunk(meta, offset)
    request = info.request(chunk)
    member = info.member(chunk)
    suffix = meta[info.suffix_at + request]
    first = member * tok_rows + row_base
    live_pages = meta[info.live_at + request]
    live_blocks = jnp.int32(0)
    for block in range(blocks):
        live_blocks = live_blocks + jnp.where(suffix > first + block * rows, 1, 0)

    def scores_of(query, keys):
        return lax.dot_general(
            query, keys, (((1,), (1,)), ((), ())), preferred_element_type=F32
        )

    def score_unit(group, block, pages, suffix_keys):
        part = slice(block * rows, (block + 1) * rows)
        lanes = slice(group * width, (group + 1) * width)
        query = jnp.concatenate(
            [
                q_ref[part, (group * GROUP + i) * width : (group * GROUP + i + 1) * width]
                for i in range(GROUP)
            ],
            axis=0,
        )
        scored = []
        if suffix_keys:
            scores = scores_of(query, suffix_ref[0, :, lanes])
            if offset == 0:
                shape = (rows, scores.shape[1])
                row = block * rows + lax.broadcasted_iota(jnp.int32, shape, 0)
                hidden = lax.broadcasted_iota(jnp.int32, shape, 1) > row
                scores = jnp.concatenate(
                    [
                        jnp.where(hidden, HIDDEN, scores[i * rows : (i + 1) * rows])
                        for i in range(GROUP)
                    ],
                    axis=0,
                )
            scored.append(scores)
        for j in range(pages):
            scores = scores_of(query, page_refs[j][0, 0, :, lanes])
            if j >= pages - 2:
                column = lax.broadcasted_iota(jnp.int32, scores.shape, 1)
                scores = jnp.where(column < info.valid(meta, request, j), scores, HIDDEN)
            scored.append(scores)
        return scored

    def weigh_unit(group, block, pages, suffix_keys, scored):
        lanes = slice(group * width, (group + 1) * width)
        values = [suffix_ref[1, :, lanes]] if suffix_keys else []
        values += [page_refs[j][0, 1, :, lanes] for j in range(pages)]
        top = scored[0]
        for scores in scored[1:]:
            top = jnp.maximum(top, scores)
        row_max = jnp.max(top, axis=1, keepdims=True).astype(BF16).astype(F32)
        weights = [jnp.exp2((scores - row_max) * RATE).astype(BF16) for scores in scored]
        summed = [
            jnp.concatenate([value, jnp.ones(value.shape, BF16)], axis=1) for value in values
        ]
        product = jnp.dot(
            jnp.concatenate(weights, axis=1),
            jnp.concatenate(summed, axis=0),
            preferred_element_type=F32,
        )
        at = group * blocks + block
        max_ref[at] = jnp.broadcast_to(row_max, (tall, STAT))
        sum_ref[at] = product[:, width:]
        acc_ref[at] = product[:, :width]

    def run(some, pages, suffix_keys):
        units = [(group, block) for group in range(span) for block in range(some)]
        coming = score_unit(*units[0], pages, suffix_keys)
        for number, unit in enumerate(units):
            scored = coming
            if number + 1 < len(units):
                coming = score_unit(*units[number + 1], pages, suffix_keys)
            weigh_unit(*unit, pages, suffix_keys, scored)

    if with_suffix:
        own = meta[info.place_at + 1]
        sees = (request == info.request(own)) & (member >= info.member(own))
        nothing = (live_pages == 0) & jnp.logical_not(sees)
    else:
        nothing = live_pages == 0
    for block in range(blocks):

        @pl.when((live_blocks <= (0 if with_suffix else block)) | nothing)
        def _(block=block):
            for group in range(span):
                at = group * blocks + block
                acc_ref[at] = jnp.zeros((tall, width), F32)
                max_ref[at] = jnp.full((tall, STAT), HIDDEN, F32)
                sum_ref[at] = jnp.zeros((tall, STAT), F32)

    for pages in [0] + list(range(holding, 0, -2)):
        if pages == 0:
            counted = live_pages == 0
        else:
            counted = (live_pages <= pages) & (live_pages >= max(pages - 1, 1))
        for some in [blocks] if with_suffix else range(1, blocks + 1):
            here = counted & (live_blocks == some)
            if with_suffix:
                here = counted & (live_blocks > 0)
                pl.when(here & sees)(functools.partial(run, some, pages, True))
                here = here & jnp.logical_not(sees)
            if pages > 0 and offset != 0:
                pl.when(here)(functools.partial(run, some, pages, False))

    stat_at = out_refs[0].shape[1] - STAT
    lane = lax.broadcasted_iota(jnp.int32, (rows, STAT), 1)
    for block, out_ref in enumerate(out_refs):

        @pl.when(step == 0)
        def _(out_ref=out_ref):
            out_ref[:, stat_at:] = jnp.zeros((rows, STAT), BF16)

        stats = out_ref[:, stat_at:].astype(F32)
        for group in range(span):
            at = group * blocks + block
            for i in range(GROUP):
                part = slice(i * rows, (i + 1) * rows)
                head = (step * span + group) * GROUP + i
                column = pl.multiple_of(head * width, width)
                out_ref[:, pl.ds(column, width)] = acc_ref[at, part, :].astype(BF16)
                total = sum_ref[at, part, :]
                high = total.astype(BF16).astype(F32)
                stats = jnp.where(lane == head, max_ref[at, part, :], stats)
                stats = jnp.where(lane == SUM_HIGH + head, high, stats)
                stats = jnp.where(lane == SUM_LOW + head, total - high, stats)
        out_ref[:, stat_at:] = stats.astype(BF16)


def attend(info, meta, query, offset, row_base, tok_rows, pages, suffix, hint):
    rows = tok_rows // 2
    blocks = query.shape[0] // rows
    columns = query.shape[1]
    holding = info.holding
    kv_local = pages.shape[3] // HEAD_WIDTH
    span = 2 if kv_local % 2 == 0 else 1
    page_rows = pages.shape[2]
    with_suffix = same_request_at(offset, info.count)

    def page_map(page, step, meta):
        request = info.request(info.chunk(meta, offset))
        return (info.slot(meta, request, page), 0, 0, step)

    in_specs = [pl.BlockSpec((query.shape[0], span * GROUP * HEAD_WIDTH), lambda g, meta: (0, g))]
    in_specs += [
        pl.BlockSpec((1, 2, page_rows, span * HEAD_WIDTH), functools.partial(page_map, j))
        for j in range(holding)
    ]
    operands = [query] + [pages] * holding
    if with_suffix:
        in_specs.append(
            pl.BlockSpec((2, tok_rows, span * HEAD_WIDTH), lambda g, meta: (0, 0, g))
        )
        operands.append(suffix)
    out = jax.ShapeDtypeStruct((rows, columns + STAT), BF16)
    scratch = pltpu.VMEM((span * blocks, GROUP * rows, STAT), F32)
    return pl.pallas_call(
        functools.partial(
            attend_kernel, info, offset, row_base, tok_rows, with_suffix, blocks, span
        ),
        grid_spec=pltpu.PrefetchScalarGridSpec(
            num_scalar_prefetch=1,
            grid=(kv_local // span,),
            in_specs=in_specs,
            out_specs=[pl.BlockSpec((rows, columns + STAT), lambda g, meta: (0, 0))] * blocks,
            scratch_shapes=[scratch] * 3,
        ),
        out_shape=[out] * blocks,
        compiler_params=pltpu.CompilerParams(vmem_limit_bytes=ATTEND_VMEM),
        cost_estimate=hint,
        name="attend",
    )(meta, *operands)


def combine(packed, divided=False):
    stat_at = packed[0].shape[1] - STAT
    stats = [one[:, stat_at:].astype(F32) for one in packed]
    top = stats[0]
    for one in stats[1:]:
        top = jnp.maximum(top, one)
    factors = [jnp.exp2((jnp.minimum(one - top, 0.0)) * RATE) for one in stats]
    total = None
    for one, factor in zip(stats, factors):
        own = pltpu.roll(one, STAT - SUM_HIGH, 1) + pltpu.roll(one, STAT - SUM_LOW, 1)
        total = own * factor if total is None else total + own * factor
    if divided:
        factors = [factor / total for factor in factors]
    heads = []
    for head in range(stat_at // HEAD_WIDTH):
        mixed = None
        for one, factor in zip(packed, factors):
            value = one[:, head * HEAD_WIDTH : (head + 1) * HEAD_WIDTH].astype(F32)
            value = value * factor[:, head : head + 1]
            mixed = value if mixed is None else mixed + value
        heads.append(mixed)
    return (heads, top, total)


def merge_kernel(a_ref, b_ref, out_ref):
    heads, top, total = combine([a_ref[...], b_ref[...]])
    for head, mixed in enumerate(heads):
        out_ref[:, head * HEAD_WIDTH : (head + 1) * HEAD_WIDTH] = mixed.astype(BF16)
    high = total.astype(BF16).astype(F32)
    lane = lax.broadcasted_iota(jnp.int32, top.shape, 1)
    stats = jnp.where(lane < SUM_HIGH, top, 0.0)
    stats = jnp.where((lane >= SUM_HIGH) & (lane < SUM_LOW), pltpu.roll(high, SUM_HIGH, 1), stats)
    low = pltpu.roll(total - high, SUM_LOW, 1)
    stats = jnp.where((lane >= SUM_LOW) & (lane < SUM_LOW + SUM_HIGH), low, stats)
    out_ref[:, len(heads) * HEAD_WIDTH :] = stats.astype(BF16)


def merge(a, b):
    return pl.pallas_call(
        merge_kernel,
        out_shape=jax.ShapeDtypeStruct(a.shape, BF16),
        in_specs=[pl.BlockSpec(memory_space=pltpu.VMEM)] * 2,
        out_specs=pl.BlockSpec(memory_space=pltpu.VMEM),
        compiler_params=pltpu.CompilerParams(vmem_limit_bytes=16 * MIB),
        cost_estimate=HINT,
        name="merge",
    )(a, b)


def window_of(columns, head_count):
    spans = [
        -(-(t + 1) * columns // STAT) - t * columns // STAT for t in range(head_count)
    ]
    return max(spans) * STAT


def window_start(target, columns, head_count):
    start = target * columns // STAT * STAT
    return jnp.minimum(start, columns * head_count - window_of(columns, head_count))


def project(head_count, wanted, attention, weight, out_refs, window, sems):
    columns = weight.shape[1] // head_count
    half = head_count // 2
    head_index = lax.axis_index("head")
    pair = head_index // 2
    copies = []
    for number, (other, turn) in enumerate(wanted):
        core = head_index % 2
        core = 1 - core if other else core
        target = 2 * ((pair + turn) % half) + core
        start = pl.multiple_of(window_start(target, columns, head_count), STAT)
        copies.append(
            pltpu.make_async_copy(
                weight.at[:, pl.ds(start, window.shape[2])], window.at[number], sems.at[number]
            )
        )
        copies[-1].start()
    rows = attention()
    for number, copy in enumerate(copies):
        copy.wait()
        product = jnp.dot(rows, window[number], preferred_element_type=F32)
        out_refs[number][...] = product.astype(BF16)


def finish_kernel(info, tok_rows, first_row, shares, head_count, wanted, meta, *refs):
    weight, rows_ref = refs[shares : shares + 2]
    rest = refs[shares + 2 :]

    def attention():
        chunk = info.chunk(meta, 0)
        suffix = meta[info.suffix_at + info.request(chunk)]
        heads, _, total = combine([ref[...] for ref in refs[:shares]], True)
        first = info.member(chunk) * tok_rows + first_row
        place = first + lax.broadcasted_iota(jnp.int32, heads[0].shape, 0)
        for head, mixed in enumerate(heads):
            value = jnp.where(place < suffix, mixed, 0.0)
            rows_ref[:, head * HEAD_WIDTH : (head + 1) * HEAD_WIDTH] = value.astype(BF16)
        return rows_ref[...]

    project(head_count, wanted, attention, weight, rest[: len(wanted)], *rest[len(wanted) :])


def share_kernel(head_count, wanted, parts, *refs):
    weight = refs[parts]
    outs = refs[parts + 1 : parts + 1 + len(wanted)]

    def attention():
        return jnp.concatenate([ref[...] for ref in refs[:parts]], axis=0)

    project(head_count, wanted, attention, weight, outs, *refs[parts + 1 + len(wanted) :])


def project_call(kernel, name, wanted, rows, weight, head_count, operands, with_rows, with_meta):
    depth = weight.shape[0]
    wide = window_of(weight.shape[1] // head_count, head_count)
    vmem = pl.BlockSpec(memory_space=pltpu.VMEM)
    smem = [pl.BlockSpec(memory_space=pltpu.SMEM)] * with_meta
    out = [jax.ShapeDtypeStruct((rows, depth), BF16)] * with_rows
    out += [jax.ShapeDtypeStruct((rows, wide), BF16)] * len(wanted)
    return pl.pallas_call(
        kernel,
        out_shape=out,
        in_specs=smem
        + [vmem] * (len(operands) - with_meta)
        + [pl.BlockSpec(memory_space=pl.ANY)],
        out_specs=[vmem] * len(out),
        scratch_shapes=[
            pltpu.VMEM((len(wanted), depth, wide), BF16),
            pltpu.SemaphoreType.DMA((len(wanted),)),
        ],
        compiler_params=pltpu.CompilerParams(vmem_limit_bytes=LARGE_VMEM),
        cost_estimate=HINT,
        name=name,
    )(*operands, weight)


def share(name, wanted, attention, weight, head_count):
    return project_call(
        functools.partial(share_kernel, head_count, wanted, len(attention)),
        name,
        wanted,
        sum(part.shape[0] for part in attention),
        weight,
        head_count,
        list(attention),
        0,
        0,
    )


def finish(info, meta, packed, first_row, weight, tok_rows, head_count):
    half = head_count // 2
    other = [(True, turn) for turn in range(1, half)]
    own = [(False, turn) for turn in range(1, half)]
    attention, *given = project_call(
        functools.partial(
            finish_kernel, info, tok_rows, first_row, len(packed), head_count, other
        ),
        "finish",
        other,
        packed[0].shape[0],
        weight,
        head_count,
        [meta, *packed],
        1,
        1,
    )
    taken = [swap_cores(one, head_count, 2) for one in given]
    return (attention, share("far", own, [attention], weight, head_count), taken)


def swap_cores(value, head_count, pieces):
    rows = value.shape[0] // pieces
    pairs = [(i, i ^ 1) for i in range(head_count)]
    return [
        lax.ppermute(value[i * rows : (i + 1) * rows], "head", pairs) for i in range(pieces)
    ]


def send_far(kept, taken, head_count):
    sent = []
    received = []
    for number, (mine, theirs) in enumerate(zip(kept, taken)):
        step = number + 1
        pairs = [(i, (i + 2 * step) % head_count) for i in range(head_count)]
        theirs = jnp.concatenate(theirs, axis=0)
        sent.append((mine.astype(F32) + theirs.astype(F32)).astype(BF16))
        received.append(lax.ppermute(sent[-1], "head", pairs))
    return (sent, received)


def last_kernel(columns, head_count, pieces, own_ref, *refs):
    near_refs = refs[:pieces]
    refs = refs[pieces:]
    out_ref, turned = refs[-2:]
    halves = [refs[: (len(refs) - 2) // 2], refs[(len(refs) - 2) // 2 : -2]]
    head_index = lax.axis_index("head")
    shift = head_index * columns - window_start(head_index, columns, head_count)
    rows = own_ref.shape[0] // 2
    for number, received in enumerate(halves):
        part = slice(number * rows, (number + 1) * rows)
        near = near_refs[number * pieces // 2 : (number + 1) * pieces // 2]
        total = own_ref[part].astype(F32)
        total = total + jnp.concatenate([ref[...] for ref in near], axis=0).astype(F32)
        for ref in received:
            total = total + ref[...].astype(F32)
        turned[:, part] = total.T
    out_ref[...] = turned[pl.ds(pl.multiple_of(shift, 8), columns), :].astype(BF16)


def last(own, near, received, columns, head_count):
    rows, wide = own.shape
    vmem = pl.BlockSpec(memory_space=pltpu.VMEM)
    return pl.pallas_call(
        functools.partial(last_kernel, columns, head_count, len(near)),
        out_shape=jax.ShapeDtypeStruct((columns, rows), BF16),
        in_specs=[vmem] * (1 + len(near) + len(received)),
        out_specs=vmem,
        scratch_shapes=[pltpu.VMEM((wide, rows), F32)],
        compiler_params=pltpu.CompilerParams(vmem_limit_bytes=16 * MIB),
        cost_estimate=HINT,
        name="last",
    )(own, *near, *received)


def after(value, *others):
    return lax.optimization_barrier((value, others))[0]


def shards(queries, suffix_key_value, pooled_pages, out_weight, page_table, prefix_len, suffix_len):
    tok_rows = queries.shape[0]
    pages_dev, page_rows = pooled_pages.shape[:2]
    count = lax.axis_size("seq")
    head_count = lax.axis_size("head")
    reach = count // 2
    info = Meta(count, 2 * pages_dev // count)
    order = ring_order(count)
    ahead = [(order[i], order[(i + 1) % count]) for i in range(count)]
    back = [(b, a) for a, b in ahead]
    middle = tok_rows // 2

    meta = tables(info, pages_dev, page_rows, page_table, prefix_len, suffix_len)
    pages = jnp.transpose(pooled_pages, (0, 2, 1, 3))
    suffix = jnp.transpose(suffix_key_value, (1, 0, 2))

    def partial_of(query, offset, row_base=0, hint=HINT):
        return attend(info, meta, query, offset, row_base, tok_rows, pages, suffix, hint)

    left = [queries]
    right = [queries]
    part_left = {}
    part_right = {}
    late = reach - 2

    def attend_both(step):
        part_left[step] = partial_of(left[step], -step)
        part_right[step] = partial_of(right[step], step)
        return (part_left[step], part_right[step])

    for step in range(1, reach + 1):
        end = step == reach
        next_left = lax.ppermute(left[-1][:middle] if end else left[-1], "seq", ahead)
        next_right = lax.ppermute(right[-1][middle:] if end else right[-1], "seq", back)
        if step == 1:
            done = (meta, pages)
        elif step == reach - 1:
            home = partial_of(queries, 0)
            part_left[late] = partial_of(left[late], -late)
            done = (home, part_left[late])
        else:
            done = attend_both(step - 1)
        next_left, next_right = after((next_left, next_right), done)
        left.append(next_left)
        right.append(next_right)

    low_right = lax.ppermute(part_right[reach - 1][0], "seq", ahead)
    high_left = lax.ppermute(part_left[reach - 1][1], "seq", back)
    far_left = partial_of(left[reach], -reach)[0]
    far_right = partial_of(right[reach], reach, middle)[0]
    low_left = lax.ppermute(far_left, "seq", back)
    high_right = lax.ppermute(far_right, "seq", ahead)
    right[late] = after(right[late], far_left, far_right)
    part_right[late] = partial_of(right[late], late, 0, LONG)
    latest = part_right[late]

    def onward(travelled, mine, pairs):
        merged = merge(after(travelled, latest), mine)
        return (lax.ppermute(merged, "seq", pairs), merged)

    for step in range(reach - 1, 1, -1):
        low_left, latest = onward(low_left, part_left[step][0], back)
        if step == 2:
            low_right, latest = onward(low_right, part_right[step - 1][0], ahead)
            high_left, high_right = after((high_left, high_right), latest)
            high_right, latest = onward(high_right, part_right[step][1], ahead)
        else:
            high_right, latest = onward(high_right, part_right[step][1], ahead)
            high_left, latest = onward(high_left, part_left[step - 1][1], back)
            low_right, latest = onward(low_right, part_right[step - 1][0], ahead)
    low_left, latest = onward(low_left, part_left[1][0], back)
    high_left, latest = onward(high_left, part_left[1][1], back)
    early = merge(after(low_right, latest), home[0])
    latest = early
    high_right, latest = onward(high_right, part_right[1][1], ahead)

    low = [early, after(low_left, latest)]
    rest = (out_weight, tok_rows, head_count)
    rows_low, kept, taken = finish(info, meta, low, 0, *rest)
    taken, high_left, high_right = after((taken, high_left, high_right))
    sent, received_low = send_far(kept, taken, head_count)
    high = [after(home[1], sent), high_left, high_right]
    rows_high, kept, taken = finish(info, meta, high, middle, *rest)
    taken, received_low = after((taken, received_low))
    sent, received_high = send_far(kept, taken, head_count)
    near, own = share(
        "near",
        [(True, 0), (False, 0)],
        after([rows_low, rows_high], sent),
        out_weight,
        head_count,
    )
    near = after(swap_cores(near, head_count, 4), received_high)
    columns = out_weight.shape[1] // head_count
    return last(own, near, received_low + received_high, columns, head_count).T


def solution(mesh):
    placed = (
        P("seq", "head"),
        P("seq", None, "head"),
        P("seq", None, None, "head"),
        P("head", None),
        P(),
        P(),
        P(),
    )
    return jax.shard_map(
        shards, mesh=mesh, in_specs=placed, out_specs=P("seq", "head"), check_vma=False
    )
```

```python
import functools
import math

import jax
import jax.numpy as jnp
from jax import lax
from jax.experimental import pallas as pl
from jax.experimental.pallas import tpu as pltpu
from jax.sharding import PartitionSpec as P

D = 5376
QUERY_HEADS = 32
KEY_VALUE_HEADS = 16
HEAD_WIDTH = 128
GROUP = QUERY_HEADS // KEY_VALUE_HEADS
RATE = float(D // QUERY_HEADS) ** (-0.5) * math.log2(math.e)
HIDDEN = -(2.0**99)
STAT = 128
SUM_HIGH = 32
SUM_LOW = 64
F32 = jnp.float32
BF16 = jnp.bfloat16
MIB = 1 << 20
LARGE_VMEM = 52 * MIB
ATTEND_VMEM = 24 * MIB
HINT = pl.CostEstimate(flops=1024, bytes_accessed=1024, transcendentals=0)
LONG = pl.CostEstimate(flops=1 << 33, bytes_accessed=1024, transcendentals=0)


def ring_member(place, count):
    return jnp.where(place < count // 2, 2 * place, 2 * (count - 1 - place) + 1)


def ring_order(count):
    return list(range(0, count, 2)) + list(range(count - 1, 0, -2))


def same_request_at(offset, count):
    order = ring_order(count)
    half = count // 2
    return any(order[(i + offset) % count] % half == order[i] % half for i in range(count))


class Meta:
    def __init__(self, count, holding):
        self.count = count
        self.half = count // 2
        self.holding = holding
        self.stride = holding + 1
        self.valid_at = self.half * self.stride
        self.live_at = 2 * self.half * self.stride
        self.suffix_at = self.live_at + self.half
        self.place_at = self.suffix_at + self.half
        self.length = self.place_at + 2

    def chunk(self, meta, offset):
        place = meta[self.place_at] + offset
        place = jnp.where(place < 0, place + self.count, place)
        place = jnp.where(place >= self.count, place - self.count, place)
        return ring_member(place, self.count)

    def request(self, chunk):
        return jnp.where(chunk >= self.half, chunk - self.half, chunk)

    def member(self, chunk):
        return jnp.where(chunk >= self.half, 1, 0)

    def slot(self, meta, request, page):
        return meta[request * self.stride + page]

    def valid(self, meta, request, page):
        return meta[self.valid_at + request * self.stride + page]


def table_kernel(info, pages_dev, page_rows, page_table, prefix_len, suffix_len, meta):
    seq_index = lax.axis_index("seq")
    first_slot = seq_index * pages_dev
    odd = seq_index % 2
    meta[info.place_at] = jnp.where(odd == 0, seq_index // 2, info.count - 1 - seq_index // 2)
    meta[info.place_at + 1] = seq_index

    def one_request(request, carry):
        prefix = prefix_len[request]
        base = request * info.stride

        def one_page(page, state):
            found, live = state
            local = page_table[request, page] - first_slot
            mine = (local >= 0) & (local < pages_dev)
            valid = jnp.minimum(jnp.maximum(prefix - page * page_rows, 0), page_rows)
            meta[base + found] = local
            meta[info.valid_at + base + found] = valid
            return (
                found + jnp.where(mine, 1, 0),
                live + jnp.where(mine & (valid > 0), 1, 0),
            )

        _, live = lax.fori_loop(0, page_table.shape[1], one_page, (0, 0))
        meta[info.live_at + request] = live
        meta[info.suffix_at + request] = suffix_len[request]
        return carry

    lax.fori_loop(0, info.half, one_request, 0)


def tables(info, pages_dev, page_rows, page_table, prefix_len, suffix_len):
    smem = pl.BlockSpec(memory_space=pltpu.SMEM)
    return pl.pallas_call(
        functools.partial(table_kernel, info, pages_dev, page_rows),
        out_shape=jax.ShapeDtypeStruct((info.length,), jnp.int32),
        in_specs=[smem] * 3,
        out_specs=smem,
        cost_estimate=HINT,
        name="tables",
    )(page_table, prefix_len, suffix_len)


def attend_kernel(info, offset, row_base, tok_rows, with_suffix, blocks, span, meta, *refs):
    holding = info.holding
    q_refs = refs[:blocks]
    refs = refs[blocks:]
    page_refs = refs[:holding]
    refs = refs[holding:]
    if with_suffix:
        suffix_ref = refs[0]
        refs = refs[1:]
    out_refs = refs[:blocks]
    acc_ref, max_ref, sum_ref = refs[blocks:]
    step = pl.program_id(0)
    rows = q_refs[0].shape[0]
    width = HEAD_WIDTH
    tall = GROUP * rows
    chunk = info.chunk(meta, offset)
    request = info.request(chunk)
    member = info.member(chunk)
    suffix = meta[info.suffix_at + request]
    first = member * tok_rows + row_base
    live_pages = meta[info.live_at + request]
    live_blocks = jnp.int32(0)
    for block in range(blocks):
        live_blocks = live_blocks + jnp.where(suffix > first + block * rows, 1, 0)

    def scores_of(query, keys):
        return lax.dot_general(
            query, keys, (((1,), (1,)), ((), ())), preferred_element_type=F32
        )

    def score_unit(group, block, pages, suffix_keys):
        lanes = slice(group * width, (group + 1) * width)
        query = jnp.concatenate(
            [
                q_refs[block][:, (group * GROUP + i) * width : (group * GROUP + i + 1) * width]
                for i in range(GROUP)
            ],
            axis=0,
        )
        scored = []
        if suffix_keys:
            scores = scores_of(query, suffix_ref[0, :, lanes])
            if offset == 0:
                shape = (rows, scores.shape[1])
                row = block * rows + lax.broadcasted_iota(jnp.int32, shape, 0)
                hidden = lax.broadcasted_iota(jnp.int32, shape, 1) > row
                scores = jnp.concatenate(
                    [
                        jnp.where(hidden, HIDDEN, scores[i * rows : (i + 1) * rows])
                        for i in range(GROUP)
                    ],
                    axis=0,
                )
            scored.append(scores)
        for j in range(pages):
            scores = scores_of(query, page_refs[j][0, 0, :, lanes])
            if j >= pages - 2:
                column = lax.broadcasted_iota(jnp.int32, scores.shape, 1)
                scores = jnp.where(column < info.valid(meta, request, j), scores, HIDDEN)
            scored.append(scores)
        return scored

    def weigh_unit(group, block, pages, suffix_keys, scored):
        lanes = slice(group * width, (group + 1) * width)
        values = [suffix_ref[1, :, lanes]] if suffix_keys else []
        values += [page_refs[j][0, 1, :, lanes] for j in range(pages)]
        top = scored[0]
        for scores in scored[1:]:
            top = jnp.maximum(top, scores)
        row_max = jnp.max(top, axis=1, keepdims=True).astype(BF16).astype(F32)
        weights = [jnp.exp2((scores - row_max) * RATE).astype(BF16) for scores in scored]
        summed = [
            jnp.concatenate([value, jnp.ones(value.shape, BF16)], axis=1) for value in values
        ]
        product = jnp.dot(
            jnp.concatenate(weights, axis=1),
            jnp.concatenate(summed, axis=0),
            preferred_element_type=F32,
        )
        at = group * blocks + block
        max_ref[at] = jnp.broadcast_to(row_max, (tall, STAT))
        sum_ref[at] = product[:, width:]
        acc_ref[at] = product[:, :width]

    def run(some, pages, suffix_keys):
        units = [(group, block) for group in range(span) for block in range(some)]
        coming = score_unit(*units[0], pages, suffix_keys)
        for number, unit in enumerate(units):
            scored = coming
            if number + 1 < len(units):
                coming = score_unit(*units[number + 1], pages, suffix_keys)
            weigh_unit(*unit, pages, suffix_keys, scored)

    if with_suffix:
        own = meta[info.place_at + 1]
        sees = (request == info.request(own)) & (member >= info.member(own))
        nothing = (live_pages == 0) & jnp.logical_not(sees)
    else:
        nothing = live_pages == 0
    for block in range(blocks):

        @pl.when((live_blocks <= (0 if with_suffix else block)) | nothing)
        def _(block=block):
            for group in range(span):
                at = group * blocks + block
                acc_ref[at] = jnp.zeros((tall, width), F32)
                max_ref[at] = jnp.full((tall, STAT), HIDDEN, F32)
                sum_ref[at] = jnp.zeros((tall, STAT), F32)

    for pages in [0] + list(range(holding, 0, -2)):
        if pages == 0:
            counted = live_pages == 0
        else:
            counted = (live_pages <= pages) & (live_pages >= max(pages - 1, 1))
        for some in [blocks] if with_suffix else range(1, blocks + 1):
            here = counted & (live_blocks == some)
            if with_suffix:
                here = counted & (live_blocks > 0)
                pl.when(here & sees)(functools.partial(run, some, pages, True))
                here = here & jnp.logical_not(sees)
            if pages > 0 and offset != 0:
                pl.when(here)(functools.partial(run, some, pages, False))

    stat_at = out_refs[0].shape[1] - STAT
    lane = lax.broadcasted_iota(jnp.int32, (rows, STAT), 1)
    for block, out_ref in enumerate(out_refs):

        @pl.when(step == 0)
        def _(out_ref=out_ref):
            out_ref[:, stat_at:] = jnp.zeros((rows, STAT), BF16)

        stats = out_ref[:, stat_at:].astype(F32)
        for group in range(span):
            at = group * blocks + block
            for i in range(GROUP):
                part = slice(i * rows, (i + 1) * rows)
                head = (step * span + group) * GROUP + i
                column = pl.multiple_of(head * width, width)
                out_ref[:, pl.ds(column, width)] = acc_ref[at, part, :].astype(BF16)
                total = sum_ref[at, part, :]
                high = total.astype(BF16).astype(F32)
                stats = jnp.where(lane == head, max_ref[at, part, :], stats)
                stats = jnp.where(lane == SUM_HIGH + head, high, stats)
                stats = jnp.where(lane == SUM_LOW + head, total - high, stats)
        out_ref[:, stat_at:] = stats.astype(BF16)


def attend(info, meta, query, offset, row_base, tok_rows, pages, suffix, hint):
    rows = tok_rows // 2
    blocks = len(query)
    columns = query[0].shape[1]
    holding = info.holding
    kv_local = pages.shape[3] // HEAD_WIDTH
    span = 2 if kv_local % 2 == 0 else 1
    page_rows = pages.shape[2]
    with_suffix = same_request_at(offset, info.count)

    def page_map(page, step, meta):
        request = info.request(info.chunk(meta, offset))
        return (info.slot(meta, request, page), 0, 0, step)

    in_specs = [pl.BlockSpec((rows, span * GROUP * HEAD_WIDTH), lambda g, meta: (0, g))] * blocks
    in_specs += [
        pl.BlockSpec((1, 2, page_rows, span * HEAD_WIDTH), functools.partial(page_map, j))
        for j in range(holding)
    ]
    operands = list(query) + [pages] * holding
    if with_suffix:
        in_specs.append(
            pl.BlockSpec((2, tok_rows, span * HEAD_WIDTH), lambda g, meta: (0, 0, g))
        )
        operands.append(suffix)
    out = jax.ShapeDtypeStruct((rows, columns + STAT), BF16)
    scratch = pltpu.VMEM((span * blocks, GROUP * rows, STAT), F32)
    return pl.pallas_call(
        functools.partial(
            attend_kernel, info, offset, row_base, tok_rows, with_suffix, blocks, span
        ),
        grid_spec=pltpu.PrefetchScalarGridSpec(
            num_scalar_prefetch=1,
            grid=(kv_local // span,),
            in_specs=in_specs,
            out_specs=[pl.BlockSpec((rows, columns + STAT), lambda g, meta: (0, 0))] * blocks,
            scratch_shapes=[scratch] * 3,
        ),
        out_shape=[out] * blocks,
        compiler_params=pltpu.CompilerParams(vmem_limit_bytes=ATTEND_VMEM),
        cost_estimate=hint,
        name="attend",
    )(meta, *operands)


def combine(packed, divided=False):
    stat_at = packed[0].shape[1] - STAT
    stats = [one[:, stat_at:].astype(F32) for one in packed]
    top = stats[0]
    for one in stats[1:]:
        top = jnp.maximum(top, one)
    factors = [jnp.exp2((jnp.minimum(one - top, 0.0)) * RATE) for one in stats]
    total = None
    for one, factor in zip(stats, factors):
        own = pltpu.roll(one, STAT - SUM_HIGH, 1) + pltpu.roll(one, STAT - SUM_LOW, 1)
        total = own * factor if total is None else total + own * factor
    if divided:
        factors = [factor / total for factor in factors]
    heads = []
    for head in range(stat_at // HEAD_WIDTH):
        mixed = None
        for one, factor in zip(packed, factors):
            value = one[:, head * HEAD_WIDTH : (head + 1) * HEAD_WIDTH].astype(F32)
            value = value * factor[:, head : head + 1]
            mixed = value if mixed is None else mixed + value
        heads.append(mixed)
    return (heads, top, total)


def merge_kernel(a_ref, b_ref, out_ref):
    heads, top, total = combine([a_ref[...], b_ref[...]])
    for head, mixed in enumerate(heads):
        out_ref[:, head * HEAD_WIDTH : (head + 1) * HEAD_WIDTH] = mixed.astype(BF16)
    high = total.astype(BF16).astype(F32)
    lane = lax.broadcasted_iota(jnp.int32, top.shape, 1)
    stats = jnp.where(lane < SUM_HIGH, top, 0.0)
    stats = jnp.where((lane >= SUM_HIGH) & (lane < SUM_LOW), pltpu.roll(high, SUM_HIGH, 1), stats)
    low = pltpu.roll(total - high, SUM_LOW, 1)
    stats = jnp.where((lane >= SUM_LOW) & (lane < SUM_LOW + SUM_HIGH), low, stats)
    out_ref[:, len(heads) * HEAD_WIDTH :] = stats.astype(BF16)


def merge(a, b):
    return pl.pallas_call(
        merge_kernel,
        out_shape=jax.ShapeDtypeStruct(a.shape, BF16),
        in_specs=[pl.BlockSpec(memory_space=pltpu.VMEM)] * 2,
        out_specs=pl.BlockSpec(memory_space=pltpu.VMEM),
        compiler_params=pltpu.CompilerParams(vmem_limit_bytes=16 * MIB),
        cost_estimate=HINT,
        name="merge",
    )(a, b)


def window_of(columns, head_count):
    spans = [
        -(-(t + 1) * columns // STAT) - t * columns // STAT for t in range(head_count)
    ]
    return max(spans) * STAT


def window_start(target, columns, head_count):
    start = target * columns // STAT * STAT
    return jnp.minimum(start, columns * head_count - window_of(columns, head_count))


def project(head_count, wanted, attention, weight, out_refs, window, sems):
    columns = weight.shape[1] // head_count
    half = head_count // 2
    head_index = lax.axis_index("head")
    pair = head_index // 2
    copies = []
    for number, (other, turn) in enumerate(wanted):
        core = head_index % 2
        core = 1 - core if other else core
        target = 2 * ((pair + turn) % half) + core
        start = pl.multiple_of(window_start(target, columns, head_count), STAT)
        copies.append(
            pltpu.make_async_copy(
                weight.at[:, pl.ds(start, window.shape[2])], window.at[number], sems.at[number]
            )
        )
        copies[-1].start()
    rows = attention()
    for number, copy in enumerate(copies):
        copy.wait()
        product = jnp.dot(rows, window[number], preferred_element_type=F32)
        out_refs[number][...] = product.astype(BF16)


def finish_kernel(info, tok_rows, first_row, shares, head_count, wanted, meta, *refs):
    weight, rows_ref = refs[shares : shares + 2]
    rest = refs[shares + 2 :]

    def attention():
        chunk = info.chunk(meta, 0)
        suffix = meta[info.suffix_at + info.request(chunk)]
        heads, _, total = combine([ref[...] for ref in refs[:shares]], True)
        first = info.member(chunk) * tok_rows + first_row
        place = first + lax.broadcasted_iota(jnp.int32, heads[0].shape, 0)
        for head, mixed in enumerate(heads):
            value = jnp.where(place < suffix, mixed, 0.0)
            rows_ref[:, head * HEAD_WIDTH : (head + 1) * HEAD_WIDTH] = value.astype(BF16)
        return rows_ref[...]

    project(head_count, wanted, attention, weight, rest[: len(wanted)], *rest[len(wanted) :])


def share_kernel(head_count, wanted, parts, *refs):
    weight = refs[parts]
    outs = refs[parts + 1 : parts + 1 + len(wanted)]

    def attention():
        return jnp.concatenate([ref[...] for ref in refs[:parts]], axis=0)

    project(head_count, wanted, attention, weight, outs, *refs[parts + 1 + len(wanted) :])


def project_call(kernel, name, wanted, rows, weight, head_count, operands, with_rows, with_meta):
    depth = weight.shape[0]
    wide = window_of(weight.shape[1] // head_count, head_count)
    vmem = pl.BlockSpec(memory_space=pltpu.VMEM)
    smem = [pl.BlockSpec(memory_space=pltpu.SMEM)] * with_meta
    out = [jax.ShapeDtypeStruct((rows, depth), BF16)] * with_rows
    out += [jax.ShapeDtypeStruct((rows, wide), BF16)] * len(wanted)
    return pl.pallas_call(
        kernel,
        out_shape=out,
        in_specs=smem
        + [vmem] * (len(operands) - with_meta)
        + [pl.BlockSpec(memory_space=pl.ANY)],
        out_specs=[vmem] * len(out),
        scratch_shapes=[
            pltpu.VMEM((len(wanted), depth, wide), BF16),
            pltpu.SemaphoreType.DMA((len(wanted),)),
        ],
        compiler_params=pltpu.CompilerParams(vmem_limit_bytes=LARGE_VMEM),
        cost_estimate=HINT,
        name=name,
    )(*operands, weight)


def share(name, wanted, attention, weight, head_count):
    return project_call(
        functools.partial(share_kernel, head_count, wanted, len(attention)),
        name,
        wanted,
        sum(part.shape[0] for part in attention),
        weight,
        head_count,
        list(attention),
        0,
        0,
    )


def finish(info, meta, packed, first_row, weight, tok_rows, head_count):
    half = head_count // 2
    other = [(True, turn) for turn in range(1, half)]
    own = [(False, turn) for turn in range(1, half)]
    attention, *given = project_call(
        functools.partial(
            finish_kernel, info, tok_rows, first_row, len(packed), head_count, other
        ),
        "finish",
        other,
        packed[0].shape[0],
        weight,
        head_count,
        [meta, *packed],
        1,
        1,
    )
    taken = [swap_cores(one, head_count, 2) for one in given]
    return (attention, share("far", own, [attention], weight, head_count), taken)


def swap_cores(value, head_count, pieces):
    rows = value.shape[0] // pieces
    pairs = [(i, i ^ 1) for i in range(head_count)]
    return [
        lax.ppermute(value[i * rows : (i + 1) * rows], "head", pairs) for i in range(pieces)
    ]


def send_far(kept, taken, head_count):
    sent = []
    received = []
    for number, (mine, theirs) in enumerate(zip(kept, taken)):
        step = number + 1
        pairs = [(i, (i + 2 * step) % head_count) for i in range(head_count)]
        theirs = jnp.concatenate(theirs, axis=0)
        sent.append((mine.astype(F32) + theirs.astype(F32)).astype(BF16))
        received.append(lax.ppermute(sent[-1], "head", pairs))
    return (sent, received)


def last_kernel(columns, head_count, pieces, own_ref, *refs):
    near_refs = refs[:pieces]
    refs = refs[pieces:]
    out_ref, turned = refs[-2:]
    halves = [refs[: (len(refs) - 2) // 2], refs[(len(refs) - 2) // 2 : -2]]
    head_index = lax.axis_index("head")
    shift = head_index * columns - window_start(head_index, columns, head_count)
    rows = own_ref.shape[0] // 2
    for number, received in enumerate(halves):
        part = slice(number * rows, (number + 1) * rows)
        near = near_refs[number * pieces // 2 : (number + 1) * pieces // 2]
        total = own_ref[part].astype(F32)
        total = total + jnp.concatenate([ref[...] for ref in near], axis=0).astype(F32)
        for ref in received:
            total = total + ref[...].astype(F32)
        turned[:, part] = total.T
    out_ref[...] = turned[pl.ds(pl.multiple_of(shift, 8), columns), :].astype(BF16)


def last(own, near, received, columns, head_count):
    rows, wide = own.shape
    vmem = pl.BlockSpec(memory_space=pltpu.VMEM)
    return pl.pallas_call(
        functools.partial(last_kernel, columns, head_count, len(near)),
        out_shape=jax.ShapeDtypeStruct((columns, rows), BF16),
        in_specs=[vmem] * (1 + len(near) + len(received)),
        out_specs=vmem,
        scratch_shapes=[pltpu.VMEM((wide, rows), F32)],
        compiler_params=pltpu.CompilerParams(vmem_limit_bytes=16 * MIB),
        cost_estimate=HINT,
        name="last",
    )(own, *near, *received)


def after(value, *others):
    return lax.optimization_barrier((value, others))[0]


def shards(queries, suffix_key_value, pooled_pages, out_weight, page_table, prefix_len, suffix_len):
    tok_rows = queries.shape[0]
    pages_dev, page_rows = pooled_pages.shape[:2]
    count = lax.axis_size("seq")
    head_count = lax.axis_size("head")
    reach = count // 2
    info = Meta(count, 2 * pages_dev // count)
    order = ring_order(count)
    ahead = [(order[i], order[(i + 1) % count]) for i in range(count)]
    back = [(b, a) for a, b in ahead]
    middle = tok_rows // 2

    meta = tables(info, pages_dev, page_rows, page_table, prefix_len, suffix_len)
    pages = jnp.transpose(pooled_pages, (0, 2, 1, 3))
    suffix = jnp.transpose(suffix_key_value, (1, 0, 2))

    def partial_of(query, offset, row_base=0, hint=HINT):
        return attend(info, meta, query, offset, row_base, tok_rows, pages, suffix, hint)

    halves = [queries[:middle], queries[middle:]]
    left = [halves]
    right = [halves]
    part_left = {}
    part_right = {}
    late = reach - 2

    for step in range(1, reach + 1):
        end = step == reach
        low_left = lax.ppermute(left[-1][0], "seq", ahead)
        if not end:
            low_right = lax.ppermute(right[-1][0], "seq", back)
            high_left = lax.ppermute(left[-1][1], "seq", ahead)
        high_right = lax.ppermute(right[-1][1], "seq", back)
        if step == 1:
            done = (meta, pages)
        elif step == reach - 1:
            home = partial_of(halves, 0)
            done = home
        elif step == reach:
            part_left[step - 1] = partial_of(left[step - 1], 1 - step)
            part_right[step - 1] = partial_of(right[step - 1], step - 1)
            done = (part_left[step - 1], part_right[step - 1])
        else:
            part_left[step - 1] = partial_of(left[step - 1], 1 - step)
            done = part_left[step - 1]
        if end:
            low_left, high_right = after((low_left, high_right), done)
            left.append([low_left])
            right.append([high_right])
        else:
            low_left, low_right = after((low_left, low_right), done)
            high_left, high_right = after((high_left, high_right), low_left, low_right)
            left.append([low_left, high_left])
            right.append([low_right, high_right])

    low_right = lax.ppermute(part_right[reach - 1][0], "seq", ahead)
    high_left = lax.ppermute(part_left[reach - 1][1], "seq", back)
    far_left = partial_of(left[reach], -reach)[0]
    far_right = partial_of(right[reach], reach, middle)[0]
    low_left = lax.ppermute(far_left, "seq", back)
    high_right = lax.ppermute(far_right, "seq", ahead)
    right[late] = after(right[late], far_left, far_right)
    part_right[late] = partial_of(right[late], late, 0, LONG)
    latest = part_right[late]

    def onward(travelled, mine, pairs):
        merged = merge(after(travelled, latest), mine)
        return (lax.ppermute(merged, "seq", pairs), merged)

    for step in range(reach - 1, 1, -1):
        low_left, latest = onward(low_left, part_left[step][0], back)
        if step - 1 not in part_right:
            right[step - 1] = after(right[step - 1], latest)
            part_right[step - 1] = partial_of(right[step - 1], step - 1)
            latest = part_right[step - 1]
        if step == 2:
            low_right, latest = onward(low_right, part_right[step - 1][0], ahead)
            high_left, high_right = after((high_left, high_right), latest)
            high_right, latest = onward(high_right, part_right[step][1], ahead)
        else:
            high_right, latest = onward(high_right, part_right[step][1], ahead)
            if step - 1 not in part_left:
                left[step - 1] = after(left[step - 1], latest)
                part_left[step - 1] = partial_of(left[step - 1], 1 - step, 0, LONG)
                latest = part_left[step - 1]
            high_left, latest = onward(high_left, part_left[step - 1][1], back)
            low_right, latest = onward(low_right, part_right[step - 1][0], ahead)
    low_left, latest = onward(low_left, part_left[1][0], back)
    high_left, latest = onward(high_left, part_left[1][1], back)
    early = merge(after(low_right, latest), home[0])
    latest = early
    high_right, latest = onward(high_right, part_right[1][1], ahead)

    low = [early, after(low_left, latest)]
    rest = (out_weight, tok_rows, head_count)
    rows_low, kept, taken = finish(info, meta, low, 0, *rest)
    taken, high_left, high_right = after((taken, high_left, high_right))
    sent, received_low = send_far(kept, taken, head_count)
    high = [after(home[1], sent), high_left, high_right]
    rows_high, kept, taken = finish(info, meta, high, middle, *rest)
    taken, received_low = after((taken, received_low))
    sent, received_high = send_far(kept, taken, head_count)
    near, own = share(
        "near",
        [(True, 0), (False, 0)],
        after([rows_low, rows_high], sent),
        out_weight,
        head_count,
    )
    near = after(swap_cores(near, head_count, 4), received_high)
    columns = out_weight.shape[1] // head_count
    return last(own, near, received_low + received_high, columns, head_count).T


def solution(mesh):
    placed = (
        P("seq", "head"),
        P("seq", None, "head"),
        P("seq", None, None, "head"),
        P("head", None),
        P(),
        P(),
        P(),
    )
    return jax.shard_map(
        shards, mesh=mesh, in_specs=placed, out_specs=P("seq", "head"), check_vma=False
    )
```

```python
import functools
import math

import jax
import jax.numpy as jnp
from jax import lax
from jax.experimental import pallas as pl
from jax.experimental.pallas import tpu as pltpu
from jax.sharding import PartitionSpec as P

D = 5376
QUERY_HEADS = 32
KEY_VALUE_HEADS = 16
HEAD_WIDTH = 128
GROUP = QUERY_HEADS // KEY_VALUE_HEADS
RATE = float(D // QUERY_HEADS) ** (-0.5) * math.log2(math.e)
HIDDEN = -(2.0**99)
STAT = 128
SUM_HIGH = 32
SUM_LOW = 64
F32 = jnp.float32
BF16 = jnp.bfloat16
MIB = 1 << 20
LARGE_VMEM = 52 * MIB
ATTEND_VMEM = 24 * MIB
HINT = pl.CostEstimate(flops=1024, bytes_accessed=1024, transcendentals=0)
LONG = pl.CostEstimate(flops=1 << 33, bytes_accessed=1024, transcendentals=0)


def ring_member(place, count):
    return jnp.where(place < count // 2, 2 * place, 2 * (count - 1 - place) + 1)


def ring_order(count):
    return list(range(0, count, 2)) + list(range(count - 1, 0, -2))


def same_request_at(offset, count):
    order = ring_order(count)
    half = count // 2
    return any(order[(i + offset) % count] % half == order[i] % half for i in range(count))


class Meta:
    def __init__(self, count, holding):
        self.count = count
        self.half = count // 2
        self.holding = holding
        self.stride = holding + 1
        self.valid_at = self.half * self.stride
        self.live_at = 2 * self.half * self.stride
        self.suffix_at = self.live_at + self.half
        self.place_at = self.suffix_at + self.half
        self.length = self.place_at + 2

    def chunk(self, meta, offset):
        place = meta[self.place_at] + offset
        place = jnp.where(place < 0, place + self.count, place)
        place = jnp.where(place >= self.count, place - self.count, place)
        return ring_member(place, self.count)

    def request(self, chunk):
        return jnp.where(chunk >= self.half, chunk - self.half, chunk)

    def member(self, chunk):
        return jnp.where(chunk >= self.half, 1, 0)

    def slot(self, meta, request, page):
        return meta[request * self.stride + page]

    def valid(self, meta, request, page):
        return meta[self.valid_at + request * self.stride + page]


def table_kernel(info, pages_dev, page_rows, page_table, prefix_len, suffix_len, meta):
    seq_index = lax.axis_index("seq")
    first_slot = seq_index * pages_dev
    odd = seq_index % 2
    meta[info.place_at] = jnp.where(odd == 0, seq_index // 2, info.count - 1 - seq_index // 2)
    meta[info.place_at + 1] = seq_index

    def one_request(request, carry):
        prefix = prefix_len[request]
        base = request * info.stride

        def one_page(page, state):
            found, live = state
            local = page_table[request, page] - first_slot
            mine = (local >= 0) & (local < pages_dev)
            valid = jnp.minimum(jnp.maximum(prefix - page * page_rows, 0), page_rows)
            meta[base + found] = local
            meta[info.valid_at + base + found] = valid
            return (
                found + jnp.where(mine, 1, 0),
                live + jnp.where(mine & (valid > 0), 1, 0),
            )

        _, live = lax.fori_loop(0, page_table.shape[1], one_page, (0, 0))
        meta[info.live_at + request] = live
        meta[info.suffix_at + request] = suffix_len[request]
        return carry

    lax.fori_loop(0, info.half, one_request, 0)


def tables(info, pages_dev, page_rows, page_table, prefix_len, suffix_len):
    smem = pl.BlockSpec(memory_space=pltpu.SMEM)
    return pl.pallas_call(
        functools.partial(table_kernel, info, pages_dev, page_rows),
        out_shape=jax.ShapeDtypeStruct((info.length,), jnp.int32),
        in_specs=[smem] * 3,
        out_specs=smem,
        cost_estimate=HINT,
        name="tables",
    )(page_table, prefix_len, suffix_len)


def attend_kernel(info, offset, row_base, tok_rows, with_suffix, blocks, span, meta, q_ref, *refs):
    holding = info.holding
    page_refs = refs[:holding]
    refs = refs[holding:]
    if with_suffix:
        suffix_ref = refs[0]
        refs = refs[1:]
    out_refs = refs[:blocks]
    acc_ref, max_ref, sum_ref = refs[blocks:]
    step = pl.program_id(0)
    rows = q_ref.shape[0] // blocks
    width = HEAD_WIDTH
    tall = GROUP * rows
    chunk = info.chunk(meta, offset)
    request = info.request(chunk)
    member = info.member(chunk)
    suffix = meta[info.suffix_at + request]
    first = member * tok_rows + row_base
    live_pages = meta[info.live_at + request]
    live_blocks = jnp.int32(0)
    for block in range(blocks):
        live_blocks = live_blocks + jnp.where(suffix > first + block * rows, 1, 0)

    def scores_of(query, keys):
        return lax.dot_general(
            query, keys, (((1,), (1,)), ((), ())), preferred_element_type=F32
        )

    def score_unit(group, block, pages, suffix_keys):
        part = slice(block * rows, (block + 1) * rows)
        lanes = slice(group * width, (group + 1) * width)
        query = jnp.concatenate(
            [
                q_ref[part, (group * GROUP + i) * width : (group * GROUP + i + 1) * width]
                for i in range(GROUP)
            ],
            axis=0,
        )
        scored = []
        if suffix_keys:
            scores = scores_of(query, suffix_ref[0, :, lanes])
            if offset == 0:
                shape = (rows, scores.shape[1])
                row = block * rows + lax.broadcasted_iota(jnp.int32, shape, 0)
                hidden = lax.broadcasted_iota(jnp.int32, shape, 1) > row
                scores = jnp.concatenate(
                    [
                        jnp.where(hidden, HIDDEN, scores[i * rows : (i + 1) * rows])
                        for i in range(GROUP)
                    ],
                    axis=0,
                )
            scored.append(scores)
        for j in range(pages):
            scores = scores_of(query, page_refs[j][0, 0, :, lanes])
            if j >= pages - 2:
                column = lax.broadcasted_iota(jnp.int32, scores.shape, 1)
                scores = jnp.where(column < info.valid(meta, request, j), scores, HIDDEN)
            scored.append(scores)
        return scored

    def weigh_unit(group, block, pages, suffix_keys, scored):
        lanes = slice(group * width, (group + 1) * width)
        values = [suffix_ref[1, :, lanes]] if suffix_keys else []
        values += [page_refs[j][0, 1, :, lanes] for j in range(pages)]
        top = scored[0]
        for scores in scored[1:]:
            top = jnp.maximum(top, scores)
        row_max = jnp.max(top, axis=1, keepdims=True).astype(BF16).astype(F32)
        weights = [jnp.exp2((scores - row_max) * RATE).astype(BF16) for scores in scored]
        summed = [
            jnp.concatenate([value, jnp.ones(value.shape, BF16)], axis=1) for value in values
        ]
        product = jnp.dot(
            jnp.concatenate(weights, axis=1),
            jnp.concatenate(summed, axis=0),
            preferred_element_type=F32,
        )
        at = group * blocks + block
        max_ref[at] = jnp.broadcast_to(row_max, (tall, STAT))
        sum_ref[at] = product[:, width:]
        acc_ref[at] = product[:, :width]

    def run(some, pages, suffix_keys):
        units = [(group, block) for group in range(span) for block in range(some)]
        coming = score_unit(*units[0], pages, suffix_keys)
        for number, unit in enumerate(units):
            scored = coming
            if number + 1 < len(units):
                coming = score_unit(*units[number + 1], pages, suffix_keys)
            weigh_unit(*unit, pages, suffix_keys, scored)

    if with_suffix:
        own = meta[info.place_at + 1]
        sees = (request == info.request(own)) & (member >= info.member(own))
        nothing = (live_pages == 0) & jnp.logical_not(sees)
    else:
        nothing = live_pages == 0
    for block in range(blocks):

        @pl.when((live_blocks <= (0 if with_suffix else block)) | nothing)
        def _(block=block):
            for group in range(span):
                at = group * blocks + block
                acc_ref[at] = jnp.zeros((tall, width), F32)
                max_ref[at] = jnp.full((tall, STAT), HIDDEN, F32)
                sum_ref[at] = jnp.zeros((tall, STAT), F32)

    for pages in [0] + list(range(holding, 0, -2)):
        if pages == 0:
            counted = live_pages == 0
        else:
            counted = (live_pages <= pages) & (live_pages >= max(pages - 1, 1))
        for some in [blocks] if with_suffix else range(1, blocks + 1):
            here = counted & (live_blocks == some)
            if with_suffix:
                here = counted & (live_blocks > 0)
                pl.when(here & sees)(functools.partial(run, some, pages, True))
                here = here & jnp.logical_not(sees)
            if pages > 0 and offset != 0:
                pl.when(here)(functools.partial(run, some, pages, False))

    stat_at = out_refs[0].shape[1] - STAT
    lane = lax.broadcasted_iota(jnp.int32, (rows, STAT), 1)
    for block, out_ref in enumerate(out_refs):

        @pl.when(step == 0)
        def _(out_ref=out_ref):
            out_ref[:, stat_at:] = jnp.zeros((rows, STAT), BF16)

        stats = out_ref[:, stat_at:].astype(F32)
        for group in range(span):
            at = group * blocks + block
            for i in range(GROUP):
                part = slice(i * rows, (i + 1) * rows)
                head = (step * span + group) * GROUP + i
                column = pl.multiple_of(head * width, width)
                out_ref[:, pl.ds(column, width)] = acc_ref[at, part, :].astype(BF16)
                total = sum_ref[at, part, :]
                high = total.astype(BF16).astype(F32)
                stats = jnp.where(lane == head, max_ref[at, part, :], stats)
                stats = jnp.where(lane == SUM_HIGH + head, high, stats)
                stats = jnp.where(lane == SUM_LOW + head, total - high, stats)
        out_ref[:, stat_at:] = stats.astype(BF16)


def attend(info, meta, query, offset, row_base, tok_rows, pages, suffix, hint):
    rows = tok_rows // 2
    blocks = query.shape[0] // rows
    columns = query.shape[1]
    holding = info.holding
    kv_local = pages.shape[3] // HEAD_WIDTH
    span = 2 if kv_local % 2 == 0 else 1
    page_rows = pages.shape[2]
    with_suffix = same_request_at(offset, info.count)

    def page_map(page, step, meta):
        request = info.request(info.chunk(meta, offset))
        return (info.slot(meta, request, page), 0, 0, step)

    in_specs = [pl.BlockSpec((query.shape[0], span * GROUP * HEAD_WIDTH), lambda g, meta: (0, g))]
    in_specs += [
        pl.BlockSpec((1, 2, page_rows, span * HEAD_WIDTH), functools.partial(page_map, j))
        for j in range(holding)
    ]
    operands = [query] + [pages] * holding
    if with_suffix:
        in_specs.append(
            pl.BlockSpec((2, tok_rows, span * HEAD_WIDTH), lambda g, meta: (0, 0, g))
        )
        operands.append(suffix)
    out = jax.ShapeDtypeStruct((rows, columns + STAT), BF16)
    scratch = pltpu.VMEM((span * blocks, GROUP * rows, STAT), F32)
    return pl.pallas_call(
        functools.partial(
            attend_kernel, info, offset, row_base, tok_rows, with_suffix, blocks, span
        ),
        grid_spec=pltpu.PrefetchScalarGridSpec(
            num_scalar_prefetch=1,
            grid=(kv_local // span,),
            in_specs=in_specs,
            out_specs=[pl.BlockSpec((rows, columns + STAT), lambda g, meta: (0, 0))] * blocks,
            scratch_shapes=[scratch] * 3,
        ),
        out_shape=[out] * blocks,
        compiler_params=pltpu.CompilerParams(vmem_limit_bytes=ATTEND_VMEM),
        cost_estimate=hint,
        name="attend",
    )(meta, *operands)


def combine(packed, divided=False):
    stat_at = packed[0].shape[1] - STAT
    stats = [one[:, stat_at:].astype(F32) for one in packed]
    top = stats[0]
    for one in stats[1:]:
        top = jnp.maximum(top, one)
    factors = [jnp.exp2((jnp.minimum(one - top, 0.0)) * RATE) for one in stats]
    total = None
    for one, factor in zip(stats, factors):
        own = pltpu.roll(one, STAT - SUM_HIGH, 1) + pltpu.roll(one, STAT - SUM_LOW, 1)
        total = own * factor if total is None else total + own * factor
    if divided:
        factors = [factor / total for factor in factors]
    heads = []
    for head in range(stat_at // HEAD_WIDTH):
        mixed = None
        for one, factor in zip(packed, factors):
            value = one[:, head * HEAD_WIDTH : (head + 1) * HEAD_WIDTH].astype(F32)
            value = value * factor[:, head : head + 1]
            mixed = value if mixed is None else mixed + value
        heads.append(mixed)
    return (heads, top, total)


def merge_kernel(a_ref, b_ref, out_ref):
    heads, top, total = combine([a_ref[...], b_ref[...]])
    for head, mixed in enumerate(heads):
        out_ref[:, head * HEAD_WIDTH : (head + 1) * HEAD_WIDTH] = mixed.astype(BF16)
    high = total.astype(BF16).astype(F32)
    lane = lax.broadcasted_iota(jnp.int32, top.shape, 1)
    stats = jnp.where(lane < SUM_HIGH, top, 0.0)
    stats = jnp.where((lane >= SUM_HIGH) & (lane < SUM_LOW), pltpu.roll(high, SUM_HIGH, 1), stats)
    low = pltpu.roll(total - high, SUM_LOW, 1)
    stats = jnp.where((lane >= SUM_LOW) & (lane < SUM_LOW + SUM_HIGH), low, stats)
    out_ref[:, len(heads) * HEAD_WIDTH :] = stats.astype(BF16)


def merge(a, b):
    return pl.pallas_call(
        merge_kernel,
        out_shape=jax.ShapeDtypeStruct(a.shape, BF16),
        in_specs=[pl.BlockSpec(memory_space=pltpu.VMEM)] * 2,
        out_specs=pl.BlockSpec(memory_space=pltpu.VMEM),
        compiler_params=pltpu.CompilerParams(vmem_limit_bytes=16 * MIB),
        cost_estimate=HINT,
        name="merge",
    )(a, b)


def window_of(columns, head_count):
    spans = [
        -(-(t + 1) * columns // STAT) - t * columns // STAT for t in range(head_count)
    ]
    return max(spans) * STAT


def window_start(target, columns, head_count):
    start = target * columns // STAT * STAT
    return jnp.minimum(start, columns * head_count - window_of(columns, head_count))


def project(head_count, wanted, attention, weight, out_refs, window, sems):
    columns = weight.shape[1] // head_count
    half = head_count // 2
    head_index = lax.axis_index("head")
    pair = head_index // 2
    copies = []
    for number, (other, turn) in enumerate(wanted):
        core = head_index % 2
        core = 1 - core if other else core
        target = 2 * ((pair + turn) % half) + core
        start = pl.multiple_of(window_start(target, columns, head_count), STAT)
        copies.append(
            pltpu.make_async_copy(
                weight.at[:, pl.ds(start, window.shape[2])], window.at[number], sems.at[number]
            )
        )
        copies[-1].start()
    rows = attention()
    for number, copy in enumerate(copies):
        copy.wait()
        product = jnp.dot(rows, window[number], preferred_element_type=F32)
        out_refs[number][...] = product.astype(BF16)


def finish_kernel(info, tok_rows, first_row, shares, head_count, wanted, meta, *refs):
    weight, rows_ref = refs[shares : shares + 2]
    rest = refs[shares + 2 :]

    def attention():
        chunk = info.chunk(meta, 0)
        suffix = meta[info.suffix_at + info.request(chunk)]
        heads, _, total = combine([ref[...] for ref in refs[:shares]], True)
        first = info.member(chunk) * tok_rows + first_row
        place = first + lax.broadcasted_iota(jnp.int32, heads[0].shape, 0)
        for head, mixed in enumerate(heads):
            value = jnp.where(place < suffix, mixed, 0.0)
            rows_ref[:, head * HEAD_WIDTH : (head + 1) * HEAD_WIDTH] = value.astype(BF16)
        return rows_ref[...]

    project(head_count, wanted, attention, weight, rest[: len(wanted)], *rest[len(wanted) :])


def share_kernel(head_count, wanted, parts, *refs):
    weight = refs[parts]
    outs = refs[parts + 1 : parts + 1 + len(wanted)]

    def attention():
        return jnp.concatenate([ref[...] for ref in refs[:parts]], axis=0)

    project(head_count, wanted, attention, weight, outs, *refs[parts + 1 + len(wanted) :])


def project_call(kernel, name, wanted, rows, weight, head_count, operands, with_rows, with_meta):
    depth = weight.shape[0]
    wide = window_of(weight.shape[1] // head_count, head_count)
    vmem = pl.BlockSpec(memory_space=pltpu.VMEM)
    smem = [pl.BlockSpec(memory_space=pltpu.SMEM)] * with_meta
    out = [jax.ShapeDtypeStruct((rows, depth), BF16)] * with_rows
    out += [jax.ShapeDtypeStruct((rows, wide), BF16)] * len(wanted)
    return pl.pallas_call(
        kernel,
        out_shape=out,
        in_specs=smem
        + [vmem] * (len(operands) - with_meta)
        + [pl.BlockSpec(memory_space=pl.ANY)],
        out_specs=[vmem] * len(out),
        scratch_shapes=[
            pltpu.VMEM((len(wanted), depth, wide), BF16),
            pltpu.SemaphoreType.DMA((len(wanted),)),
        ],
        compiler_params=pltpu.CompilerParams(vmem_limit_bytes=LARGE_VMEM),
        cost_estimate=HINT,
        name=name,
    )(*operands, weight)


def share(name, wanted, attention, weight, head_count):
    return project_call(
        functools.partial(share_kernel, head_count, wanted, len(attention)),
        name,
        wanted,
        sum(part.shape[0] for part in attention),
        weight,
        head_count,
        list(attention),
        0,
        0,
    )


def finish(info, meta, packed, first_row, weight, tok_rows, head_count):
    half = head_count // 2
    other = [(True, turn) for turn in range(1, half)]
    own = [(False, turn) for turn in range(1, half)]
    attention, *given = project_call(
        functools.partial(
            finish_kernel, info, tok_rows, first_row, len(packed), head_count, other
        ),
        "finish",
        other,
        packed[0].shape[0],
        weight,
        head_count,
        [meta, *packed],
        1,
        1,
    )
    taken = [swap_cores(one, head_count, 2) for one in given]
    return (attention, share("far", own, [attention], weight, head_count), taken)


def swap_cores(value, head_count, pieces):
    rows = value.shape[0] // pieces
    pairs = [(i, i ^ 1) for i in range(head_count)]
    return [
        lax.ppermute(value[i * rows : (i + 1) * rows], "head", pairs) for i in range(pieces)
    ]


def send_far(kept, taken, head_count):
    sent = []
    received = []
    for number, (mine, theirs) in enumerate(zip(kept, taken)):
        step = number + 1
        pairs = [(i, (i + 2 * step) % head_count) for i in range(head_count)]
        theirs = jnp.concatenate(theirs, axis=0)
        sent.append((mine.astype(F32) + theirs.astype(F32)).astype(BF16))
        received.append(lax.ppermute(sent[-1], "head", pairs))
    return (sent, received)


def last_kernel(columns, head_count, pieces, own_ref, *refs):
    near_refs = refs[:pieces]
    refs = refs[pieces:]
    out_ref, turned = refs[-2:]
    halves = [refs[: (len(refs) - 2) // 2], refs[(len(refs) - 2) // 2 : -2]]
    head_index = lax.axis_index("head")
    shift = head_index * columns - window_start(head_index, columns, head_count)
    rows = own_ref.shape[0] // 2
    for number, received in enumerate(halves):
        part = slice(number * rows, (number + 1) * rows)
        near = near_refs[number * pieces // 2 : (number + 1) * pieces // 2]
        total = own_ref[part].astype(F32)
        total = total + jnp.concatenate([ref[...] for ref in near], axis=0).astype(F32)
        for ref in received:
            total = total + ref[...].astype(F32)
        turned[:, part] = total.T
    out_ref[...] = turned[pl.ds(pl.multiple_of(shift, 8), columns), :].astype(BF16)


def last(own, near, received, columns, head_count):
    rows, wide = own.shape
    vmem = pl.BlockSpec(memory_space=pltpu.VMEM)
    return pl.pallas_call(
        functools.partial(last_kernel, columns, head_count, len(near)),
        out_shape=jax.ShapeDtypeStruct((columns, rows), BF16),
        in_specs=[vmem] * (1 + len(near) + len(received)),
        out_specs=vmem,
        scratch_shapes=[pltpu.VMEM((wide, rows), F32)],
        compiler_params=pltpu.CompilerParams(vmem_limit_bytes=16 * MIB),
        cost_estimate=HINT,
        name="last",
    )(own, *near, *received)


def after(value, *others):
    return lax.optimization_barrier((value, others))[0]


def shards(queries, suffix_key_value, pooled_pages, out_weight, page_table, prefix_len, suffix_len):
    tok_rows = queries.shape[0]
    pages_dev, page_rows = pooled_pages.shape[:2]
    count = lax.axis_size("seq")
    head_count = lax.axis_size("head")
    reach = count // 2
    info = Meta(count, 2 * pages_dev // count)
    order = ring_order(count)
    ahead = [(order[i], order[(i + 1) % count]) for i in range(count)]
    back = [(b, a) for a, b in ahead]
    middle = tok_rows // 2

    meta = tables(info, pages_dev, page_rows, page_table, prefix_len, suffix_len)
    pages = jnp.transpose(pooled_pages, (0, 2, 1, 3))
    suffix = jnp.transpose(suffix_key_value, (1, 0, 2))

    def partial_of(query, offset, row_base=0, hint=HINT):
        return attend(info, meta, query, offset, row_base, tok_rows, pages, suffix, hint)

    left = [queries]
    right = [queries]
    part_left = {}
    part_right = {}
    late = reach - 2

    def attend_both(step):
        part_left[step] = partial_of(left[step], -step)
        part_right[step] = partial_of(right[step], step)
        return (part_left[step], part_right[step])

    for step in range(1, reach + 1):
        end = step == reach
        next_left = lax.ppermute(left[-1][:middle] if end else left[-1], "seq", ahead)
        next_right = lax.ppermute(right[-1][middle:] if end else right[-1], "seq", back)
        if step == 1:
            done = (meta, pages)
        elif step == reach - 1:
            home = partial_of(queries, 0)
            part_left[late] = partial_of(left[late], -late)
            done = (home, part_left[late])
        else:
            done = attend_both(step - 1)
        next_left, next_right = after((next_left, next_right), done)
        left.append(next_left)
        right.append(next_right)

    low_right = lax.ppermute(part_right[reach - 1][0], "seq", ahead)
    high_left = lax.ppermute(part_left[reach - 1][1], "seq", back)
    far_left = partial_of(left[reach], -reach)[0]
    far_right = partial_of(right[reach], reach, middle)[0]
    low_left = lax.ppermute(far_left, "seq", back)
    high_right = lax.ppermute(far_right, "seq", ahead)
    right[late] = after(right[late], far_left, far_right)
    part_right[late] = partial_of(right[late], late, 0, LONG)
    latest = part_right[late]

    def onward(travelled, mine, pairs):
        merged = merge(after(travelled, latest), mine)
        return (lax.ppermute(merged, "seq", pairs), merged)

    for step in range(reach - 1, 1, -1):
        low_left, latest = onward(low_left, part_left[step][0], back)
        if step == 2:
            low_right, latest = onward(low_right, part_right[step - 1][0], ahead)
            high_right, latest = onward(high_right, part_right[step][1], ahead)
            low_left, high_left = after((low_left, high_left), latest)
        else:
            high_right, latest = onward(high_right, part_right[step][1], ahead)
            high_left, latest = onward(high_left, part_left[step - 1][1], back)
            low_right, latest = onward(low_right, part_right[step - 1][0], ahead)
    low_left, latest = onward(low_left, part_left[1][0], back)
    high_left, latest = onward(high_left, part_left[1][1], back)
    early = merge(after(low_right, latest), home[0])
    latest = early
    high_right, latest = onward(high_right, part_right[1][1], ahead)

    low = [early, after(low_left, latest)]
    rest = (out_weight, tok_rows, head_count)
    rows_low, kept, taken = finish(info, meta, low, 0, *rest)
    taken, high_left, high_right = after((taken, high_left, high_right))
    sent, received_low = send_far(kept, taken, head_count)
    high = [after(home[1], sent), high_left, high_right]
    rows_high, kept, taken = finish(info, meta, high, middle, *rest)
    taken, received_low = after((taken, received_low))
    sent, received_high = send_far(kept, taken, head_count)
    near, own = share(
        "near",
        [(True, 0), (False, 0)],
        after([rows_low, rows_high], sent),
        out_weight,
        head_count,
    )
    near = after(swap_cores(near, head_count, 4), received_high)
    columns = out_weight.shape[1] // head_count
    return last(own, near, received_low + received_high, columns, head_count).T


def solution(mesh):
    placed = (
        P("seq", "head"),
        P("seq", None, "head"),
        P("seq", None, None, "head"),
        P("head", None),
        P(),
        P(),
        P(),
    )
    return jax.shard_map(
        shards, mesh=mesh, in_specs=placed, out_specs=P("seq", "head"), check_vma=False
    )
```
